32 devices in a mesh: tower: 2 (over x), dp: 16 (over z, y, core).
Axes of the slice: x: 2, y: 2, z: 4, core: 2. Of those that a mesh axis runs over, the one named last changes fastest.
Arguments:
- tokens: bfloat16 [24576, 768], P(('tower', 'dp')), may hold values from -6 to 6
- cotangent: bfloat16 [24576, 768], P(('tower', 'dp')), may hold values from -6 to 6
- caption_lengths: int32 [32, 24], P(('tower', 'dp')), may hold values from 1 to 64, 768 in all within a row
- image_index: int32 [32, 24], P(('tower', 'dp')), may hold values from 0 to 3
- image_states: bfloat16 [128, 576, 768], P(('tower', 'dp')), may hold values from -6 to 6
- master_weights: float32 [12288, 768], P(('tower', 'dp')), as said below
- first_moments: float32 [12288, 768], P(('tower', 'dp')), as said below
- second_moments: float32 [12288, 768], P(('tower', 'dp')), as said below
- owner_list: int32 [64], replicated, may hold values from 0 to 63, as said below
- norm_params: float32 [8, 768], replicated, as said below
- norm_first: float32 [8, 768], replicated, as said below
- norm_second: float32 [8, 768], replicated, as said below
Outputs:
- layer_out: bfloat16 [24576, 768], P(('tower', 'dp'))
- grad_tokens: float32 [24576, 768], P(('tower', 'dp'))
- grad_images: float32 [128, 576, 768], P(('tower', 'dp'))
- new_weights: float32 [12288, 768], P(('tower', 'dp'))
- new_first: float32 [12288, 768], P(('tower', 'dp'))
- new_second: float32 [12288, 768], P(('tower', 'dp'))
- weight_copy: bfloat16 [12288, 768], P(('tower', 'dp'))
- norm_new: float32 [8, 768], replicated
- norm_first_new: float32 [8, 768], replicated
- norm_second_new: float32 [8, 768], replicated
The draws below stay inside these ranges and needn't reach their ends.
Inputs may be any that keep to these rules, and one draw needn't show every extreme that they name: `caption_lengths`: each row holds one device's 24 caption lengths, summing to 768, the longest exactly 64. `owner_list`: a permutation of the 64 groups. `master_weights`: weights of the scale of their fan-in. `first_moments`: both signs. `second_moments`: positive. `norm_params`: gains near one, biases of both signs. `norm_first`: both signs. `norm_second`: positive.
All inputs are finite; a program needn't handle non-finite values.
Results may differ from the reference program's by a relative error of at most 0.02.
Values may be sent and summed in bfloat16 or wider, within the bound.
A program may use at most 384 MiB of HBM per device.

```python
import math
import jax
import jax.numpy as jnp
import numpy as np
from jax import lax

D = 768
HEADS = 12
HDIM = 64
FF = 3072
PATCHES = 576
MAXLEN = 64
IMG_DEV = 4
STEP = 5
TOK_DEV = 768
CAP_DEV = 24
SHARDS = 32
TOKENS = 24576
IMAGES = 128
ROWS = 12288
GROUPS = 64
GROUP_ROWS = 192
N_TOWER = 2
N_DP = 16


def owner_permutation(key):
    return jax.random.permutation(jax.random.fold_in(key, 101), GROUPS).astype(jnp.int32)


def row_scales(key):
    owners = owner_permutation(key)
    slot_rows = jnp.arange(ROWS, dtype=jnp.int32)
    logical = owners[slot_rows // GROUP_ROWS] * GROUP_ROWS + slot_rows % GROUP_ROWS
    base = D ** (-0.5)
    scales = jnp.where(logical < 3 * D, base, jnp.where(logical < 4 * D, 3.0 * base, jnp.where(logical < 7 * D, base, jnp.where(logical < 8 * D, 3.0 * base, jnp.where(logical < 8 * D + FF, base, 1.5 * FF ** (-0.5))))))
    return scales.astype(jnp.float32)


def draw_owner_list(key, part):
    return owner_permutation(key)


def draw_master_weights(key, part):
    scales = row_scales(key)
    key = jax.random.fold_in(key, 3)
    normal_part = jax.random.truncated_normal(key, -4.0, 4.0, (ROWS, D), jnp.float32)
    return normal_part * scales[:, None]


def draw_first_moments(key, part):
    key = jax.random.fold_in(key, 4)
    grad_scale = 0.5 * math.sqrt(TOKENS)
    return grad_scale * jax.random.truncated_normal(key, -4.0, 4.0, (ROWS, D), jnp.float32)


def draw_second_moments(key, part):
    key = jax.random.fold_in(key, 5)
    grad_scale = 0.5 * math.sqrt(TOKENS)
    spread = jnp.exp(jax.random.uniform(key, (ROWS, D), jnp.float32, -math.log(2.0), math.log(2.0)))
    return 2.0 * 0.667 * grad_scale * grad_scale * spread


def draw_norm_params(key, part):
    key = jax.random.fold_in(key, 6)
    key_gain, key_shift = jax.random.split(key)
    gains = 1.0 + 0.3 * jax.random.uniform(key_gain, (4, D), jnp.float32, -1.0, 1.0)
    shifts = 0.3 * jax.random.truncated_normal(key_shift, -3.0, 3.0, (4, D), jnp.float32)
    return jnp.concatenate([gains, shifts], axis=0)


def draw_norm_first(key, part):
    key = jax.random.fold_in(key, 7)
    grad_scale = math.sqrt(TOKENS)
    return grad_scale * jax.random.truncated_normal(key, -4.0, 4.0, (8, D), jnp.float32)


def draw_norm_second(key, part):
    key = jax.random.fold_in(key, 8)
    grad_scale = math.sqrt(TOKENS)
    spread = jnp.exp(jax.random.uniform(key, (8, D), jnp.float32, -math.log(2.0), math.log(2.0)))
    return 2.0 * 0.667 * grad_scale * grad_scale * spread


def touch_ends(array, rng, smallest, high):
    place = [jax.random.randint(jax.random.fold_in(rng, axis), (), 0, length) for axis, length in enumerate(array.shape)]
    widest = array.shape.index(max(array.shape))
    beside = place[:widest] + [(place[widest] + 1) % array.shape[widest]] + place[widest + 1:]
    return array.at[tuple(place)].set(smallest).at[tuple(beside)].set(high)


def levels(rng, dims, shards, low, high):
    def one(axis_at, shards_of):
        draws = jax.random.uniform(jax.random.fold_in(jax.random.fold_in(rng, 6), axis_at), (shards_of,), jnp.float32, low / len(shards), high / len(shards))
        return jnp.repeat(jnp.exp(draws), dims[axis_at] // shards_of).reshape((-1,) + (1,) * (len(dims) - axis_at - 1))

    gain = one(*shards[0])
    for cut in shards[1:]:
        gain = gain * one(*cut)
    return gain


def split_up(number_of, total, bound, slope):
    portions = [(1 << 20) // math.isqrt(standing ** slope) + 1 for standing in range(2, number_of + 1)]
    surplus, given = total - bound - (number_of - 1), [1] * (number_of - 1)
    while surplus > 0:
        movable = [i for i in range(number_of - 1) if given[i] < bound]
        mass, left = sum([portions[i] for i in movable]), surplus
        for i in movable:
            addition = min(bound - given[i], max(1, left * portions[i] // mass), surplus)
            given[i] = given[i] + addition
            surplus = surplus - addition
    return np.array([bound] + given)


def uneven(rng, number_of, total, limit, slope):
    if number_of == 2:
        one = jax.random.randint(rng, (), max(1, total - limit), min(limit, total - 1) + 1)
        return jnp.stack([one, total - one])
    tallies = jnp.asarray(split_up(number_of, total, limit, slope), jnp.int32)
    twos = (number_of - 1) // 2
    source_of, receiver = tallies[1:1 + 2 * twos:2], tallies[2:2 + 2 * twos:2]
    margin = jnp.minimum(source_of - 1, limit - receiver)
    moved = jax.random.randint(jax.random.fold_in(rng, 1), (twos,), 0, 1 << 20) % (margin + 1)
    tallies = tallies.at[1:1 + 2 * twos:2].set(source_of - moved).at[2:2 + 2 * twos:2].set(receiver + moved)
    return tallies[jax.random.permutation(jax.random.fold_in(rng, 2), number_of)]


def bell_draw(rng, extent, scale, reach, shards=(), held_as=jnp.bfloat16):
    values = scale * jax.random.normal(rng, extent, jnp.float32)
    if shards:
        values = values * levels(rng, extent, shards, -0.22, 0.18)
    return jnp.clip(values, -reach, reach).astype(held_as)


def setup_inputs(seed: int = 0) -> dict:
    arg_keys = jax.random.split(jax.random.key(seed), 13)
    return {
        "tokens": bell_draw(arg_keys[0], (TOKENS, D), 1.0, 6.0, ((0, 32),)),
        "cotangent": bell_draw(arg_keys[1], (TOKENS, D), 1.0, 6.0, ((0, 32),)),
        "caption_lengths": jax.vmap(lambda own: uneven(own, CAP_DEV, TOK_DEV, MAXLEN, 2))(jax.random.split(arg_keys[2], SHARDS)).reshape((SHARDS, CAP_DEV)).astype(jnp.int32),
        "image_index": touch_ends(jax.random.randint(arg_keys[3], (SHARDS, CAP_DEV), 0, IMG_DEV), jax.random.fold_in(arg_keys[3], 1), 0, IMG_DEV - 1).astype(jnp.int32),
        "image_states": bell_draw(arg_keys[4], (IMAGES, PATCHES, D), 1.0, 6.0, ((0, 32),)),
        "master_weights": draw_master_weights(jax.random.fold_in(arg_keys[12], 71), 0),
        "first_moments": draw_first_moments(jax.random.fold_in(arg_keys[12], 71), 0),
        "second_moments": draw_second_moments(jax.random.fold_in(arg_keys[12], 71), 0),
        "owner_list": draw_owner_list(jax.random.fold_in(arg_keys[12], 71), 0),
        "norm_params": draw_norm_params(jax.random.fold_in(arg_keys[12], 71), 0),
        "norm_first": draw_norm_first(jax.random.fold_in(arg_keys[12], 71), 0),
        "norm_second": draw_norm_second(jax.random.fold_in(arg_keys[12], 71), 0),
    }


@jax.custom_vjp
def low(v):
    return lax.optimization_barrier(v.astype(jnp.bfloat16)).astype(jnp.float32)

@jax.custom_vjp
def low_back(v):
    return v

def low_keep(v):
    return (low(v), None)

def low_pass(kept, grad):
    return (grad,)

def back_keep(v):
    return (v, None)

def back_low(kept, grad):
    return (low(grad),)
low.defvjp(low_keep, low_pass)
low_back.defvjp(back_keep, back_low)
beta_one = 0.5
beta_two = 0.6
learn_rate = 0.03
norm_rate = 0.4
weight_decay = 0.01
epsilon = 1e-08
norm_eps = 1e-05
masked_score = -1000000000.0
highest = lax.Precision.HIGHEST

def layer_norm(inputs, gains, shifts):
    average = lax.optimization_barrier(jnp.mean(inputs, axis=-1, keepdims=True))
    centred = inputs - average
    inv_std = lax.rsqrt(lax.optimization_barrier(jnp.mean(centred * centred, axis=-1, keepdims=True)) + norm_eps)
    return centred * inv_std * gains + shifts

def row_softmax(scores):
    row_top = lax.optimization_barrier(jnp.max(scores, axis=-1, keepdims=True))
    exponent = jnp.exp(scores - row_top)
    return exponent / lax.optimization_barrier(jnp.sum(exponent, axis=-1, keepdims=True))

def matmul(left, right):
    return jnp.dot(left, right, precision=highest, preferred_element_type=jnp.float32)

def split_rows(packed):
    pieces = [packed[index_row * D:(index_row + 1) * D] for index_row in range(8)]
    up_rows = packed[8 * D:8 * D + FF]
    down_rows = packed[8 * D + FF:8 * D + 2 * FF]
    return tuple(pieces) + (up_rows, down_rows)

def device_forward(packed, norms, inputs, arrived, lengths, picks):
    w_query, w_key, w_value, w_output, c_query, c_key, c_value, c_output, up_rows, down_rows = split_rows(packed)
    tok_rows = inputs.shape[0]
    score_scale = HDIM ** (-0.5)
    ends = jnp.cumsum(lengths).astype(jnp.int32)
    positions = jnp.arange(tok_rows, dtype=jnp.int32)
    segment = lax.optimization_barrier(jnp.sum((positions[:, None] >= ends[None, :]).astype(jnp.int32), axis=1))
    caption_ids = jnp.arange(lengths.shape[0], dtype=jnp.int32)
    token_image = lax.optimization_barrier(jnp.sum(jnp.where(segment[:, None] == caption_ids[None, :], picks[None, :], 0), axis=1))
    same_doc = (segment[:, None] == segment[None, :]) & (positions[None, :] <= positions[:, None])
    first = low(layer_norm(inputs, norms[0], norms[4]))
    query = low(low_back(matmul(first, w_query))).reshape(tok_rows, HEADS, HDIM)
    keys = low(low_back(matmul(first, w_key))).reshape(tok_rows, HEADS, HDIM)
    values = low(low_back(matmul(first, w_value))).reshape(tok_rows, HEADS, HDIM)
    raw = low_back(jnp.einsum('qhd,khd->hqk', query, keys, precision=highest) * score_scale)
    probs = low(row_softmax(jnp.where(same_doc[None], raw, masked_score)))
    attended = low(low_back(jnp.einsum('hqk,khd->qhd', probs, values, precision=highest))).reshape(tok_rows, D)
    resid_one = inputs + low_back(matmul(attended, w_output))
    second = low(layer_norm(resid_one, norms[1], norms[5]))
    cross_query = low(low_back(matmul(second, c_query))).reshape(tok_rows, HEADS, HDIM)
    images_dev = arrived.shape[0]
    cross_keys = low(low_back(jnp.einsum('ipd,de->ipe', arrived, c_key, precision=highest))).reshape(images_dev, PATCHES, HEADS, HDIM)
    cross_values = low(low_back(jnp.einsum('ipd,de->ipe', arrived, c_value, precision=highest))).reshape(images_dev, PATCHES, HEADS, HDIM)
    cross_sum = jnp.zeros((tok_rows, HEADS, HDIM), jnp.float32)
    for image_pos in range(images_dev):
        cross_raw = low_back(jnp.einsum('qhd,khd->hqk', cross_query, cross_keys[image_pos], precision=highest) * score_scale)
        cross_probs = low(row_softmax(cross_raw))
        portion = jnp.einsum('hqk,khd->qhd', cross_probs, cross_values[image_pos], precision=highest)
        cross_sum = cross_sum + jnp.where((token_image == image_pos)[:, None, None], portion, 0.0)
    cross_out = low(low_back(cross_sum)).reshape(tok_rows, D)
    resid_two = resid_one + low_back(matmul(cross_out, c_output))
    third = low(layer_norm(resid_two, norms[2], norms[6]))
    pre_act = low_back(jnp.einsum('td,fd->tf', third, up_rows, precision=highest))
    hidden = low(jax.nn.gelu(pre_act))
    return resid_two + low_back(matmul(hidden, down_rows))

def forward(inputs, images, logical, norms, lengths, picks):
    packed = low(logical)
    encoded = low(low_back(layer_norm(images, norms[3], norms[7])))
    shard_count = N_TOWER * N_DP
    per_device = encoded.reshape(shard_count, IMG_DEV, PATCHES, D)
    partner = jnp.roll(per_device, N_DP, axis=0)
    token_blocks = inputs.reshape(shard_count, TOK_DEV, D)

    def one_device(operands):
        block_in, block_images, block_lengths, block_picks = operands
        return device_forward(packed, norms, block_in, block_images, block_lengths, block_picks)
    results = lax.map(jax.checkpoint(one_device), (token_blocks, partner, lengths, picks))
    return results.reshape(shard_count * TOK_DEV, D)

def adamw_update(weight, moment, second, grad_in, rate, decay_rate):
    new_moment = beta_one * moment + (1.0 - beta_one) * grad_in
    new_second = beta_two * second + (1.0 - beta_two) * grad_in * grad_in
    moment_hat = new_moment / (1.0 - beta_one ** STEP)
    second_hat = new_second / (1.0 - beta_two ** STEP)
    new_weight = weight - rate * (moment_hat / (jnp.sqrt(second_hat) + epsilon) + decay_rate * weight)
    return (new_weight, new_moment, new_second)

def reference(tokens, cotangent, caption_lengths, image_index, image_states, master_weights, first_moments, second_moments, owner_list, norm_params, norm_first, norm_second):
    groups = owner_list.shape[0]
    group_rows = master_weights.shape[0] // groups
    inverse = jnp.argsort(owner_list).astype(jnp.int32)
    logical = master_weights.reshape(groups, group_rows, D)[inverse].reshape(groups * group_rows, D)

    def wrapped(inputs, images, weights, norms):
        return forward(inputs, images, weights, norms, caption_lengths, image_index)
    result, pullback = jax.vjp(wrapped, tokens.astype(jnp.float32), image_states.astype(jnp.float32), logical, norm_params)
    grad_tokens, grad_images, grad_logical, grad_norms = pullback(cotangent.astype(jnp.float32))
    slot_grads = grad_logical.reshape(groups, group_rows, D)[owner_list].reshape(groups * group_rows, D)
    new_weights, new_first, new_second = adamw_update(master_weights, first_moments, second_moments, slot_grads, learn_rate, weight_decay)
    norm_new, norm_first_new, norm_second_new = adamw_update(norm_params, norm_first, norm_second, grad_norms, norm_rate, 0.0)
    return (result.astype(jnp.bfloat16), grad_tokens, grad_images, new_weights, new_first, new_second, new_weights.astype(jnp.bfloat16), norm_new, norm_first_new, norm_second_new)
```

```python
import functools

import jax
import jax.numpy as jnp
from jax import lax
from jax.experimental import pallas as pl
from jax.experimental.pallas import tpu as pltpu
from jax.sharding import PartitionSpec as P

D = 768
HEADS = 12
HDIM = 64
FF = 3072
STEP = 5
PAIRS = HEADS // 2
LANES = 2 * HDIM
QB = 128
GROUP = 192
PER = D // GROUP
SCALE = HDIM ** (-0.5)

beta_one = 0.5
beta_two = 0.6
learn_rate = 0.03
norm_rate = 0.4
weight_decay = 0.01
epsilon = 1e-08
norm_eps = 1e-05
masked_score = -1000000000.0

W_Q, W_K, W_V, W_O, C_Q, C_K, C_V, C_O, UP, DOWN = 0, 1, 2, 3, 4, 5, 6, 7, 8, 12

BF = jnp.bfloat16
F32 = jnp.float32
VM = pl.BlockSpec(memory_space=pltpu.VMEM)
SM = pl.BlockSpec(memory_space=pltpu.SMEM)
ANY = pl.BlockSpec(memory_space=pl.ANY)
VLIM = 58 * 2**20


def nn(a, b):
    return lax.dot_general(a, b, (((1,), (0,)), ((), ())), preferred_element_type=F32)


def nt(a, b):
    return lax.dot_general(a, b, (((1,), (1,)), ((), ())), preferred_element_type=F32)


def tn(a, b):
    return lax.dot_general(a, b, (((0,), (0,)), ((), ())), preferred_element_type=F32)


def blk(i, size=QB):
    return pl.ds(pl.multiple_of(i * size, size), size)


def lanes(p):
    return slice(p * LANES, (p + 1) * LANES)


def normalise(x):
    centred = x - jnp.mean(x, axis=-1, keepdims=True)
    inv = lax.rsqrt(jnp.mean(centred * centred, axis=-1, keepdims=True) + norm_eps)
    return centred * inv, inv


def norm_back(grad, normed, inv, gain):
    gn = grad * gain
    m1 = jnp.mean(gn, axis=-1, keepdims=True)
    m2 = jnp.mean(gn * normed, axis=-1, keepdims=True)
    return inv * (gn - m1 - normed * m2)


def head_masks():
    low = (lax.broadcasted_iota(jnp.int32, (1, LANES), 1) < HDIM).astype(F32)
    return low.astype(BF), (1.0 - low).astype(BF)


def two_heads(x, masks):
    return jnp.concatenate([x * masks[0], x * masks[1]], axis=0)


def merge_heads(both):
    return jnp.concatenate([both[:HDIM, :QB], both[HDIM:, QB:]], axis=0)


def weight_copies(slots, inv, buf, sem, matrix, slot):
    return [
        pltpu.make_async_copy(
            slots.at[inv[matrix * PER + j]], buf.at[slot, pl.ds(j * GROUP, GROUP)], sem.at[slot, j]
        )
        for j in range(PER)
    ]


def grad_copies(grads, inv, buf, sem, matrix, slot):
    return [
        pltpu.make_async_copy(
            buf.at[slot, pl.ds(j * GROUP, GROUP)], grads.at[inv[matrix * PER + j]], sem.at[slot, j]
        )
        for j in range(PER)
    ]


def start(copies):
    for copy in copies:
        copy.start()


def wait(copies):
    for copy in copies:
        copy.wait()


def causal_mask(starts, b):
    query = lax.broadcasted_iota(jnp.int32, (1, QB), 1) + b * QB
    first = jnp.zeros((1, QB), jnp.int32)
    for c in range(starts.shape[0]):
        first = jnp.maximum(first, jnp.where(query >= starts[c], starts[c], 0))
    key = lax.broadcasted_iota(jnp.int32, (2 * QB, QB), 0) + (b - 1) * QB
    allowed = (key >= first) & (key <= query)
    return jnp.concatenate([allowed, allowed], axis=1)


def column_softmax(scores):
    top = jnp.max(scores, axis=0, keepdims=True)
    exponent = jnp.exp(scores - top)
    return exponent, 1.0 / jnp.sum(exponent, axis=0, keepdims=True)


def self_forward(
    inv, starts, x, norms, slots, q_o, k_o, v_o, att_o, r1_o, cq_o, wbuf, low, kpad, vpad, wsem
):
    rows = x.shape[0]
    loads = [weight_copies(slots, inv, wbuf, wsem, m, m) for m in range(5)]
    for load in loads:
        start(load)
    masks = head_masks()

    def norm_one(i, _):
        normed, _i = normalise(x[blk(i), :].astype(F32))
        low[blk(i), :] = (normed * norms[0:1, :] + norms[4:5, :]).astype(BF)
        return 0

    lax.fori_loop(0, rows // QB, norm_one, 0)
    kpad[pl.ds(0, QB), :] = jnp.zeros((QB, D), BF)
    vpad[pl.ds(0, QB), :] = jnp.zeros((QB, D), BF)
    wait(loads[0])
    q_o[...] = (nn(low[...], wbuf[0]) * SCALE).astype(BF)
    wait(loads[1])
    kpad[pl.ds(QB, rows), :] = nn(low[...], wbuf[1]).astype(BF)
    wait(loads[2])
    vpad[pl.ds(QB, rows), :] = nn(low[...], wbuf[2]).astype(BF)
    k_o[...] = kpad[pl.ds(QB, rows), :]
    v_o[...] = vpad[pl.ds(QB, rows), :]

    def attend(b, _):
        allowed = causal_mask(starts, b)
        for p in range(PAIRS):
            q2 = two_heads(q_o[blk(b), lanes(p)], masks)
            keys = kpad[pl.ds(pl.multiple_of(b * QB, QB), 2 * QB), lanes(p)]
            vals = vpad[pl.ds(pl.multiple_of(b * QB, QB), 2 * QB), lanes(p)]
            scores = jnp.where(allowed, nt(keys, q2), masked_score)
            exponent, scale = column_softmax(scores)
            out = tn(vals, (exponent * scale).astype(BF))
            att_o[blk(b), lanes(p)] = merge_heads(out).T.astype(BF)
        return 0

    lax.fori_loop(0, rows // QB, attend, 0)
    wait(loads[3])
    r1_o[...] = x[...].astype(F32) + nn(att_o[...], wbuf[3])

    def norm_two(i, _):
        normed, _i = normalise(r1_o[blk(i), :])
        low[blk(i), :] = (normed * norms[1:2, :] + norms[5:6, :]).astype(BF)
        return 0

    lax.fori_loop(0, rows // QB, norm_two, 0)
    wait(loads[4])
    cq_o[...] = (nn(low[...], wbuf[4]) * SCALE).astype(BF)


def call(body, out_shape, in_specs, out_specs, scratch, aliases=None, effects=False):
    return pl.pallas_call(
        body,
        out_shape=out_shape,
        in_specs=in_specs,
        out_specs=out_specs,
        scratch_shapes=scratch,
        input_output_aliases=aliases or {},
        compiler_params=pltpu.CompilerParams(vmem_limit_bytes=VLIM, has_side_effects=effects),
    )


def run_self_forward(inv, starts, x, norms, slots):
    rows = x.shape[0]
    one = jax.ShapeDtypeStruct((rows, D), BF)
    return call(
        self_forward,
        (one, one, one, one, jax.ShapeDtypeStruct((rows, D), F32), one),
        [SM, SM, VM, VM, ANY],
        (VM,) * 6,
        [
            pltpu.VMEM((5, D, D), BF),
            pltpu.VMEM((rows, D), BF),
            pltpu.VMEM((rows + QB, D), BF),
            pltpu.VMEM((rows + QB, D), BF),
            pltpu.SemaphoreType.DMA((5, PER)),
        ],
    )(inv, starts, x, norms, slots)


def image_blocks(bounds, i):
    low, high = bounds[i], bounds[i + 1]
    first = low // QB
    last = jnp.where(high > low, (high + QB - 1) // QB, first)
    return low, high, first, last


def cross_forward(
    images, inv, bounds, enc, cq, r1, slots, k_o, v_o, cross_o, r2_o, wbuf, acc, wsem
):
    patches = enc.shape[0] // images
    loads = [weight_copies(slots, inv, wbuf, wsem, m, i) for i, m in enumerate((C_K, C_V, C_O))]
    for load in loads:
        start(load)
    masks = head_masks()
    cross_o[...] = jnp.zeros_like(cross_o)
    for i, out in ((0, k_o), (1, v_o)):
        wait(loads[i])

        def project(c, _, i=i, out=out):
            out[blk(c, D), :] = nn(enc[blk(c, D), :], wbuf[i]).astype(BF)
            return 0

        lax.fori_loop(0, enc.shape[0] // D, project, 0)

    def image(i, _):
        low, high, first, last = image_blocks(bounds, i)

        def attend(b, _):
            token = lax.broadcasted_iota(jnp.int32, (1, QB), 1) + b * QB
            here = ((token >= low) & (token < high)).astype(F32)
            here = jnp.concatenate([here, here], axis=1)
            for p in range(PAIRS):
                q2 = two_heads(cq[blk(b), lanes(p)], masks)
                keys = k_o[blk_of(i, patches), lanes(p)]
                vals = v_o[blk_of(i, patches), lanes(p)]
                exponent, scale = column_softmax(nt(keys, q2))
                out = tn(vals, exponent.astype(BF)) * (scale * here)
                acc[blk(b), lanes(p)] += merge_heads(out).T
            return 0

        lax.fori_loop(first, last, attend, 0)
        return 0

    acc[...] = jnp.zeros_like(acc)
    lax.fori_loop(0, images, image, 0)
    cross_o[...] = acc[...].astype(BF)
    wait(loads[2])
    r2_o[...] = r1[...] + nn(cross_o[...], wbuf[2])


def blk_of(i, size):
    return pl.ds(pl.multiple_of(i * size, 64), size)


def run_cross_forward(images, inv, bounds, enc, cq, r1, slots):
    rows = cq.shape[0]
    kv = jax.ShapeDtypeStruct(enc.shape, BF)
    return call(
        functools.partial(cross_forward, images),
        (kv, kv, jax.ShapeDtypeStruct((rows, D), BF), jax.ShapeDtypeStruct((rows, D), F32)),
        [SM, SM, VM, VM, VM, ANY],
        (VM,) * 4,
        [
            pltpu.VMEM((3, D, D), BF),
            pltpu.VMEM((rows, D), F32),
            pltpu.SemaphoreType.DMA((3, PER)),
        ],
    )(inv, bounds, enc, cq, r1, slots)


GELU_A = 0.7978845608028654
GELU_B = GELU_A * 0.044715


def feed_forward(
    inv, r2, cot, norms, slots, out_o, g2_o, ng_o, grads,
    wup, wdown, third, pre, gh, hid, gpre, acc, gthird, gup, gdown, usem, dsem, gusem, gdsem,
):
    rows = r2.shape[0]
    chunks = FF // D

    def loads(c, slot):
        return weight_copies(slots, inv, wup, usem, UP + c, slot) + weight_copies(
            slots, inv, wdown, dsem, DOWN + c, slot
        )

    def stores(c, slot):
        return grad_copies(grads, inv, gup, gusem, UP + c, slot) + grad_copies(
            grads, inv, gdown, gdsem, DOWN + c, slot
        )

    start(loads(0, 0))

    def norm_three(i, _):
        normed, _i = normalise(r2[blk(i), :])
        third[blk(i), :] = (normed * norms[2:3, :] + norms[6:7, :]).astype(BF)
        return 0

    lax.fori_loop(0, rows // QB, norm_three, 0)
    acc[...] = r2[...]
    gthird[...] = jnp.zeros_like(gthird)

    def chunk(c, _):
        slot = c % 2

        @pl.when(c + 1 < chunks)
        def _():
            start(loads(c + 1, 1 - slot))

        wait(loads(c, slot))
        pre[...] = nt(third[...], wup[slot])
        gh[...] = nt(cot[...], wdown[slot])

        def gelu(i, _):
            x = pre[blk(i, 64), :]
            x2 = x * x
            t = jnp.tanh(x * (GELU_A + GELU_B * x2))
            half = 0.5 + 0.5 * t
            value = x * half
            hid[blk(i, 64), :] = value.astype(BF)
            slope = half + value * (1.0 - t) * (GELU_A + 3.0 * GELU_B * x2)
            gpre[blk(i, 64), :] = (gh[blk(i, 64), :] * slope).astype(BF)
            return 0

        lax.fori_loop(0, rows // 64, gelu, 0)

        @pl.when(c >= 2)
        def _():
            wait(stores(c - 2, slot))

        acc[...] += nn(hid[...], wdown[slot])
        gdown[slot] = tn(hid[...], cot[...]).astype(BF)
        gup[slot] = tn(gpre[...], third[...]).astype(BF)
        start(stores(c, slot))
        gthird[...] += nn(gpre[...], wup[slot])
        return 0

    lax.fori_loop(0, chunks, chunk, 0)
    out_o[...] = acc[...].astype(BF)
    ng_o[...] = jnp.zeros_like(ng_o)

    def back(i, _):
        normed, inv_std = normalise(r2[blk(i), :])
        grad = gthird[blk(i), :]
        ng_o[0:1, :] += jnp.sum(grad * normed, axis=0, keepdims=True)
        ng_o[1:2, :] += jnp.sum(grad, axis=0, keepdims=True)
        g2_o[blk(i), :] = cot[blk(i), :].astype(F32) + norm_back(
            grad, normed, inv_std, norms[2:3, :]
        )
        return 0

    lax.fori_loop(0, rows // QB, back, 0)
    for c in range(chunks - 2, chunks):
        wait(stores(c, c % 2))


def run_feed_forward(inv, r2, cot, norms, slots):
    rows = r2.shape[0]
    big = pltpu.VMEM((rows, D), F32)
    low = pltpu.VMEM((rows, D), BF)
    two = pltpu.VMEM((2, D, D), BF)
    sem = pltpu.SemaphoreType.DMA((2, PER))
    return call(
        feed_forward,
        (
            jax.ShapeDtypeStruct((rows, D), BF),
            jax.ShapeDtypeStruct((rows, D), F32),
            jax.ShapeDtypeStruct((2, D), F32),
            jax.ShapeDtypeStruct(slots.shape, BF),
        ),
        [SM, VM, VM, VM, ANY],
        (VM, VM, VM, ANY),
        [two, two, low, big, big, low, low, big, big, two, two, sem, sem, sem, sem],
    )(inv, r2, cot, norms, slots)


def cross_backward(
    images, inv, bounds, g2, cross, k, v, cq, r1, enc, img, norms, slots, grads_in,
    g1_o, gi_o, ng_o, grads,
    wbuf, gbuf, gca, dq, acck, accv, dk, dv, big, wsem, gsem,
):
    rows = g2.shape[0]
    patches = enc.shape[0] // images
    names = (C_O, C_Q, C_K, C_V)
    loads = [weight_copies(slots, inv, wbuf, wsem, m, i) for i, m in enumerate(names)]
    stores = [grad_copies(grads, inv, gbuf, gsem, m, i) for i, m in enumerate(names)]
    for load in loads:
        start(load)
    masks = head_masks()
    ng_o[...] = jnp.zeros_like(ng_o)
    low = dq
    low[...] = g2[...].astype(BF)
    gbuf[0] = tn(cross[...], low[...]).astype(BF)
    start(stores[0])
    wait(loads[0])
    gca[...] = nt(low[...], wbuf[0]).astype(BF)
    dq[...] = jnp.zeros_like(dq)

    def image(i, _):
        first_row, end_row, first, last = image_blocks(bounds, i)
        acck[...] = jnp.zeros_like(acck)
        accv[...] = jnp.zeros_like(accv)

        def attend(b, _):
            token = lax.broadcasted_iota(jnp.int32, (QB, LANES), 0) + b * QB
            here = ((token >= first_row) & (token < end_row)).astype(F32).astype(BF)
            for p in range(PAIRS):
                q2 = two_heads(cq[blk(b), lanes(p)], masks)
                go2 = two_heads(gca[blk(b), lanes(p)] * here, masks)
                keys = k[blk_of(i, patches), lanes(p)]
                vals = v[blk_of(i, patches), lanes(p)]
                exponent, scale = column_softmax(nt(keys, q2))
                probs = exponent * scale
                accv[:, lanes(p)] += nn(probs.astype(BF), go2)
                gp = nt(vals, go2)
                gs = probs * (gp - jnp.sum(gp * probs, axis=0, keepdims=True))
                gs = gs.astype(BF)
                acck[:, lanes(p)] += nn(gs, q2)
                gq = merge_heads(tn(keys, gs)).T * SCALE
                dq[blk(b), lanes(p)] += gq.astype(BF)
            return 0

        lax.fori_loop(first, last, attend, 0)
        dk[blk_of(i, patches), :] = acck[...].astype(BF)
        dv[blk_of(i, patches), :] = accv[...].astype(BF)
        return 0

    lax.fori_loop(0, images, image, 0)
    for slot, grad in ((2, dk), (3, dv)):
        big[...] = jnp.zeros_like(big)

        def gather(c, _, grad=grad):
            big[...] += tn(enc[blk(c, D), :], grad[blk(c, D), :])
            return 0

        lax.fori_loop(0, enc.shape[0] // D, gather, 0)
        gbuf[slot] = big[...].astype(BF)
        start(stores[slot])
    wait(loads[2])
    wait(loads[3])

    def encoder(c, _):
        sent = nt(dk[blk(c, D), :], wbuf[2]) + nt(dv[blk(c, D), :], wbuf[3])
        big[...] = sent

        def back(j, _):
            rows_j = pl.ds(pl.multiple_of(c * D + j * QB, QB), QB)
            normed, inv_std = normalise(img[rows_j, :].astype(F32))
            grad = big[blk(j), :].astype(BF).astype(F32)
            ng_o[2:3, :] += jnp.sum(grad * normed, axis=0, keepdims=True)
            ng_o[3:4, :] += jnp.sum(grad, axis=0, keepdims=True)
            gi_o[rows_j, :] = norm_back(grad, normed, inv_std, norms[3:4, :])
            return 0

        lax.fori_loop(0, D // QB, back, 0)
        return 0

    lax.fori_loop(0, enc.shape[0] // D, encoder, 0)

    def norm_two(i, _):
        normed, _i = normalise(r1[blk(i), :])
        gca[blk(i), :] = (normed * norms[1:2, :] + norms[5:6, :]).astype(BF)
        return 0

    lax.fori_loop(0, rows // QB, norm_two, 0)
    gbuf[1] = tn(gca[...], dq[...]).astype(BF)
    start(stores[1])
    wait(loads[1])
    big[...] = nt(dq[...], wbuf[1])

    def back_two(i, _):
        normed, inv_std = normalise(r1[blk(i), :])
        grad = big[blk(i), :]
        ng_o[0:1, :] += jnp.sum(grad * normed, axis=0, keepdims=True)
        ng_o[1:2, :] += jnp.sum(grad, axis=0, keepdims=True)
        g1_o[blk(i), :] = g2[blk(i), :] + norm_back(grad, normed, inv_std, norms[1:2, :])
        return 0

    lax.fori_loop(0, rows // QB, back_two, 0)
    for store in stores:
        wait(store)


def run_cross_backward(images, inv, bounds, g2, cross, k, v, cq, r1, enc, img, norms, slots, grads):
    rows = g2.shape[0]
    patches = enc.shape[0] // images
    four = pltpu.VMEM((4, D, D), BF)
    low = pltpu.VMEM((rows, D), BF)
    part = pltpu.VMEM((patches, D), F32)
    wide = pltpu.VMEM(enc.shape, BF)
    sem = pltpu.SemaphoreType.DMA((4, PER))
    return call(
        functools.partial(cross_backward, images),
        (
            jax.ShapeDtypeStruct((rows, D), F32),
            jax.ShapeDtypeStruct(enc.shape, F32),
            jax.ShapeDtypeStruct((4, D), F32),
            jax.ShapeDtypeStruct(slots.shape, BF),
        ),
        [SM, SM] + [VM] * 9 + [ANY, ANY],
        (VM, VM, VM, ANY),
        [four, four, low, low, part, part, wide, wide, pltpu.VMEM((D, D), F32), sem, sem],
        aliases={12: 3},
    )(inv, bounds, g2, cross, k, v, cq, r1, enc, img, norms, slots, grads)


def self_backward(
    inv, starts, g1, x, q, k, v, att, norms, slots, grads_in,
    gt_o, ng_o, grads,
    wbuf, gbuf, ga, dq, kpad, vpad, acck, accv, dk, dv, big, wsem, gsem,
):
    rows = g1.shape[0]
    names = (W_O, W_Q, W_K, W_V)
    loads = [weight_copies(slots, inv, wbuf, wsem, m, i) for i, m in enumerate(names)]
    stores = [grad_copies(grads, inv, gbuf, gsem, m, i) for i, m in enumerate(names)]
    for load in loads:
        start(load)
    masks = head_masks()
    ng_o[...] = jnp.zeros_like(ng_o)
    low = dq
    low[...] = g1[...].astype(BF)
    gbuf[0] = tn(att[...], low[...]).astype(BF)
    start(stores[0])
    wait(loads[0])
    ga[...] = nt(low[...], wbuf[0]).astype(BF)
    kpad[pl.ds(0, QB), :] = jnp.zeros((QB, D), BF)
    vpad[pl.ds(0, QB), :] = jnp.zeros((QB, D), BF)
    kpad[pl.ds(QB, rows), :] = k[...]
    vpad[pl.ds(QB, rows), :] = v[...]
    acck[...] = jnp.zeros_like(acck)
    accv[...] = jnp.zeros_like(accv)

    def attend(b, _):
        allowed = causal_mask(starts, b)
        span = pl.ds(pl.multiple_of(b * QB, QB), 2 * QB)
        for p in range(PAIRS):
            q2 = two_heads(q[blk(b), lanes(p)], masks)
            go2 = two_heads(ga[blk(b), lanes(p)], masks)
            keys = kpad[span, lanes(p)]
            vals = vpad[span, lanes(p)]
            scores = jnp.where(allowed, nt(keys, q2), masked_score)
            exponent, scale = column_softmax(scores)
            probs = exponent * scale
            accv[span, lanes(p)] += nn(probs.astype(BF), go2)
            gp = nt(vals, go2)
            gs = probs * (gp - jnp.sum(gp * probs, axis=0, keepdims=True))
            gs = gs.astype(BF)
            acck[span, lanes(p)] += nn(gs, q2)
            dq[blk(b), lanes(p)] = (merge_heads(tn(keys, gs)).T * SCALE).astype(BF)
        return 0

    lax.fori_loop(0, rows // QB, attend, 0)
    dk[...] = acck[pl.ds(QB, rows), :].astype(BF)
    dv[...] = accv[pl.ds(QB, rows), :].astype(BF)

    def norm_one(i, _):
        normed, _i = normalise(x[blk(i), :].astype(F32))
        ga[blk(i), :] = (normed * norms[0:1, :] + norms[4:5, :]).astype(BF)
        return 0

    lax.fori_loop(0, rows // QB, norm_one, 0)
    for slot, grad in ((1, dq), (2, dk), (3, dv)):
        gbuf[slot] = tn(ga[...], grad[...]).astype(BF)
        start(stores[slot])
    wait(loads[1])
    big[...] = nt(dq[...], wbuf[1])
    wait(loads[2])
    big[...] += nt(dk[...], wbuf[2])
    wait(loads[3])
    big[...] += nt(dv[...], wbuf[3])

    def back_one(i, _):
        normed, inv_std = normalise(x[blk(i), :].astype(F32))
        grad = big[blk(i), :]
        ng_o[0:1, :] += jnp.sum(grad * normed, axis=0, keepdims=True)
        ng_o[1:2, :] += jnp.sum(grad, axis=0, keepdims=True)
        gt_o[blk(i), :] = (g1[blk(i), :] + norm_back(grad, normed, inv_std, norms[0:1, :])).astype(
            BF
        )
        return 0

    lax.fori_loop(0, rows // QB, back_one, 0)
    for store in stores:
        wait(store)


def run_self_backward(inv, starts, g1, x, q, k, v, att, norms, slots, grads):
    rows = g1.shape[0]
    four = pltpu.VMEM((4, D, D), BF)
    low = pltpu.VMEM((rows, D), BF)
    pad = pltpu.VMEM((rows + QB, D), BF)
    wide = pltpu.VMEM((rows + QB, D), F32)
    sem = pltpu.SemaphoreType.DMA((4, PER))
    return call(
        self_backward,
        (
            jax.ShapeDtypeStruct((rows, D), BF),
            jax.ShapeDtypeStruct((2, D), F32),
            jax.ShapeDtypeStruct(slots.shape, BF),
        ),
        [SM, SM] + [VM] * 7 + [ANY, ANY],
        (VM, VM, ANY),
        [
            four, four, low, low, pad, pad, wide, wide, low, low,
            pltpu.VMEM((rows, D), F32), sem, sem,
        ],
        aliases={10: 2},
    )(inv, starts, g1, x, q, k, v, att, norms, slots, grads)


def from_partner(block, axis):
    half = lax.axis_size(axis) // 2
    count = lax.axis_size(axis)
    return lax.ppermute(block, axis, [(i, (i + half) % count) for i in range(count)])


def adamw_update(weight, moment, second, grad_in, rate, decay_rate):
    new_moment = beta_one * moment + (1.0 - beta_one) * grad_in
    new_second = beta_two * second + (1.0 - beta_two) * grad_in * grad_in
    moment_hat = new_moment / (1.0 - beta_one**STEP)
    second_hat = new_second / (1.0 - beta_two**STEP)
    new_weight = weight - rate * (
        moment_hat / (jnp.sqrt(second_hat) + epsilon) + decay_rate * weight
    )
    return (new_weight, new_moment, new_second)


def caption_plan(lengths, picks, rows, images):
    ends = jnp.cumsum(lengths)
    starts = ends - lengths
    rank = picks * lengths.shape[0] + jnp.arange(lengths.shape[0], dtype=jnp.int32)
    ahead = rank[None, :] < rank[:, None]
    sorted_starts = jnp.sum(jnp.where(ahead, lengths[None, :], 0), axis=1)
    token = jnp.arange(rows, dtype=jnp.int32)
    inside = (token[:, None] >= starts[None, :]) & (token[:, None] < ends[None, :])
    place = token + jnp.sum(jnp.where(inside, (sorted_starts - starts)[None, :], 0), axis=1)
    edges = jnp.arange(images + 1, dtype=jnp.int32)
    bounds = jnp.sum(jnp.where(picks[None, :] < edges[:, None], lengths[None, :], 0), axis=1)
    return place, sorted_starts, bounds


def per_device(
    tokens,
    cotangent,
    caption_lengths,
    image_index,
    image_states,
    master_weights,
    first_moments,
    second_moments,
    owner_list,
    norm_params,
    norm_first,
    norm_second,
):
    rows = tokens.shape[0]
    groups = owner_list.shape[0]
    total_rows = 8 * D + 2 * FF
    group_rows = total_rows // groups
    images = image_states.shape[0]
    axes = ("tower", "dp")
    direct = group_rows == GROUP
    gathered = lax.all_gather(master_weights.astype(BF), axes, axis=0, tiled=True)
    ids = jnp.arange(groups, dtype=jnp.int32)
    inverse = jnp.sum(jnp.where(owner_list[None, :] == ids[:, None], ids[None, :], 0), axis=1)
    if direct:
        slots = gathered.reshape(groups, GROUP, D)
        inv = inverse
    else:
        slots = gathered.reshape(groups, group_rows, D)[inverse].reshape(-1, GROUP, D)
        inv = jnp.arange(total_rows // GROUP, dtype=jnp.int32)

    place, own_starts, own_bounds = caption_plan(caption_lengths[0], image_index[0], rows, images)
    into = (place[None, :] == jnp.arange(rows, dtype=jnp.int32)[:, None]).astype(BF)
    plan = from_partner(jnp.concatenate([own_starts, own_bounds]), "tower")
    starts, bounds = plan[: own_starts.shape[0]], plan[own_starts.shape[0] :]
    sent_tokens = jnp.dot(into, tokens, preferred_element_type=F32).astype(BF)
    sent_cot = jnp.dot(into, cotangent, preferred_element_type=F32).astype(BF)
    x = from_partner(sent_tokens, "tower")
    cot = from_partner(sent_cot, "tower")

    img = image_states.reshape(-1, D)
    normed, _i = normalise(img.astype(F32))
    enc = (normed * norm_params[3] + norm_params[7]).astype(BF)

    q, k, v, att, r1, cq = run_self_forward(inv, starts, x, norm_params, slots)
    ck, cv, cross, r2 = run_cross_forward(images, inv, bounds, enc, cq, r1, slots)
    out, g2, ng3, grads = run_feed_forward(inv, r2, cot, norm_params, slots)
    out_back = from_partner(out, "tower")
    g1, grad_images, ng2, grads = run_cross_backward(
        images, inv, bounds, g2, cross, ck, cv, cq, r1, enc, img, norm_params, slots, grads
    )
    gt, ng1, grads = run_self_backward(
        inv, starts, g1, x, q, k, v, att, norm_params, slots, grads
    )
    gt_back = from_partner(gt, "tower")
    layer_out = lax.dot_general(
        into, out_back, (((0,), (0,)), ((), ())), preferred_element_type=F32
    ).astype(BF)
    grad_tokens = lax.dot_general(
        into, gt_back, (((0,), (0,)), ((), ())), preferred_element_type=F32
    )
    if direct:
        arranged = grads.reshape(total_rows, D)
    else:
        arranged = grads.reshape(groups, group_rows, D)[owner_list].reshape(total_rows, D)
    reduced = lax.psum_scatter(arranged, axes, scatter_dimension=0, tiled=True).astype(F32)
    norm_terms = jnp.stack(
        [ng1[0], ng2[0], ng3[0], ng2[2], ng1[1], ng2[1], ng3[1], ng2[3]]
    )
    norm_grads = lax.psum(norm_terms, axes)
    new_weights, new_first, new_second = adamw_update(
        master_weights, first_moments, second_moments, reduced, learn_rate, weight_decay
    )
    norm_new, norm_first_new, norm_second_new = adamw_update(
        norm_params, norm_first, norm_second, norm_grads, norm_rate, 0.0
    )
    return (
        layer_out,
        grad_tokens,
        grad_images.reshape(image_states.shape),
        new_weights,
        new_first,
        new_second,
        new_weights.astype(BF),
        norm_new,
        norm_first_new,
        norm_second_new,
    )


def solution(mesh):
    split = P(("tower", "dp"), None)
    wide = P(("tower", "dp"), None, None)
    in_specs = (split,) * 4 + (wide,) + (split,) * 3 + (P(),) * 4
    out_specs = (split, split, wide) + (split,) * 4 + (P(),) * 3
    return jax.shard_map(
        per_device, mesh=mesh, in_specs=in_specs, out_specs=out_specs, check_vma=False
    )
```

```python
import functools

import jax
import jax.numpy as jnp
from jax import lax
from jax.experimental import pallas as pl
from jax.experimental.pallas import tpu as pltpu
from jax.sharding import PartitionSpec as P

D = 768
HEADS = 12
HDIM = 64
FF = 3072
STEP = 5
PAIRS = HEADS // 2
LANES = 2 * HDIM
QB = 128
GROUP = 192
BOUND_LANE = 64
PER = D // GROUP
SCALE = HDIM ** (-0.5)

beta_one = 0.5
beta_two = 0.6
learn_rate = 0.03
norm_rate = 0.4
weight_decay = 0.01
epsilon = 1e-08
norm_eps = 1e-05
masked_score = -1000000000.0

W_Q, W_K, W_V, W_O, C_Q, C_K, C_V, C_O, UP, DOWN = 0, 1, 2, 3, 4, 5, 6, 7, 8, 12

BF = jnp.bfloat16
F32 = jnp.float32
VM = pl.BlockSpec(memory_space=pltpu.VMEM)
SM = pl.BlockSpec(memory_space=pltpu.SMEM)
ANY = pl.BlockSpec(memory_space=pl.ANY)
VLIM = 58 * 2**20


def nn(a, b):
    return lax.dot_general(a, b, (((1,), (0,)), ((), ())), preferred_element_type=F32)


def nt(a, b):
    return lax.dot_general(a, b, (((1,), (1,)), ((), ())), preferred_element_type=F32)


def tn(a, b):
    return lax.dot_general(a, b, (((0,), (0,)), ((), ())), preferred_element_type=F32)


def blk(i, size=QB):
    return pl.ds(pl.multiple_of(i * size, size), size)


def lanes(p):
    return slice(p * LANES, (p + 1) * LANES)


def normalise(x):
    centred = x - jnp.mean(x, axis=-1, keepdims=True)
    inv = lax.rsqrt(jnp.mean(centred * centred, axis=-1, keepdims=True) + norm_eps)
    return centred * inv, inv


def norm_back(grad, normed, inv, gain):
    gn = grad * gain
    m1 = jnp.mean(gn, axis=-1, keepdims=True)
    m2 = jnp.mean(gn * normed, axis=-1, keepdims=True)
    return inv * (gn - m1 - normed * m2)


def head_masks():
    low = (lax.broadcasted_iota(jnp.int32, (1, LANES), 1) < HDIM).astype(F32)
    return low.astype(BF), (1.0 - low).astype(BF)


def two_heads(x, masks):
    return jnp.concatenate([x * masks[0], x * masks[1]], axis=0)


def merge_heads(both):
    return jnp.concatenate([both[:HDIM, :QB], both[HDIM:, QB:]], axis=0)


def weight_copies(slots, inv, buf, sem, matrix, slot):
    return [
        pltpu.make_async_copy(
            slots.at[inv[matrix * PER + j]], buf.at[slot, pl.ds(j * GROUP, GROUP)], sem.at[slot, j]
        )
        for j in range(PER)
    ]


def grad_copies(grads, inv, buf, sem, matrix, slot):
    return [
        pltpu.make_async_copy(
            buf.at[slot, pl.ds(j * GROUP, GROUP)], grads.at[inv[matrix * PER + j]], sem.at[slot, j]
        )
        for j in range(PER)
    ]


def start(copies):
    for copy in copies:
        copy.start()


def wait(copies):
    for copy in copies:
        copy.wait()


def causal_mask(meta, captions, b):
    query = lax.broadcasted_iota(jnp.int32, (1, QB), 1) + b * QB
    first = jnp.zeros((1, QB), jnp.int32)
    for c in range(captions):
        first = jnp.maximum(first, jnp.where(query >= meta[0, c], meta[0, c], 0))
    key = lax.broadcasted_iota(jnp.int32, (2 * QB, QB), 0) + (b - 1) * QB
    allowed = (key >= first) & (key <= query)
    return jnp.concatenate([allowed, allowed], axis=1)


def column_softmax(scores):
    top = jnp.max(scores, axis=0, keepdims=True)
    exponent = jnp.exp(scores - top)
    return exponent, 1.0 / jnp.sum(exponent, axis=0, keepdims=True)


def self_forward(
    captions, inv, meta, x, norms, slots, q_o, k_o, v_o, att_o, r1_o, cq_o, wbuf, low, kpad, vpad, wsem
):
    rows = x.shape[0]
    loads = [weight_copies(slots, inv, wbuf, wsem, m, m) for m in range(5)]
    for load in loads:
        start(load)
    masks = head_masks()

    def norm_one(i, _):
        normed, _i = normalise(x[blk(i), :].astype(F32))
        low[blk(i), :] = (normed * norms[0:1, :] + norms[4:5, :]).astype(BF)
        return 0

    lax.fori_loop(0, rows // QB, norm_one, 0)
    kpad[pl.ds(0, QB), :] = jnp.zeros((QB, D), BF)
    vpad[pl.ds(0, QB), :] = jnp.zeros((QB, D), BF)
    wait(loads[0])
    q_o[...] = (nn(low[...], wbuf[0]) * SCALE).astype(BF)
    wait(loads[1])
    kpad[pl.ds(QB, rows), :] = nn(low[...], wbuf[1]).astype(BF)
    wait(loads[2])
    vpad[pl.ds(QB, rows), :] = nn(low[...], wbuf[2]).astype(BF)
    k_o[...] = kpad[pl.ds(QB, rows), :]
    v_o[...] = vpad[pl.ds(QB, rows), :]

    def attend(b, _):
        allowed = causal_mask(meta, captions, b)
        for p in range(PAIRS):
            q2 = two_heads(q_o[blk(b), lanes(p)], masks)
            keys = kpad[pl.ds(pl.multiple_of(b * QB, QB), 2 * QB), lanes(p)]
            vals = vpad[pl.ds(pl.multiple_of(b * QB, QB), 2 * QB), lanes(p)]
            scores = jnp.where(allowed, nt(keys, q2), masked_score)
            exponent, scale = column_softmax(scores)
            out = tn(vals, (exponent * scale).astype(BF))
            att_o[blk(b), lanes(p)] = merge_heads(out).T.astype(BF)
        return 0

    lax.fori_loop(0, rows // QB, attend, 0)
    wait(loads[3])
    r1_o[...] = x[...].astype(F32) + nn(att_o[...], wbuf[3])

    def norm_two(i, _):
        normed, _i = normalise(r1_o[blk(i), :])
        low[blk(i), :] = (normed * norms[1:2, :] + norms[5:6, :]).astype(BF)
        return 0

    lax.fori_loop(0, rows // QB, norm_two, 0)
    wait(loads[4])
    cq_o[...] = (nn(low[...], wbuf[4]) * SCALE).astype(BF)


def call(body, out_shape, in_specs, out_specs, scratch, aliases=None, effects=False):
    return pl.pallas_call(
        body,
        out_shape=out_shape,
        in_specs=in_specs,
        out_specs=out_specs,
        scratch_shapes=scratch,
        input_output_aliases=aliases or {},
        compiler_params=pltpu.CompilerParams(vmem_limit_bytes=VLIM, has_side_effects=effects),
    )


def run_self_forward(captions, inv, meta, x, norms, slots):
    rows = x.shape[0]
    one = jax.ShapeDtypeStruct((rows, D), BF)
    return call(
        functools.partial(self_forward, captions),
        (one, one, one, one, jax.ShapeDtypeStruct((rows, D), F32), one),
        [SM, SM, VM, VM, ANY],
        (VM,) * 6,
        [
            pltpu.VMEM((5, D, D), BF),
            pltpu.VMEM((rows, D), BF),
            pltpu.VMEM((rows + QB, D), BF),
            pltpu.VMEM((rows + QB, D), BF),
            pltpu.SemaphoreType.DMA((5, PER)),
        ],
    )(inv, meta, x, norms, slots)


def image_blocks(meta, i):
    low, high = meta[0, BOUND_LANE + i], meta[0, BOUND_LANE + i + 1]
    first = low // QB
    last = jnp.where(high > low, (high + QB - 1) // QB, first)
    return low, high, first, last


def cross_forward(
    images, inv, meta, enc, cq, r1, slots, k_o, v_o, cross_o, r2_o, wbuf, acc, wsem
):
    patches = enc.shape[0] // images
    loads = [weight_copies(slots, inv, wbuf, wsem, m, i) for i, m in enumerate((C_K, C_V, C_O))]
    for load in loads:
        start(load)
    masks = head_masks()
    cross_o[...] = jnp.zeros_like(cross_o)
    for i, out in ((0, k_o), (1, v_o)):
        wait(loads[i])

        def project(c, _, i=i, out=out):
            out[blk(c, D), :] = nn(enc[blk(c, D), :], wbuf[i]).astype(BF)
            return 0

        lax.fori_loop(0, enc.shape[0] // D, project, 0)

    def image(i, _):
        low, high, first, last = image_blocks(meta, i)

        def attend(b, _):
            token = lax.broadcasted_iota(jnp.int32, (1, QB), 1) + b * QB
            here = ((token >= low) & (token < high)).astype(F32)
            here = jnp.concatenate([here, here], axis=1)
            for p in range(PAIRS):
                q2 = two_heads(cq[blk(b), lanes(p)], masks)
                keys = k_o[blk_of(i, patches), lanes(p)]
                vals = v_o[blk_of(i, patches), lanes(p)]
                exponent, scale = column_softmax(nt(keys, q2))
                out = tn(vals, exponent.astype(BF)) * (scale * here)
                acc[blk(b), lanes(p)] += merge_heads(out).T
            return 0

        lax.fori_loop(first, last, attend, 0)
        return 0

    acc[...] = jnp.zeros_like(acc)
    lax.fori_loop(0, images, image, 0)
    cross_o[...] = acc[...].astype(BF)
    wait(loads[2])
    r2_o[...] = r1[...] + nn(cross_o[...], wbuf[2])


def blk_of(i, size):
    return pl.ds(pl.multiple_of(i * size, 64), size)


def run_cross_forward(images, inv, meta, enc, cq, r1, slots):
    rows = cq.shape[0]
    kv = jax.ShapeDtypeStruct(enc.shape, BF)
    return call(
        functools.partial(cross_forward, images),
        (kv, kv, jax.ShapeDtypeStruct((rows, D), BF), jax.ShapeDtypeStruct((rows, D), F32)),
        [SM, SM, VM, VM, VM, ANY],
        (VM,) * 4,
        [
            pltpu.VMEM((3, D, D), BF),
            pltpu.VMEM((rows, D), F32),
            pltpu.SemaphoreType.DMA((3, PER)),
        ],
    )(inv, meta, enc, cq, r1, slots)


GELU_A = 0.7978845608028654
GELU_B = GELU_A * 0.044715


def feed_forward(
    inv, r2, cot, norms, slots, out_o, g2_o, ng_o, grads,
    wup, wdown, third, pre, gh, hid, gpre, acc, gthird, gup, gdown, usem, dsem, gusem, gdsem,
):
    rows = r2.shape[0]
    chunks = FF // D

    def loads(c, slot):
        return weight_copies(slots, inv, wup, usem, UP + c, slot) + weight_copies(
            slots, inv, wdown, dsem, DOWN + c, slot
        )

    def stores(c, slot):
        return grad_copies(grads, inv, gup, gusem, UP + c, slot) + grad_copies(
            grads, inv, gdown, gdsem, DOWN + c, slot
        )

    start(loads(0, 0))

    def norm_three(i, _):
        normed, _i = normalise(r2[blk(i), :])
        third[blk(i), :] = (normed * norms[2:3, :] + norms[6:7, :]).astype(BF)
        return 0

    lax.fori_loop(0, rows // QB, norm_three, 0)
    acc[...] = r2[...]
    gthird[...] = jnp.zeros_like(gthird)

    def chunk(c, _):
        slot = c % 2

        @pl.when(c + 1 < chunks)
        def _():
            start(loads(c + 1, 1 - slot))

        wait(loads(c, slot))
        pre[...] = nt(third[...], wup[slot])
        gh[...] = nt(cot[...], wdown[slot])

        def gelu(i, _):
            x = pre[blk(i, 64), :]
            x2 = x * x
            t = jnp.tanh(x * (GELU_A + GELU_B * x2))
            half = 0.5 + 0.5 * t
            value = x * half
            hid[blk(i, 64), :] = value.astype(BF)
            slope = half + value * (1.0 - t) * (GELU_A + 3.0 * GELU_B * x2)
            gpre[blk(i, 64), :] = (gh[blk(i, 64), :] * slope).astype(BF)
            return 0

        lax.fori_loop(0, rows // 64, gelu, 0)

        @pl.when(c >= 2)
        def _():
            wait(stores(c - 2, slot))

        acc[...] += nn(hid[...], wdown[slot])
        gdown[slot] = tn(hid[...], cot[...]).astype(BF)
        gup[slot] = tn(gpre[...], third[...]).astype(BF)
        start(stores(c, slot))
        gthird[...] += nn(gpre[...], wup[slot])
        return 0

    lax.fori_loop(0, chunks, chunk, 0)
    out_o[...] = acc[...].astype(BF)
    ng_o[...] = jnp.zeros_like(ng_o)

    def back(i, _):
        normed, inv_std = normalise(r2[blk(i), :])
        grad = gthird[blk(i), :]
        ng_o[0:1, :] += jnp.sum(grad * normed, axis=0, keepdims=True)
        ng_o[1:2, :] += jnp.sum(grad, axis=0, keepdims=True)
        g2_o[blk(i), :] = cot[blk(i), :].astype(F32) + norm_back(
            grad, normed, inv_std, norms[2:3, :]
        )
        return 0

    lax.fori_loop(0, rows // QB, back, 0)
    for c in range(chunks - 2, chunks):
        wait(stores(c, c % 2))


def run_feed_forward(inv, r2, cot, norms, slots):
    rows = r2.shape[0]
    big = pltpu.VMEM((rows, D), F32)
    low = pltpu.VMEM((rows, D), BF)
    two = pltpu.VMEM((2, D, D), BF)
    sem = pltpu.SemaphoreType.DMA((2, PER))
    return call(
        feed_forward,
        (
            jax.ShapeDtypeStruct((rows, D), BF),
            jax.ShapeDtypeStruct((rows, D), F32),
            jax.ShapeDtypeStruct((2, D), F32),
            jax.ShapeDtypeStruct(slots.shape, BF),
        ),
        [SM, VM, VM, VM, ANY],
        (VM, VM, VM, ANY),
        [two, two, low, big, big, low, low, big, big, two, two, sem, sem, sem, sem],
    )(inv, r2, cot, norms, slots)


def cross_backward(
    images, inv, meta, g2, cross, k, v, cq, r1, enc, img, norms, slots, grads_in,
    g1_o, gi_o, ng_o, grads,
    wbuf, gbuf, gca, dq, acck, accv, dk, dv, big, wsem, gsem,
):
    rows = g2.shape[0]
    patches = enc.shape[0] // images
    names = (C_O, C_Q, C_K, C_V)
    loads = [weight_copies(slots, inv, wbuf, wsem, m, i) for i, m in enumerate(names)]
    stores = [grad_copies(grads, inv, gbuf, gsem, m, i) for i, m in enumerate(names)]
    for load in loads:
        start(load)
    masks = head_masks()
    ng_o[...] = jnp.zeros_like(ng_o)
    low = dq
    low[...] = g2[...].astype(BF)
    gbuf[0] = tn(cross[...], low[...]).astype(BF)
    start(stores[0])
    wait(loads[0])
    gca[...] = nt(low[...], wbuf[0]).astype(BF)
    dq[...] = jnp.zeros_like(dq)

    def image(i, _):
        first_row, end_row, first, last = image_blocks(meta, i)
        acck[...] = jnp.zeros_like(acck)
        accv[...] = jnp.zeros_like(accv)

        def attend(b, _):
            token = lax.broadcasted_iota(jnp.int32, (QB, LANES), 0) + b * QB
            here = ((token >= first_row) & (token < end_row)).astype(F32).astype(BF)
            for p in range(PAIRS):
                q2 = two_heads(cq[blk(b), lanes(p)], masks)
                go2 = two_heads(gca[blk(b), lanes(p)] * here, masks)
                keys = k[blk_of(i, patches), lanes(p)]
                vals = v[blk_of(i, patches), lanes(p)]
                exponent, scale = column_softmax(nt(keys, q2))
                probs = exponent * scale
                accv[:, lanes(p)] += nn(probs.astype(BF), go2)
                gp = nt(vals, go2)
                gs = probs * (gp - jnp.sum(gp * probs, axis=0, keepdims=True))
                gs = gs.astype(BF)
                acck[:, lanes(p)] += nn(gs, q2)
                gq = merge_heads(tn(keys, gs)).T * SCALE
                dq[blk(b), lanes(p)] += gq.astype(BF)
            return 0

        lax.fori_loop(first, last, attend, 0)
        dk[blk_of(i, patches), :] = acck[...].astype(BF)
        dv[blk_of(i, patches), :] = accv[...].astype(BF)
        return 0

    lax.fori_loop(0, images, image, 0)
    for slot, grad in ((2, dk), (3, dv)):
        big[...] = jnp.zeros_like(big)

        def gather(c, _, grad=grad):
            big[...] += tn(enc[blk(c, D), :], grad[blk(c, D), :])
            return 0

        lax.fori_loop(0, enc.shape[0] // D, gather, 0)
        gbuf[slot] = big[...].astype(BF)
        start(stores[slot])
    wait(loads[2])
    wait(loads[3])

    def encoder(c, _):
        sent = nt(dk[blk(c, D), :], wbuf[2]) + nt(dv[blk(c, D), :], wbuf[3])
        big[...] = sent

        def back(j, _):
            rows_j = pl.ds(pl.multiple_of(c * D + j * QB, QB), QB)
            normed, inv_std = normalise(img[rows_j, :].astype(F32))
            grad = big[blk(j), :].astype(BF).astype(F32)
            ng_o[2:3, :] += jnp.sum(grad * normed, axis=0, keepdims=True)
            ng_o[3:4, :] += jnp.sum(grad, axis=0, keepdims=True)
            gi_o[rows_j, :] = norm_back(grad, normed, inv_std, norms[3:4, :])
            return 0

        lax.fori_loop(0, D // QB, back, 0)
        return 0

    lax.fori_loop(0, enc.shape[0] // D, encoder, 0)

    def norm_two(i, _):
        normed, _i = normalise(r1[blk(i), :])
        gca[blk(i), :] = (normed * norms[1:2, :] + norms[5:6, :]).astype(BF)
        return 0

    lax.fori_loop(0, rows // QB, norm_two, 0)
    gbuf[1] = tn(gca[...], dq[...]).astype(BF)
    start(stores[1])
    wait(loads[1])
    big[...] = nt(dq[...], wbuf[1])

    def back_two(i, _):
        normed, inv_std = normalise(r1[blk(i), :])
        grad = big[blk(i), :]
        ng_o[0:1, :] += jnp.sum(grad * normed, axis=0, keepdims=True)
        ng_o[1:2, :] += jnp.sum(grad, axis=0, keepdims=True)
        g1_o[blk(i), :] = g2[blk(i), :] + norm_back(grad, normed, inv_std, norms[1:2, :])
        return 0

    lax.fori_loop(0, rows // QB, back_two, 0)
    for store in stores:
        wait(store)


def run_cross_backward(images, inv, meta, g2, cross, k, v, cq, r1, enc, img, norms, slots, grads):
    rows = g2.shape[0]
    patches = enc.shape[0] // images
    four = pltpu.VMEM((4, D, D), BF)
    low = pltpu.VMEM((rows, D), BF)
    part = pltpu.VMEM((patches, D), F32)
    wide = pltpu.VMEM(enc.shape, BF)
    sem = pltpu.SemaphoreType.DMA((4, PER))
    return call(
        functools.partial(cross_backward, images),
        (
            jax.ShapeDtypeStruct((rows, D), F32),
            jax.ShapeDtypeStruct(enc.shape, F32),
            jax.ShapeDtypeStruct((4, D), F32),
            jax.ShapeDtypeStruct(slots.shape, BF),
        ),
        [SM, SM] + [VM] * 9 + [ANY, ANY],
        (VM, VM, VM, ANY),
        [four, four, low, low, part, part, wide, wide, pltpu.VMEM((D, D), F32), sem, sem],
        aliases={12: 3},
    )(inv, meta, g2, cross, k, v, cq, r1, enc, img, norms, slots, grads)


def self_backward(
    captions, inv, meta, g1, x, q, k, v, att, norms, slots, grads_in,
    gt_o, ng_o, grads,
    wbuf, gbuf, ga, dq, kpad, vpad, acck, accv, dk, dv, big, wsem, gsem,
):
    rows = g1.shape[0]
    names = (W_O, W_Q, W_K, W_V)
    loads = [weight_copies(slots, inv, wbuf, wsem, m, i) for i, m in enumerate(names)]
    stores = [grad_copies(grads, inv, gbuf, gsem, m, i) for i, m in enumerate(names)]
    for load in loads:
        start(load)
    masks = head_masks()
    ng_o[...] = jnp.zeros_like(ng_o)
    low = dq
    low[...] = g1[...].astype(BF)
    gbuf[0] = tn(att[...], low[...]).astype(BF)
    start(stores[0])
    wait(loads[0])
    ga[...] = nt(low[...], wbuf[0]).astype(BF)
    kpad[pl.ds(0, QB), :] = jnp.zeros((QB, D), BF)
    vpad[pl.ds(0, QB), :] = jnp.zeros((QB, D), BF)
    kpad[pl.ds(QB, rows), :] = k[...]
    vpad[pl.ds(QB, rows), :] = v[...]
    acck[...] = jnp.zeros_like(acck)
    accv[...] = jnp.zeros_like(accv)

    def attend(b, _):
        allowed = causal_mask(meta, captions, b)
        span = pl.ds(pl.multiple_of(b * QB, QB), 2 * QB)
        for p in range(PAIRS):
            q2 = two_heads(q[blk(b), lanes(p)], masks)
            go2 = two_heads(ga[blk(b), lanes(p)], masks)
            keys = kpad[span, lanes(p)]
            vals = vpad[span, lanes(p)]
            scores = jnp.where(allowed, nt(keys, q2), masked_score)
            exponent, scale = column_softmax(scores)
            probs = exponent * scale
            accv[span, lanes(p)] += nn(probs.astype(BF), go2)
            gp = nt(vals, go2)
            gs = probs * (gp - jnp.sum(gp * probs, axis=0, keepdims=True))
            gs = gs.astype(BF)
            acck[span, lanes(p)] += nn(gs, q2)
            dq[blk(b), lanes(p)] = (merge_heads(tn(keys, gs)).T * SCALE).astype(BF)
        return 0

    lax.fori_loop(0, rows // QB, attend, 0)
    dk[...] = acck[pl.ds(QB, rows), :].astype(BF)
    dv[...] = accv[pl.ds(QB, rows), :].astype(BF)

    def norm_one(i, _):
        normed, _i = normalise(x[blk(i), :].astype(F32))
        ga[blk(i), :] = (normed * norms[0:1, :] + norms[4:5, :]).astype(BF)
        return 0

    lax.fori_loop(0, rows // QB, norm_one, 0)
    for slot, grad in ((1, dq), (2, dk), (3, dv)):
        gbuf[slot] = tn(ga[...], grad[...]).astype(BF)
        start(stores[slot])
    wait(loads[1])
    big[...] = nt(dq[...], wbuf[1])
    wait(loads[2])
    big[...] += nt(dk[...], wbuf[2])
    wait(loads[3])
    big[...] += nt(dv[...], wbuf[3])

    def back_one(i, _):
        normed, inv_std = normalise(x[blk(i), :].astype(F32))
        grad = big[blk(i), :]
        ng_o[0:1, :] += jnp.sum(grad * normed, axis=0, keepdims=True)
        ng_o[1:2, :] += jnp.sum(grad, axis=0, keepdims=True)
        gt_o[blk(i), :] = (g1[blk(i), :] + norm_back(grad, normed, inv_std, norms[0:1, :])).astype(
            BF
        )
        return 0

    lax.fori_loop(0, rows // QB, back_one, 0)
    for store in stores:
        wait(store)


def run_self_backward(captions, inv, meta, g1, x, q, k, v, att, norms, slots, grads):
    rows = g1.shape[0]
    four = pltpu.VMEM((4, D, D), BF)
    low = pltpu.VMEM((rows, D), BF)
    pad = pltpu.VMEM((rows + QB, D), BF)
    wide = pltpu.VMEM((rows + QB, D), F32)
    sem = pltpu.SemaphoreType.DMA((4, PER))
    return call(
        functools.partial(self_backward, captions),
        (
            jax.ShapeDtypeStruct((rows, D), BF),
            jax.ShapeDtypeStruct((2, D), F32),
            jax.ShapeDtypeStruct(slots.shape, BF),
        ),
        [SM, SM] + [VM] * 7 + [ANY, ANY],
        (VM, VM, ANY),
        [
            four, four, low, low, pad, pad, wide, wide, low, low,
            pltpu.VMEM((rows, D), F32), sem, sem,
        ],
        aliases={10: 2},
    )(inv, meta, g1, x, q, k, v, att, norms, slots, grads)


MESH = pl.DeviceIdType.MESH
PART_ROWS = (256, 128)
PART_OFF = (0, 256)
X_, Y_, UP_, DN_ = 0, 1, 2, 3
OPPOSITE = (X_, Y_, DN_, UP_)
ARRIVALS = (
    (1, 1, 0, 0), (0, 0, 0, 1), (0, 0, 1, 0), (1, 0, 1, 0), (1, 0, 0, 1), (0, 1, 0, 0),
    (1, 1, 1, 0), (1, 1, 0, 1), (0, 0, 2, 0), (1, 0, 1, 1), (0, 0, 1, 1), (1, 0, 2, 0),
    (1, 1, 1, 1), (0, 1, 0, 1), (1, 1, 2, 0), (0, 0, 2, 1), (0, 1, 1, 0), (0, 0, 3, 0),
    (1, 0, 2, 1), (1, 0, 3, 0), (1, 1, 2, 1), (0, 1, 2, 0), (0, 1, 1, 1), (0, 1, 3, 0),
    (0, 0, 3, 1), (1, 1, 3, 0), (1, 0, 3, 1), (0, 1, 2, 1), (1, 1, 3, 1), (0, 1, 3, 1),
)
OWN_SENDS = (
    (1, X_), (0, Y_), (0, UP_), (0, DN_), (1, UP_), (1, DN_), (1, Y_), (0, X_),
)
Z_CHIPS = 4


def signed_arrivals():
    for part, dt, dz, dy in ARRIVALS:
        for step in (-dz, dz) if dz else (0,):
            yield part, dt, step, dy


def routes(part, dt, dz, dy):
    along = [UP_] * (dz <= 0) + [DN_] * (dz >= 0)
    if part == 0:
        return [] if dy else [Y_] if dt else along + [X_, Y_]
    return along if dz or dy else along + [Y_] if dt else [X_, Y_] + along


def source(part, dt, dz, dy):
    last = UP_ if dz > 0 else DN_
    if part == 0:
        return Y_ if dy else X_ if dt else last
    return last if dz else Y_ if dy else X_


class Place:
    def __init__(self):
        self.t = lax.axis_index("tower")
        d = lax.axis_index("dp")
        self.z, self.y, self.c = d // 4, (d // 2) % 2, d % 2

    def device(self, t, z, y, c):
        return (t, z * 4 + y * 2 + c)

    def neighbour(self, kind):
        t, z, y, c = self.t, self.z, self.y, self.c
        return (
            self.device(1 - t, z, y, c),
            self.device(t, z, 1 - y, c),
            self.device(t, jnp.minimum(z + 1, Z_CHIPS - 1), y, c),
            self.device(t, jnp.maximum(z - 1, 0), y, c),
        )[kind]

    def line(self):
        return [
            self.device(self.t, lax.rem(self.z + k, Z_CHIPS), self.y, self.c)
            for k in range(1, Z_CHIPS)
        ]

    def sibling(self):
        return self.device(self.t, self.z, self.y, 1 - self.c)

    def has(self, kind):
        return {UP_: self.z < Z_CHIPS - 1, DN_: self.z > 0}.get(kind)

    def chip(self, dt=0, dz=0, dy=0):
        t = 1 - self.t if dt else self.t
        y = 1 - self.y if dy else self.y
        return t * 8 + (self.z + dz) * 2 + y

    def exists(self, dz):
        return None if dz == 0 else self.z >= -dz if dz < 0 else self.z < Z_CHIPS - dz


def rows_of(chip, core, part):
    return pl.ds(
        pl.multiple_of((chip * 2 + core) * sum(PART_ROWS) + PART_OFF[part], 128), PART_ROWS[part]
    )


def both(first, second):
    return second if first is None else first if second is None else first & second


def when(condition, body):
    if condition is None:
        body()
    else:
        pl.when(condition)(body)


def greet(place, whole_line):
    barrier = pltpu.get_barrier_semaphore()
    targets = [place.neighbour(X_), place.neighbour(Y_), place.sibling()]
    if whole_line:
        targets += place.line()
    for target in targets:
        pl.semaphore_signal(barrier, inc=1, device_id=target, device_id_type=MESH)
    if whole_line:
        pl.semaphore_wait(barrier, len(targets))
        return
    for kind in (UP_, DN_):

        @pl.when(place.has(kind))
        def _(kind=kind):
            pl.semaphore_signal(
                barrier, inc=1, device_id=place.neighbour(kind), device_id_type=MESH
            )

    inner = (place.z > 0) & (place.z < Z_CHIPS - 1)
    pl.semaphore_wait(barrier, jnp.where(inner, len(targets) + 2, len(targets) + 1))


def plan_captions(lengths, picks, start_s, sorted_s, bound_s, images):
    captions = lengths.shape[1]

    def begin(c, run):
        start_s[c] = run
        return run + lengths[0, c]

    lax.fori_loop(0, captions, begin, jnp.int32(0))

    def image(i, run):
        bound_s[i] = run

        def caption(c, run):
            hit = picks[0, c] == i
            sorted_s[c] = jnp.where(hit, run, sorted_s[c])
            return run + jnp.where(hit, lengths[0, c], 0)

        return lax.fori_loop(0, captions, caption, run)

    def clear(c, run):
        sorted_s[c] = 0
        return run

    lax.fori_loop(0, captions, clear, 0)
    bound_s[images] = lax.fori_loop(0, images, image, jnp.int32(0))


def gather_kernel(
    images, lengths, picks, tokens, cot, img, master, norms,
    slots, x_o, meta_o, cot_o, enc_o, place_o,
    own, xs, metas, start_s, sorted_s, bound_s,
    ssem, rsem, sibsem, sibrecv, xsem, lsem,
):
    place = Place()
    rows = tokens.shape[0]
    captions = lengths.shape[1]
    own[...] = master[...].astype(BF)
    greet(place, False)
    sends = []

    def push(condition, part, chip, kind, mine=False):
        target = place.sibling() if kind == 4 else place.neighbour(kind)
        if kind < 4:
            condition = both(condition, place.has(kind))
        rows_p = rows_of(chip, place.c, part)
        src = own.at[pl.ds(PART_OFF[part], PART_ROWS[part])] if mine else slots.at[rows_p]
        sem = sibrecv if kind == 4 else rsem
        out = sibsem.at[part, chip] if kind == 4 else ssem.at[kind, part, chip]
        copy = pltpu.make_async_remote_copy(
            src_ref=src, dst_ref=slots.at[rows_p], send_sem=out, recv_sem=sem.at[part, chip],
            device_id=target, device_id_type=MESH,
        )
        when(condition, copy.start)
        sends.append((condition, copy))

    me = place.chip()
    for part, kind in OWN_SENDS + ((0, 4), (1, 4)):
        push(None, part, me, kind, mine=True)
    keep = pltpu.make_async_copy(
        own, slots.at[pl.ds(pl.multiple_of((me * 2 + place.c) * own.shape[0], 128), own.shape[0])], lsem
    )
    keep.start()

    plan_captions(lengths, picks, start_s, sorted_s, bound_s, images)
    token = lax.broadcasted_iota(jnp.int32, (1, rows), 1)

    def locate(c, where_to):
        inside = (token >= start_s[c]) & (token < start_s[c] + lengths[0, c])
        return jnp.where(inside, token + (sorted_s[c] - start_s[c]), where_to)

    where_to = lax.fori_loop(0, captions, locate, token)
    place_o[...] = jnp.broadcast_to(where_to, place_o.shape)
    lane = lax.broadcasted_iota(jnp.int32, metas.shape, 1)

    def note(c, row):
        return jnp.where(lane == c, sorted_s[c], row)

    row = lax.fori_loop(0, captions, note, jnp.zeros(metas.shape, jnp.int32))
    for i in range(images + 1):
        row = jnp.where(lane == BOUND_LANE + i, bound_s[i], row)
    metas[...] = row

    def sort(out, array):
        def body(b, _):
            target = lax.broadcasted_iota(jnp.int32, (QB, rows), 0) + b * QB
            onehot = (target == place_o[0:1, :]).astype(F32).astype(BF)
            out[blk(b), :] = nn(onehot, array[...]).astype(BF)
            return 0

        lax.fori_loop(0, rows // QB, body, 0)

    sort(xs, tokens)
    swaps = []
    for i, (src, dst) in enumerate(((metas, meta_o), (xs, x_o))):
        swaps.append(
            pltpu.make_async_remote_copy(
                src_ref=src, dst_ref=dst, send_sem=xsem.at[0, i], recv_sem=xsem.at[1, i],
                device_id=place.neighbour(X_), device_id_type=MESH,
            )
        )
        swaps[-1].start()

    def encode(i):
        def body(j, _):
            at = pl.ds(pl.multiple_of(i * IMG_ROWS + j * 64, 64), 64)
            normed, _i = normalise(img[at, :].astype(F32))
            enc_o[at, :] = (normed * norms[3:4, :] + norms[7:8, :]).astype(BF)
            return 0

        lax.fori_loop(0, IMG_ROWS // 64, body, 0)

    steps = img.shape[0] // IMG_ROWS
    done = 0
    for number, (part, dt, dz, dy) in enumerate(signed_arrivals()):
        there = place.exists(dz)
        chip = place.chip(dt, dz, dy)

        def arrived(part=part, chip=chip):
            rows_p = rows_of(chip, place.c, part)
            pltpu.make_async_remote_copy(
                src_ref=slots.at[rows_p], dst_ref=slots.at[rows_p], send_sem=ssem.at[0, part, chip],
                recv_sem=rsem.at[part, chip], device_id=place.neighbour(X_), device_id_type=MESH,
            ).wait_recv()

        when(there, arrived)
        for kind in routes(part, dt, dz, dy) + [4]:
            push(there, part, chip, kind)
        if number == 4:
            sort(cot_o, cot)
        if number >= 6 and done < steps:
            encode(done)
            done += 1
    for i in range(done, steps):
        encode(i)

    def from_sibling(chip, _):
        for part in range(2):
            rows_p = rows_of(chip, 1 - place.c, part)
            pltpu.make_async_remote_copy(
                src_ref=slots.at[rows_p], dst_ref=slots.at[rows_p], send_sem=sibsem.at[part, chip],
                recv_sem=sibrecv.at[part, chip], device_id=place.sibling(), device_id_type=MESH,
            ).wait_recv()
        return 0

    lax.fori_loop(0, 4 * Z_CHIPS, from_sibling, 0)
    for condition, copy in sends:
        when(condition, copy.wait_send)
    for swap in swaps:
        swap.wait()
    keep.wait()


IMG_ROWS = 192


def run_gather(images, lengths, picks, tokens, cot, img, master, norms, total_rows):
    rows = tokens.shape[0]
    dma = pltpu.SemaphoreType.DMA
    low = jax.ShapeDtypeStruct((rows, D), BF)
    return pl.pallas_call(
        functools.partial(gather_kernel, images),
        out_shape=(
            jax.ShapeDtypeStruct((total_rows, D), BF),
            low,
            jax.ShapeDtypeStruct((8, 128), jnp.int32),
            low,
            jax.ShapeDtypeStruct(img.shape, BF),
            jax.ShapeDtypeStruct((8, rows), jnp.int32),
        ),
        in_specs=[SM, SM, VM, VM, VM, VM, VM],
        out_specs=(ANY, ANY, ANY, VM, VM, VM),
        scratch_shapes=[
            pltpu.VMEM(master.shape, BF),
            pltpu.VMEM((rows, D), BF),
            pltpu.VMEM((8, 128), jnp.int32),
            pltpu.SMEM((lengths.shape[1],), jnp.int32),
            pltpu.SMEM((lengths.shape[1],), jnp.int32),
            pltpu.SMEM((images + 1,), jnp.int32),
            dma((4, 2, 16)),
            dma((2, 16)),
            dma((2, 16)),
            dma((2, 16)),
            dma((2, 2)),
            dma,
        ],
        compiler_params=pltpu.CompilerParams(
            vmem_limit_bytes=VLIM, has_side_effects=True, collective_id=0
        ),
    )(lengths, picks, tokens, cot, img, master, norms)


def sum_kernel(
    grads, norm_terms, place_row, gt, out_back,
    red_o, norm_o, gt_o, lay_o,
    acc, sib, ya, xa, ba, aa, zb_b, zb_a, yb, xb, gtr, nbuf, nrecv,
    lsem, sibsem, sibrecv, ssem, rsem, gsem, nsend, nrs,
):
    place = Place()
    rows = gt.shape[0]
    greet(place, True)
    order = list(signed_arrivals())[::-1] + [(0, 0, 0, 0), (1, 0, 0, 0)]
    sends = []

    def local(part, chip):
        off = pl.ds(PART_OFF[part], PART_ROWS[part])
        return pltpu.make_async_copy(
            grads.at[rows_of(chip, place.c, part)], acc.at[chip, off], lsem.at[part, chip]
        )

    def across(part, chip):
        off = pl.ds(PART_OFF[part], PART_ROWS[part])
        return pltpu.make_async_remote_copy(
            src_ref=grads.at[rows_of(chip, 1 - place.c, part)], dst_ref=sib.at[chip, off],
            send_sem=sibsem.at[part, chip], recv_sem=sibrecv.at[part, chip],
            device_id=place.sibling(), device_id_type=MESH,
        )

    for part, dt, dz, dy in order:
        chip = place.chip(dt, dz, dy)

        def begin(part=part, chip=chip):
            across(part, chip).start()
            local(part, chip).start()

        when(place.exists(dz), begin)
    back = pltpu.make_async_remote_copy(
        src_ref=gt, dst_ref=gtr, send_sem=gsem.at[0], recv_sem=gsem.at[1],
        device_id=place.neighbour(X_), device_id_type=MESH,
    )
    back.start()

    def landing(part, kind, chip):
        t, z = chip // 8, (chip // 2) % Z_CHIPS
        if part == 0:
            ref, index = {X_: (xa, z), Y_: (ya, t * Z_CHIPS + z), UP_: (ba, z), DN_: (aa, z)}[kind]
        else:
            ref, index = {X_: (xb, 0), Y_: (yb, t), UP_: (zb_b, chip), DN_: (zb_a, chip)}[kind]
        return ref.at[index]

    def flow(part, kind, chip):
        off = pl.ds(PART_OFF[part], PART_ROWS[part])
        return pltpu.make_async_remote_copy(
            src_ref=acc.at[chip, off], dst_ref=landing(part, kind, chip),
            send_sem=ssem.at[part, chip], recv_sem=rsem.at[kind, part, chip],
            device_id=place.neighbour(kind), device_id_type=MESH,
        )

    def add(part, chip, other, final):
        def body(i, _):
            at = pl.ds(pl.multiple_of(PART_OFF[part] + i * 64, 64), 64)
            value = acc[chip, at, :].astype(F32)
            for ref in other:
                value = value + ref(part, pl.ds(pl.multiple_of(i * 64, 64), 64), at).astype(F32)
            if final:
                red_o[at, :] = value
            else:
                acc[chip, at, :] = value.astype(BF)
            return 0

        lax.fori_loop(0, PART_ROWS[part] // 64, body, 0)

    def norm_round(i, target):
        return pltpu.make_async_remote_copy(
            src_ref=nbuf.at[i], dst_ref=nrecv.at[i], send_sem=nsend.at[i], recv_sem=nrs.at[i],
            device_id=target, device_id_type=MESH,
        )

    def norm_line(k, target):
        return pltpu.make_async_remote_copy(
            src_ref=nbuf.at[3], dst_ref=nrecv.at[3 + place.z], send_sem=nsend.at[3 + k],
            recv_sem=nrs.at[3 + place.z], device_id=target, device_id_type=MESH,
        )

    def norm_from(z):
        return pltpu.make_async_remote_copy(
            src_ref=nbuf.at[3], dst_ref=nrecv.at[3 + z], send_sem=nsend.at[3], recv_sem=nrs.at[3 + z],
            device_id=place.neighbour(X_), device_id_type=MESH,
        )

    line = [norm_line(k, target) for k, target in enumerate(place.line())]
    rounds = [place.sibling(), place.neighbour(X_), place.neighbour(Y_)]
    nbuf[0] = norm_terms[...]
    norm_round(0, rounds[0]).start()

    def unsort(out, array):
        def body(b, _):
            target = lax.broadcasted_iota(jnp.int32, (rows, QB), 0)
            onehot = (target == place_row[0:1, blk(b)]).astype(F32).astype(BF)
            out[blk(b), :] = tn(onehot, array[...]).astype(out.dtype)
            return 0

        lax.fori_loop(0, rows // QB, body, 0)

    for number, (part, dt, dz, dy) in enumerate(order):
        chip = place.chip(dt, dz, dy)
        there = place.exists(dz)
        final = (dt, dz, dy) == (0, 0, 0)
        kinds = routes(part, dt, dz, dy)

        def step(part=part, chip=chip, kinds=kinds, final=final, dt=dt, dz=dz, dy=dy):
            local(part, chip).wait()
            across(part, chip).wait_recv()
            refs = [lambda p, i, at: sib[chip, at, :]]
            fixed = [kind for kind in kinds if kind in (X_, Y_)]
            edge = [kind for kind in kinds if kind in (UP_, DN_)]
            for kind in fixed:
                flow(part, OPPOSITE[kind], chip).wait_recv()
                refs.append(
                    lambda p, i, at, kind=kind: landing(part, OPPOSITE[kind], chip)[i, :]
                )
            for kind in edge:

                def one(kind=kind):
                    flow(part, OPPOSITE[kind], chip).wait_recv()
                    add(part, chip, [lambda p, i, at: landing(part, OPPOSITE[kind], chip)[i, :]], False)

                pl.when(place.has(kind))(one)
            add(part, chip, refs, final)
            if not final:
                flow(part, source(part, dt, dz, dy), chip).start()

        when(there, step)
        if not final:
            sends.append((there, part, chip, source(part, dt, dz, dy)))
        if number in (12, 20, 28):
            i = (12, 20, 28).index(number)
            norm_round(i, rounds[i]).wait()
            nbuf[i + 1] = nbuf[i] + nrecv[i]
            if i < 2:
                norm_round(i + 1, rounds[i + 1]).start()
            else:
                for copy in line:
                    copy.start()
        if number == 16:
            unsort(lay_o, out_back)
        if number == 40:
            back.wait()
            unsort(gt_o, gtr)

    for z in range(Z_CHIPS):

        @pl.when(place.z != z)
        def _(z=z):
            norm_from(z).wait_recv()

        @pl.when(place.z == z)
        def _(z=z):
            nrecv[3 + z] = nbuf[3]

    norm_o[...] = (nrecv[3] + nrecv[4]) + (nrecv[5] + nrecv[6])
    for copy in line:
        copy.wait_send()
    for there, part, chip, kind in sends:
        when(there, flow(part, kind, chip).wait_send)

    def sent(chip, _):
        for part in range(2):
            across(part, chip).wait_send()
        return 0

    lax.fori_loop(0, 4 * Z_CHIPS, sent, 0)


def run_sum(grads, norm_terms, place_row, gt, out_back):
    rows = gt.shape[0]
    dma = pltpu.SemaphoreType.DMA
    a, b = PART_ROWS
    shard = a + b
    line = 4 * Z_CHIPS
    return pl.pallas_call(
        sum_kernel,
        out_shape=(
            jax.ShapeDtypeStruct((shard, D), F32),
            jax.ShapeDtypeStruct((8, D), F32),
            jax.ShapeDtypeStruct((rows, D), F32),
            jax.ShapeDtypeStruct((rows, D), BF),
        ),
        in_specs=[ANY, VM, VM, ANY, VM],
        out_specs=(VM,) * 4,
        scratch_shapes=[
            pltpu.VMEM((line, shard, D), BF),
            pltpu.VMEM((line, shard, D), BF),
            pltpu.VMEM((2 * Z_CHIPS, a, D), BF),
            pltpu.VMEM((Z_CHIPS, a, D), BF),
            pltpu.VMEM((Z_CHIPS, a, D), BF),
            pltpu.VMEM((Z_CHIPS, a, D), BF),
            pltpu.VMEM((line, b, D), BF),
            pltpu.VMEM((line, b, D), BF),
            pltpu.VMEM((2, b, D), BF),
            pltpu.VMEM((1, b, D), BF),
            pltpu.VMEM((rows, D), BF),
            pltpu.VMEM((4, 8, D), F32),
            pltpu.VMEM((7, 8, D), F32),
            dma((2, line)),
            dma((2, line)),
            dma((2, line)),
            dma((2, line)),
            dma((4, 2, line)),
            dma((2,)),
            dma((7,)),
            dma((7,)),
        ],
        compiler_params=pltpu.CompilerParams(
            vmem_limit_bytes=VLIM, has_side_effects=True, collective_id=1
        ),
    )(grads, norm_terms, place_row, gt, out_back)


def from_partner(block, axis):
    half = lax.axis_size(axis) // 2
    count = lax.axis_size(axis)
    return lax.ppermute(block, axis, [(i, (i + half) % count) for i in range(count)])


def adamw_update(weight, moment, second, grad_in, rate, decay_rate):
    new_moment = beta_one * moment + (1.0 - beta_one) * grad_in
    new_second = beta_two * second + (1.0 - beta_two) * grad_in * grad_in
    moment_hat = new_moment / (1.0 - beta_one**STEP)
    second_hat = new_second / (1.0 - beta_two**STEP)
    new_weight = weight - rate * (
        moment_hat / (jnp.sqrt(second_hat) + epsilon) + decay_rate * weight
    )
    return (new_weight, new_moment, new_second)


def caption_plan(lengths, picks, rows, images):
    ends = jnp.cumsum(lengths)
    starts = ends - lengths
    rank = picks * lengths.shape[0] + jnp.arange(lengths.shape[0], dtype=jnp.int32)
    ahead = rank[None, :] < rank[:, None]
    sorted_starts = jnp.sum(jnp.where(ahead, lengths[None, :], 0), axis=1)
    token = jnp.arange(rows, dtype=jnp.int32)
    inside = (token[:, None] >= starts[None, :]) & (token[:, None] < ends[None, :])
    place = token + jnp.sum(jnp.where(inside, (sorted_starts - starts)[None, :], 0), axis=1)
    edges = jnp.arange(images + 1, dtype=jnp.int32)
    bounds = jnp.sum(jnp.where(picks[None, :] < edges[:, None], lengths[None, :], 0), axis=1)
    return place, sorted_starts, bounds


def per_device(
    kernels,
    tokens,
    cotangent,
    caption_lengths,
    image_index,
    image_states,
    master_weights,
    first_moments,
    second_moments,
    owner_list,
    norm_params,
    norm_first,
    norm_second,
):
    rows = tokens.shape[0]
    groups = owner_list.shape[0]
    total_rows = 8 * D + 2 * FF
    group_rows = total_rows // groups
    images = image_states.shape[0]
    captions = caption_lengths.shape[1]
    axes = ("tower", "dp")
    direct = group_rows == GROUP
    ids = jnp.arange(groups, dtype=jnp.int32)
    inverse = jnp.sum(jnp.where(owner_list[None, :] == ids[:, None], ids[None, :], 0), axis=1)
    img = image_states.reshape(-1, D)
    if kernels:
        gathered, x, meta, sent_cot, enc, place_row = run_gather(
            images, caption_lengths, image_index, tokens, cotangent, img, master_weights,
            norm_params, total_rows,
        )
    else:
        gathered = lax.all_gather(master_weights.astype(BF), axes, axis=0, tiled=True)
        place, starts, bounds = caption_plan(caption_lengths[0], image_index[0], rows, images)
        into = (place[None, :] == jnp.arange(rows, dtype=jnp.int32)[:, None]).astype(BF)
        meta = jnp.zeros((8, 128), jnp.int32)
        meta = meta.at[0, :captions].set(starts)
        meta = meta.at[0, BOUND_LANE : BOUND_LANE + images + 1].set(bounds)
        meta = from_partner(meta, "tower")
        x = from_partner(nn(into, tokens).astype(BF), "tower")
        sent_cot = nn(into, cotangent).astype(BF)
        normed, _i = normalise(img.astype(F32))
        enc = (normed * norm_params[3] + norm_params[7]).astype(BF)
    if direct:
        slots = gathered.reshape(groups, GROUP, D)
        inv = inverse
    else:
        slots = gathered.reshape(groups, group_rows, D)[inverse].reshape(-1, GROUP, D)
        inv = jnp.arange(total_rows // GROUP, dtype=jnp.int32)
    cot = from_partner(sent_cot, "tower")
    q, k, v, att, r1, cq = run_self_forward(captions, inv, meta, x, norm_params, slots)
    ck, cv, cross, r2 = run_cross_forward(images, inv, meta, enc, cq, r1, slots)
    out, g2, ng3, grads = run_feed_forward(inv, r2, cot, norm_params, slots)
    out_back = from_partner(out, "tower")
    g1, grad_images, ng2, grads = run_cross_backward(
        images, inv, meta, g2, cross, ck, cv, cq, r1, enc, img, norm_params, slots, grads
    )
    gt, ng1, grads = run_self_backward(
        captions, inv, meta, g1, x, q, k, v, att, norm_params, slots, grads
    )
    norm_terms = jnp.stack([ng1[0], ng2[0], ng3[0], ng2[2], ng1[1], ng2[1], ng3[1], ng2[3]])
    if kernels:
        reduced, norm_grads, grad_tokens, layer_out = run_sum(
            grads.reshape(total_rows, D), norm_terms, place_row, gt, out_back
        )
    else:
        layer_out = tn(into, out_back).astype(BF)
        grad_tokens = tn(into, from_partner(gt, "tower"))
        if direct:
            arranged = grads.reshape(total_rows, D)
        else:
            arranged = grads.reshape(groups, group_rows, D)[owner_list].reshape(total_rows, D)
        reduced = lax.psum_scatter(arranged, axes, scatter_dimension=0, tiled=True).astype(F32)
        norm_grads = lax.psum(norm_terms, axes)
    new_weights, new_first, new_second = adamw_update(
        master_weights, first_moments, second_moments, reduced, learn_rate, weight_decay
    )
    norm_new, norm_first_new, norm_second_new = adamw_update(
        norm_params, norm_first, norm_second, norm_grads, norm_rate, 0.0
    )
    return (
        layer_out,
        grad_tokens,
        grad_images.reshape(image_states.shape),
        new_weights,
        new_first,
        new_second,
        new_weights.astype(BF),
        norm_new,
        norm_first_new,
        norm_second_new,
    )


def solution(mesh):
    split = P(("tower", "dp"), None)
    wide = P(("tower", "dp"), None, None)
    in_specs = (split,) * 4 + (wide,) + (split,) * 3 + (P(),) * 4
    out_specs = (split, split, wide) + (split,) * 4 + (P(),) * 3
    shape = dict(mesh.shape)
    kernels = shape["tower"] == 2 and shape["dp"] == 4 * Z_CHIPS
    return jax.shard_map(
        functools.partial(per_device, kernels),
        mesh=mesh,
        in_specs=in_specs,
        out_specs=out_specs,
        check_vma=False,
    )
```

```python
import functools

import jax
import jax.numpy as jnp
from jax import lax
from jax.experimental import pallas as pl
from jax.experimental.pallas import tpu as pltpu
from jax.sharding import PartitionSpec as P

D = 768
HEADS = 12
HDIM = 64
FF = 3072
STEP = 5
PAIRS = HEADS // 2
LANES = 2 * HDIM
QB = 128
PAIR_GROUPS = ((0, 1, 2), (3, 4, 5))
GROUP = 192
BOUND_LANE = 64
PER = D // GROUP
SCALE = HDIM ** (-0.5)

beta_one = 0.5
beta_two = 0.6
learn_rate = 0.03
norm_rate = 0.4
weight_decay = 0.01
epsilon = 1e-08
norm_eps = 1e-05
masked_score = -1000000000.0

W_Q, W_K, W_V, W_O, C_Q, C_K, C_V, C_O, UP, DOWN = 0, 1, 2, 3, 4, 5, 6, 7, 8, 12

BF = jnp.bfloat16
F32 = jnp.float32
VM = pl.BlockSpec(memory_space=pltpu.VMEM)
SM = pl.BlockSpec(memory_space=pltpu.SMEM)
ANY = pl.BlockSpec(memory_space=pl.ANY)
VLIM = 58 * 2**20


def nn(a, b):
    return lax.dot_general(a, b, (((1,), (0,)), ((), ())), preferred_element_type=F32)


def nt(a, b):
    return lax.dot_general(a, b, (((1,), (1,)), ((), ())), preferred_element_type=F32)


def tn(a, b):
    return lax.dot_general(a, b, (((0,), (0,)), ((), ())), preferred_element_type=F32)


def blk(i, size=QB):
    return pl.ds(pl.multiple_of(i * size, size), size)


def lanes(p):
    return slice(p * LANES, (p + 1) * LANES)


def normalise(x):
    centred = x - jnp.mean(x, axis=-1, keepdims=True)
    inv = lax.rsqrt(jnp.mean(centred * centred, axis=-1, keepdims=True) + norm_eps)
    return centred * inv, inv


def norm_back(grad, normed, inv, gain):
    gn = grad * gain
    m1 = jnp.mean(gn, axis=-1, keepdims=True)
    m2 = jnp.mean(gn * normed, axis=-1, keepdims=True)
    return inv * (gn - m1 - normed * m2)


def head_masks():
    low = (lax.broadcasted_iota(jnp.int32, (1, LANES), 1) < HDIM).astype(F32)
    return low.astype(BF), (1.0 - low).astype(BF)


def two_heads(x, masks):
    return jnp.concatenate([x * masks[0], x * masks[1]], axis=0)


def merge_heads(both):
    return jnp.concatenate([both[:HDIM, :QB], both[HDIM:, QB:]], axis=0)


def weight_copies(slots, inv, buf, sem, matrix, slot):
    return [
        pltpu.make_async_copy(
            slots.at[inv[matrix * PER + j]], buf.at[slot, pl.ds(j * GROUP, GROUP)], sem.at[slot, j]
        )
        for j in range(PER)
    ]


def grad_copies(grads, inv, buf, sem, matrix, slot):
    return [
        pltpu.make_async_copy(
            buf.at[slot, pl.ds(j * GROUP, GROUP)], grads.at[inv[matrix * PER + j]], sem.at[slot, j]
        )
        for j in range(PER)
    ]


def start(copies):
    for copy in copies:
        copy.start()


def wait(copies):
    for copy in copies:
        copy.wait()


def causal_mask(meta, captions, b):
    query = lax.broadcasted_iota(jnp.int32, (1, QB), 1) + b * QB
    first = jnp.zeros((1, QB), jnp.int32)
    for c in range(captions):
        first = jnp.maximum(first, jnp.where(query >= meta[0, c], meta[0, c], 0))
    key = lax.broadcasted_iota(jnp.int32, (2 * QB, QB), 0) + (b - 1) * QB
    allowed = (key >= first) & (key <= query)
    return jnp.concatenate([allowed, allowed], axis=1)


def column_softmax(scores):
    top = jnp.max(scores, axis=0, keepdims=True)
    exponent = jnp.exp(scores - top)
    return exponent, 1.0 / jnp.sum(exponent, axis=0, keepdims=True)


def score_grad(probs, grad):
    return (probs * (grad - jnp.sum(grad * probs, axis=0, keepdims=True))).astype(BF)


def call(body, out_shape, in_specs, out_specs, scratch, aliases=None, effects=False):
    return pl.pallas_call(
        body,
        out_shape=out_shape,
        in_specs=in_specs,
        out_specs=out_specs,
        scratch_shapes=scratch,
        input_output_aliases=aliases or {},
        compiler_params=pltpu.CompilerParams(vmem_limit_bytes=VLIM, has_side_effects=effects),
    )


def image_blocks(meta, i):
    low, high = meta[0, BOUND_LANE + i], meta[0, BOUND_LANE + i + 1]
    first = low // QB
    last = jnp.where(high > low, (high + QB - 1) // QB, first)
    return low, high, first, last


def blk_of(i, size):
    return pl.ds(pl.multiple_of(i * size, 64), size)


def attention_forward(
    captions, images, inv, meta, x, enc_h, norms, slots,
    q_h, k_h, v_h, att_h, r1_h, cq_h, kk_h, vv_h, cross_h, w_h, r2_o,
    wbuf, low, q, kpad, vpad, att, r1, cq, enc, kk, vv, cross, acc, wsem, esem, osem,
):
    rows = x.shape[0]
    patches = enc.shape[0] // images
    loads = [weight_copies(slots, inv, wbuf, wsem, m, m) for m in range(8)]
    for load in loads[:3]:
        start(load)
    enc_copy = pltpu.make_async_copy(enc_h, enc, esem)
    enc_copy.start()
    for m in (C_K, C_V, W_O, C_Q, C_O):
        start(loads[m])
    masks = head_masks()
    copies = []

    def store(i, vmem, hbm):
        copies.append(pltpu.make_async_copy(vmem, hbm, osem.at[i]))
        copies[-1].start()

    def norm_one(i, _):
        normed, _i = normalise(x[blk(i), :].astype(F32))
        low[blk(i), :] = (normed * norms[0:1, :] + norms[4:5, :]).astype(BF)
        return 0

    lax.fori_loop(0, rows // QB, norm_one, 0)
    kpad[pl.ds(0, QB), :] = jnp.zeros((QB, D), BF)
    vpad[pl.ds(0, QB), :] = jnp.zeros((QB, D), BF)
    wait(loads[W_Q])
    q[...] = (nn(low[...], wbuf[W_Q]) * SCALE).astype(BF)
    store(0, q, q_h)
    wait(loads[W_K])
    kpad[pl.ds(QB, rows), :] = nn(low[...], wbuf[W_K]).astype(BF)
    store(1, kpad.at[pl.ds(QB, rows)], k_h)
    wait(loads[W_V])
    vpad[pl.ds(QB, rows), :] = nn(low[...], wbuf[W_V]).astype(BF)
    store(2, vpad.at[pl.ds(QB, rows)], v_h)
    enc_copy.wait()
    wait(loads[C_K])
    wait(loads[C_V])
    store(3, wbuf.at[pl.ds(C_K, 2)], w_h)

    def attend(b, _):
        allowed = causal_mask(meta, captions, b)
        span = pl.ds(pl.multiple_of(b * QB, QB), 2 * QB)
        scores = [
            nt(kpad[span, lanes(p)], two_heads(q[blk(b), lanes(p)], masks)) for p in range(PAIRS)
        ]
        soft = [column_softmax(jnp.where(allowed, score, masked_score)) for score in scores]
        probs = [(exponent * scale).astype(BF) for exponent, scale in soft]
        for p in range(PAIRS):
            out = tn(vpad[span, lanes(p)], probs[p])
            att[blk(b), lanes(p)] = merge_heads(out).T.astype(BF)
        return 0

    lax.fori_loop(0, rows // QB, attend, 0)
    store(4, att, att_h)

    def project(c, _):
        kk[blk(c, D), :] = nn(enc[blk(c, D), :], wbuf[C_K]).astype(BF)
        vv[blk(c, D), :] = nn(enc[blk(c, D), :], wbuf[C_V]).astype(BF)
        return 0

    lax.fori_loop(0, enc.shape[0] // D, project, 0)
    store(5, kk, kk_h)
    store(6, vv, vv_h)
    wait(loads[W_O])
    r1[...] = x[...].astype(F32) + nn(att[...], wbuf[W_O])
    store(7, r1, r1_h)

    def norm_two(i, _):
        normed, _i = normalise(r1[blk(i), :])
        low[blk(i), :] = (normed * norms[1:2, :] + norms[5:6, :]).astype(BF)
        return 0

    lax.fori_loop(0, rows // QB, norm_two, 0)
    wait(loads[C_Q])
    cq[...] = (nn(low[...], wbuf[C_Q]) * SCALE).astype(BF)
    store(8, cq, cq_h)
    acc[...] = jnp.zeros_like(acc)

    def image(i, _):
        first_row, end_row, first, last = image_blocks(meta, i)

        def attend_image(b, _):
            token = lax.broadcasted_iota(jnp.int32, (1, QB), 1) + b * QB
            here = ((token >= first_row) & (token < end_row)).astype(F32)
            here = jnp.concatenate([here, here], axis=1)
            at = blk_of(i, patches)
            scores = [
                nt(kk[at, lanes(p)], two_heads(cq[blk(b), lanes(p)], masks)) for p in range(PAIRS)
            ]
            soft = [column_softmax(score) for score in scores]
            for p in range(PAIRS):
                exponent, scale = soft[p]
                out = tn(vv[at, lanes(p)], exponent.astype(BF)) * (scale * here)
                acc[blk(b), lanes(p)] += merge_heads(out).T
            return 0

        lax.fori_loop(first, last, attend_image, 0)
        return 0

    lax.fori_loop(0, images, image, 0)
    cross[...] = acc[...].astype(BF)
    store(9, cross, cross_h)
    wait(loads[C_O])
    r2_o[...] = r1[...] + nn(cross[...], wbuf[C_O])
    for copy in copies:
        copy.wait()


def run_attention_forward(captions, images, inv, meta, x, enc, norms, slots):
    rows = x.shape[0]
    one = jax.ShapeDtypeStruct((rows, D), BF)
    full = jax.ShapeDtypeStruct((rows, D), F32)
    kv = jax.ShapeDtypeStruct(enc.shape, BF)
    low = pltpu.VMEM((rows, D), BF)
    pad = pltpu.VMEM((rows + QB, D), BF)
    big = pltpu.VMEM((rows, D), F32)
    wide = pltpu.VMEM(enc.shape, BF)
    return call(
        functools.partial(attention_forward, captions, images),
        (one, one, one, one, full, one, kv, kv, one, jax.ShapeDtypeStruct((2, D, D), BF), full),
        [SM, SM, VM, ANY, VM, ANY],
        (ANY,) * 10 + (VM,),
        [
            pltpu.VMEM((8, D, D), BF), low, low, pad, pad, low, big, low, wide, wide, wide, low,
            big, pltpu.SemaphoreType.DMA((8, PER)), pltpu.SemaphoreType.DMA,
            pltpu.SemaphoreType.DMA((10,)),
        ],
    )(inv, meta, x, enc, norms, slots)


GELU_A = 0.7978845608028654
GELU_B = GELU_A * 0.044715


def feed_forward(
    inv, r2, cot, norms, slots, out_o, g2_o, ng_o, grads,
    wup, wdown, third, pre, gh, hid, gpre, acc, gthird, gup, gdown, usem, dsem, gusem, gdsem,
):
    rows = r2.shape[0]
    chunks = FF // D

    def loads(c, slot):
        return weight_copies(slots, inv, wup, usem, UP + c, slot) + weight_copies(
            slots, inv, wdown, dsem, DOWN + c, slot
        )

    def stores(c, slot):
        return grad_copies(grads, inv, gup, gusem, UP + c, slot) + grad_copies(
            grads, inv, gdown, gdsem, DOWN + c, slot
        )

    start(loads(0, 0))

    def norm_three(i, _):
        normed, _i = normalise(r2[blk(i), :])
        third[blk(i), :] = (normed * norms[2:3, :] + norms[6:7, :]).astype(BF)
        return 0

    lax.fori_loop(0, rows // QB, norm_three, 0)
    acc[...] = r2[...]
    gthird[...] = jnp.zeros_like(gthird)

    def chunk(c, _):
        slot = c % 2

        @pl.when(c + 1 < chunks)
        def _():
            start(loads(c + 1, 1 - slot))

        wait(loads(c, slot))
        pre[...] = nt(third[...], wup[slot])
        gh[...] = nt(cot[...], wdown[slot])

        def gelu(i, _):
            x = pre[blk(i, 64), :]
            x2 = x * x
            t = jnp.tanh(x * (GELU_A + GELU_B * x2))
            half = 0.5 + 0.5 * t
            value = x * half
            hid[blk(i, 64), :] = value.astype(BF)
            slope = half + value * (1.0 - t) * (GELU_A + 3.0 * GELU_B * x2)
            gpre[blk(i, 64), :] = (gh[blk(i, 64), :] * slope).astype(BF)
            return 0

        lax.fori_loop(0, rows // 64, gelu, 0)

        @pl.when(c >= 2)
        def _():
            wait(stores(c - 2, slot))

        acc[...] += nn(hid[...], wdown[slot])
        gdown[slot] = tn(hid[...], cot[...]).astype(BF)
        gup[slot] = tn(gpre[...], third[...]).astype(BF)
        start(stores(c, slot))
        gthird[...] += nn(gpre[...], wup[slot])
        return 0

    lax.fori_loop(0, chunks, chunk, 0)
    out_o[...] = acc[...].astype(BF)
    ng_o[...] = jnp.zeros_like(ng_o)

    def back(i, _):
        normed, inv_std = normalise(r2[blk(i), :])
        grad = gthird[blk(i), :]
        ng_o[0:1, :] += jnp.sum(grad * normed, axis=0, keepdims=True)
        ng_o[1:2, :] += jnp.sum(grad, axis=0, keepdims=True)
        g2_o[blk(i), :] = cot[blk(i), :].astype(F32) + norm_back(
            grad, normed, inv_std, norms[2:3, :]
        )
        return 0

    lax.fori_loop(0, rows // QB, back, 0)
    for c in range(chunks - 2, chunks):
        wait(stores(c, c % 2))


def run_feed_forward(inv, r2, cot, norms, slots):
    rows = r2.shape[0]
    big = pltpu.VMEM((rows, D), F32)
    low = pltpu.VMEM((rows, D), BF)
    two = pltpu.VMEM((2, D, D), BF)
    sem = pltpu.SemaphoreType.DMA((2, PER))
    return call(
        feed_forward,
        (
            jax.ShapeDtypeStruct((rows, D), BF),
            jax.ShapeDtypeStruct((rows, D), F32),
            jax.ShapeDtypeStruct((2, D), F32),
            jax.ShapeDtypeStruct(slots.shape, BF),
        ),
        [SM, VM, VM, VM, ANY],
        (VM, VM, VM, ANY),
        [two, two, low, big, big, low, low, big, big, two, two, sem, sem, sem, sem],
    )(inv, r2, cot, norms, slots)


def attention_backward(
    captions, images,
    inv, meta, g2, x_h, q_h, k_h, v_h, att_h, r1_h, cq_h, kk_h, vv_h, cross, enc_h, norms,
    slots, grads_in,
    gt_o, ng_o, dk_h, dv_h, grads,
    wbuf, gbuf, x, q, kpad, vpad, att, r1, cq, kk, vv, enc, gca, dq, acck, accv, dk, dv, big,
    wsem, gsem, isem, osem,
):
    rows = g2.shape[0]
    patches = enc.shape[0] // images
    names = (C_O, C_Q, W_O, W_Q, W_K, W_V)
    loads = [weight_copies(slots, inv, wbuf, wsem, m, i) for i, m in enumerate(names)]
    body = pl.ds(QB, rows)
    inputs = [
        pltpu.make_async_copy(hbm, vmem, isem.at[i])
        for i, (hbm, vmem) in enumerate(
            (
                (cq_h, cq), (kk_h, kk), (vv_h, vv), (enc_h, enc), (r1_h, r1), (att_h, att),
                (q_h, q), (k_h, kpad.at[body]), (v_h, vpad.at[body]), (x_h, x),
            )
        )
    ]
    start(loads[0])
    start(inputs[:4])
    start(loads[1])
    start(inputs[4:])
    for load in loads[2:]:
        start(load)

    def store(matrix, slot):
        copies = grad_copies(grads, inv, gbuf, gsem, matrix, slot)
        start(copies)
        return copies

    masks = head_masks()
    ng_o[...] = jnp.zeros_like(ng_o)
    low = dq
    low[...] = g2[...].astype(BF)
    gbuf[0] = tn(cross[...], low[...]).astype(BF)
    store_co = store(C_O, 0)
    wait(loads[0])
    gca[...] = nt(low[...], wbuf[0]).astype(BF)
    dq[...] = jnp.zeros_like(dq)
    wait(inputs[:3])

    def image(i, _):
        first_row, end_row, first, last = image_blocks(meta, i)
        ik = acck.at[pl.ds(0, patches)]
        iv = accv.at[pl.ds(0, patches)]
        ik[...] = jnp.zeros_like(ik)
        iv[...] = jnp.zeros_like(iv)

        def attend_image(b, _):
            token = lax.broadcasted_iota(jnp.int32, (QB, LANES), 0) + b * QB
            here = ((token >= first_row) & (token < end_row)).astype(F32).astype(BF)
            at = blk_of(i, patches)
            for group in PAIR_GROUPS:
                q2 = [two_heads(cq[blk(b), lanes(p)], masks) for p in group]
                go2 = [two_heads(gca[blk(b), lanes(p)] * here, masks) for p in group]
                scores = [nt(kk[at, lanes(p)], one) for p, one in zip(group, q2)]
                gps = [nt(vv[at, lanes(p)], go) for p, go in zip(group, go2)]
                soft = [column_softmax(score) for score in scores]
                probs = [exponent * scale for exponent, scale in soft]
                for p, prob, go in zip(group, probs, go2):
                    iv[:, lanes(p)] += nn(prob.astype(BF), go)
                gss = [score_grad(prob, gp) for prob, gp in zip(probs, gps)]
                for p, gs, one in zip(group, gss, q2):
                    ik[:, lanes(p)] += nn(gs, one)
                for p, gs in zip(group, gss):
                    gq = merge_heads(tn(kk[at, lanes(p)], gs)).T * SCALE
                    dq[blk(b), lanes(p)] += gq.astype(BF)
            return 0

        lax.fori_loop(first, last, attend_image, 0)
        dk[blk_of(i, patches), :] = ik[...].astype(BF)
        dv[blk_of(i, patches), :] = iv[...].astype(BF)
        return 0

    lax.fori_loop(0, images, image, 0)
    out_k = pltpu.make_async_copy(dk, dk_h, osem.at[0])
    out_v = pltpu.make_async_copy(dv, dv_h, osem.at[1])
    start([out_k, out_v])
    wait(inputs[3:4])
    stores = []
    for slot, matrix, grad in ((1, C_K, dk), (2, C_V, dv)):
        big[...] = jnp.zeros_like(big)

        def gather(c, _, grad=grad):
            big[...] += tn(enc[blk(c, D), :], grad[blk(c, D), :])
            return 0

        lax.fori_loop(0, enc.shape[0] // D, gather, 0)
        gbuf[slot] = big[...].astype(BF)
        stores.append(store(matrix, slot))
    wait(inputs[4:5])

    def norm_two(i, _):
        normed, _i = normalise(r1[blk(i), :])
        gca[blk(i), :] = (normed * norms[1:2, :] + norms[5:6, :]).astype(BF)
        return 0

    lax.fori_loop(0, rows // QB, norm_two, 0)
    gbuf[3] = tn(gca[...], dq[...]).astype(BF)
    stores.append(store(C_Q, 3))
    wait(loads[1])
    big[...] = nt(dq[...], wbuf[1])

    def back_two(i, _):
        normed, inv_std = normalise(r1[blk(i), :])
        grad = big[blk(i), :]
        ng_o[2:3, :] += jnp.sum(grad * normed, axis=0, keepdims=True)
        ng_o[3:4, :] += jnp.sum(grad, axis=0, keepdims=True)
        total = g2[blk(i), :] + norm_back(grad, normed, inv_std, norms[1:2, :])
        r1[blk(i), :] = total
        low[blk(i), :] = total.astype(BF)
        return 0

    lax.fori_loop(0, rows // QB, back_two, 0)
    g1 = r1
    wait(inputs[5:])
    wait(store_co)
    gbuf[0] = tn(att[...], low[...]).astype(BF)
    stores.append(store(W_O, 0))
    wait(loads[2])
    gca[...] = nt(low[...], wbuf[2]).astype(BF)
    kpad[pl.ds(0, QB), :] = jnp.zeros((QB, D), BF)
    vpad[pl.ds(0, QB), :] = jnp.zeros((QB, D), BF)
    acck[...] = jnp.zeros_like(acck)
    accv[...] = jnp.zeros_like(accv)
    wait([out_k, out_v])

    def attend(b, _):
        allowed = causal_mask(meta, captions, b)
        span = pl.ds(pl.multiple_of(b * QB, QB), 2 * QB)
        group = range(PAIRS)
        q2 = [two_heads(q[blk(b), lanes(p)], masks) for p in group]
        go2 = [two_heads(gca[blk(b), lanes(p)], masks) for p in group]
        scores = [nt(kpad[span, lanes(p)], q2[p]) for p in group]
        gps = [nt(vpad[span, lanes(p)], go2[p]) for p in group]
        soft = [column_softmax(jnp.where(allowed, score, masked_score)) for score in scores]
        probs = [exponent * scale for exponent, scale in soft]
        for p in group:
            accv[span, lanes(p)] += nn(probs[p].astype(BF), go2[p])
        gss = [score_grad(prob, gp) for prob, gp in zip(probs, gps)]
        for p in group:
            acck[span, lanes(p)] += nn(gss[p], q2[p])
        for p in group:
            gq = merge_heads(tn(kpad[span, lanes(p)], gss[p])).T * SCALE
            dq[blk(b), lanes(p)] = gq.astype(BF)
        return 0

    lax.fori_loop(0, rows // QB, attend, 0)
    sk, sv = dk.at[pl.ds(0, rows)], dv.at[pl.ds(0, rows)]
    sk[...] = acck[body, :].astype(BF)
    sv[...] = accv[body, :].astype(BF)

    def norm_one(i, _):
        normed, _i = normalise(x[blk(i), :].astype(F32))
        gca[blk(i), :] = (normed * norms[0:1, :] + norms[4:5, :]).astype(BF)
        return 0

    lax.fori_loop(0, rows // QB, norm_one, 0)
    for done in stores[:3]:
        wait(done)
    for slot, matrix, grad in ((1, W_Q, dq), (2, W_K, sk), (3, W_V, sv)):
        gbuf[slot] = tn(gca[...], grad[...]).astype(BF)
        stores.append(store(matrix, slot))
    for load in loads[3:]:
        wait(load)
    big[...] = nt(dq[...], wbuf[3])
    big[...] += nt(sk[...], wbuf[4])
    big[...] += nt(sv[...], wbuf[5])

    def back_one(i, _):
        normed, inv_std = normalise(x[blk(i), :].astype(F32))
        grad = big[blk(i), :]
        ng_o[0:1, :] += jnp.sum(grad * normed, axis=0, keepdims=True)
        ng_o[1:2, :] += jnp.sum(grad, axis=0, keepdims=True)
        gt_o[blk(i), :] = (g1[blk(i), :] + norm_back(grad, normed, inv_std, norms[0:1, :])).astype(
            BF
        )
        return 0

    lax.fori_loop(0, rows // QB, back_one, 0)
    for done in stores[3:]:
        wait(done)


def run_attention_backward(captions, images, inv, meta, g2, x, kept, enc, norms, slots, grads):
    rows = g2.shape[0]
    low = pltpu.VMEM((rows, D), BF)
    pad = pltpu.VMEM((rows + QB, D), BF)
    padf = pltpu.VMEM((rows + QB, D), F32)
    big = pltpu.VMEM((rows, D), F32)
    wide = pltpu.VMEM(enc.shape, BF)
    kv = jax.ShapeDtypeStruct(enc.shape, BF)
    dma = pltpu.SemaphoreType.DMA
    return call(
        functools.partial(attention_backward, captions, images),
        (
            jax.ShapeDtypeStruct((rows, D), BF),
            jax.ShapeDtypeStruct((4, D), F32),
            kv,
            kv,
            jax.ShapeDtypeStruct(slots.shape, BF),
        ),
        [SM, SM, VM] + [ANY] * 9 + [VM, ANY, VM, ANY, ANY],
        (VM, VM, ANY, ANY, ANY),
        [
            pltpu.VMEM((6, D, D), BF), pltpu.VMEM((4, D, D), BF), low, low, pad, pad, low, big, low,
            wide, wide, wide, low, low, padf, padf, wide, wide, big,
            dma((6, PER)), dma((4, PER)), dma((10,)), dma((2,)),
        ],
        aliases={16: 4},
    )(inv, meta, g2, x, *kept, enc, norms, slots, grads)


MESH = pl.DeviceIdType.MESH
PART_ROWS = (256, 128)
PART_OFF = (0, 256)
X_, Y_, UP_, DN_ = 0, 1, 2, 3
OPPOSITE = (X_, Y_, DN_, UP_)
ARRIVALS = (
    (1, 1, 0, 0), (0, 0, 0, 1), (0, 0, 1, 0), (1, 0, 1, 0), (1, 0, 0, 1), (0, 1, 0, 0),
    (1, 1, 1, 0), (1, 1, 0, 1), (0, 0, 2, 0), (1, 0, 1, 1), (0, 0, 1, 1), (1, 0, 2, 0),
    (1, 1, 1, 1), (0, 1, 0, 1), (1, 1, 2, 0), (0, 0, 2, 1), (0, 1, 1, 0), (0, 0, 3, 0),
    (1, 0, 2, 1), (1, 0, 3, 0), (1, 1, 2, 1), (0, 1, 2, 0), (0, 1, 1, 1), (0, 1, 3, 0),
    (0, 0, 3, 1), (1, 1, 3, 0), (1, 0, 3, 1), (0, 1, 2, 1), (1, 1, 3, 1), (0, 1, 3, 1),
)
OWN_SENDS = (
    (1, X_), (0, Y_), (0, UP_), (0, DN_), (1, UP_), (1, DN_), (1, Y_), (0, X_),
)
Z_CHIPS = 4


def signed_arrivals():
    for part, dt, dz, dy in ARRIVALS:
        for step in (-dz, dz) if dz else (0,):
            yield part, dt, step, dy


def routes(part, dt, dz, dy):
    along = [UP_] * (dz <= 0) + [DN_] * (dz >= 0)
    if part == 0:
        return [] if dy else [Y_] if dt else along + [X_, Y_]
    return along if dz or dy else along + [Y_] if dt else [X_, Y_] + along


def source(part, dt, dz, dy):
    last = UP_ if dz > 0 else DN_
    if part == 0:
        return Y_ if dy else X_ if dt else last
    return last if dz else Y_ if dy else X_


class Place:
    def __init__(self):
        self.t = lax.axis_index("tower")
        d = lax.axis_index("dp")
        self.z, self.y, self.c = d // 4, (d // 2) % 2, d % 2

    def device(self, t, z, y, c):
        return (t, z * 4 + y * 2 + c)

    def neighbour(self, kind):
        t, z, y, c = self.t, self.z, self.y, self.c
        return (
            self.device(1 - t, z, y, c),
            self.device(t, z, 1 - y, c),
            self.device(t, jnp.minimum(z + 1, Z_CHIPS - 1), y, c),
            self.device(t, jnp.maximum(z - 1, 0), y, c),
        )[kind]

    def line(self):
        return [
            self.device(self.t, lax.rem(self.z + k, Z_CHIPS), self.y, self.c)
            for k in range(1, Z_CHIPS)
        ]

    def sibling(self):
        return self.device(self.t, self.z, self.y, 1 - self.c)

    def has(self, kind):
        return {UP_: self.z < Z_CHIPS - 1, DN_: self.z > 0}.get(kind)

    def chip(self, dt=0, dz=0, dy=0):
        t = 1 - self.t if dt else self.t
        y = 1 - self.y if dy else self.y
        return t * 8 + (self.z + dz) * 2 + y

    def exists(self, dz):
        return None if dz == 0 else self.z >= -dz if dz < 0 else self.z < Z_CHIPS - dz


def rows_of(chip, core, part):
    return pl.ds(
        pl.multiple_of((chip * 2 + core) * sum(PART_ROWS) + PART_OFF[part], 128), PART_ROWS[part]
    )


def both(first, second):
    return second if first is None else first if second is None else first & second


def when(condition, body):
    if condition is None:
        body()
    else:
        pl.when(condition)(body)


def greet(place, whole_line):
    barrier = pltpu.get_barrier_semaphore()
    targets = [place.neighbour(X_), place.neighbour(Y_), place.sibling()]
    if whole_line:
        targets += place.line()
    for target in targets:
        pl.semaphore_signal(barrier, inc=1, device_id=target, device_id_type=MESH)
    if whole_line:
        pl.semaphore_wait(barrier, len(targets))
        return
    for kind in (UP_, DN_):

        @pl.when(place.has(kind))
        def _(kind=kind):
            pl.semaphore_signal(
                barrier, inc=1, device_id=place.neighbour(kind), device_id_type=MESH
            )

    inner = (place.z > 0) & (place.z < Z_CHIPS - 1)
    pl.semaphore_wait(barrier, jnp.where(inner, len(targets) + 2, len(targets) + 1))


def plan_captions(lengths, picks, start_s, sorted_s, bound_s, images):
    captions = lengths.shape[1]

    def begin(c, run):
        start_s[c] = run
        return run + lengths[0, c]

    lax.fori_loop(0, captions, begin, jnp.int32(0))

    def image(i, run):
        bound_s[i] = run

        def caption(c, run):
            hit = picks[0, c] == i
            sorted_s[c] = jnp.where(hit, run, sorted_s[c])
            return run + jnp.where(hit, lengths[0, c], 0)

        return lax.fori_loop(0, captions, caption, run)

    def clear(c, run):
        sorted_s[c] = 0
        return run

    lax.fori_loop(0, captions, clear, 0)
    bound_s[images] = lax.fori_loop(0, images, image, jnp.int32(0))


def gather_kernel(
    images, lengths, picks, tokens, cot, img, master, norms,
    slots, x_o, meta_o, cot_o, enc_o, place_o,
    own, xs, metas, start_s, sorted_s, bound_s,
    ssem, rsem, sibsem, sibrecv, xsem, lsem,
):
    place = Place()
    rows = tokens.shape[0]
    captions = lengths.shape[1]
    own[...] = master[...].astype(BF)
    greet(place, False)
    sends = []

    def push(condition, part, chip, kind, mine=False):
        target = place.sibling() if kind == 4 else place.neighbour(kind)
        if kind < 4:
            condition = both(condition, place.has(kind))
        rows_p = rows_of(chip, place.c, part)
        src = own.at[pl.ds(PART_OFF[part], PART_ROWS[part])] if mine else slots.at[rows_p]
        sem = sibrecv if kind == 4 else rsem
        out = sibsem.at[part, chip] if kind == 4 else ssem.at[kind, part, chip]
        copy = pltpu.make_async_remote_copy(
            src_ref=src, dst_ref=slots.at[rows_p], send_sem=out, recv_sem=sem.at[part, chip],
            device_id=target, device_id_type=MESH,
        )
        when(condition, copy.start)
        sends.append((condition, copy))

    me = place.chip()
    for part, kind in OWN_SENDS + ((0, 4), (1, 4)):
        push(None, part, me, kind, mine=True)
    keep = pltpu.make_async_copy(
        own, slots.at[pl.ds(pl.multiple_of((me * 2 + place.c) * own.shape[0], 128), own.shape[0])], lsem
    )
    keep.start()

    plan_captions(lengths, picks, start_s, sorted_s, bound_s, images)
    token = lax.broadcasted_iota(jnp.int32, (1, rows), 1)

    def locate(c, where_to):
        inside = (token >= start_s[c]) & (token < start_s[c] + lengths[0, c])
        return jnp.where(inside, token + (sorted_s[c] - start_s[c]), where_to)

    where_to = lax.fori_loop(0, captions, locate, token)
    place_o[...] = jnp.broadcast_to(where_to, place_o.shape)
    lane = lax.broadcasted_iota(jnp.int32, metas.shape, 1)

    def note(c, row):
        return jnp.where(lane == c, sorted_s[c], row)

    row = lax.fori_loop(0, captions, note, jnp.zeros(metas.shape, jnp.int32))
    for i in range(images + 1):
        row = jnp.where(lane == BOUND_LANE + i, bound_s[i], row)
    metas[...] = row

    def sort(out, array):
        def body(b, _):
            target = lax.broadcasted_iota(jnp.int32, (QB, rows), 0) + b * QB
            onehot = (target == place_o[0:1, :]).astype(F32).astype(BF)
            out[blk(b), :] = nn(onehot, array[...]).astype(BF)
            return 0

        lax.fori_loop(0, rows // QB, body, 0)

    sort(xs, tokens)
    swaps = []
    for i, (src, dst) in enumerate(((metas, meta_o), (xs, x_o))):
        swaps.append(
            pltpu.make_async_remote_copy(
                src_ref=src, dst_ref=dst, send_sem=xsem.at[0, i], recv_sem=xsem.at[1, i],
                device_id=place.neighbour(X_), device_id_type=MESH,
            )
        )
        swaps[-1].start()

    def encode(i):
        def body(j, _):
            at = pl.ds(pl.multiple_of(i * IMG_ROWS + j * 64, 64), 64)
            normed, _i = normalise(img[at, :].astype(F32))
            enc_o[at, :] = (normed * norms[3:4, :] + norms[7:8, :]).astype(BF)
            return 0

        lax.fori_loop(0, IMG_ROWS // 64, body, 0)

    steps = img.shape[0] // IMG_ROWS
    done = 0
    for number, (part, dt, dz, dy) in enumerate(signed_arrivals()):
        there = place.exists(dz)
        chip = place.chip(dt, dz, dy)

        def arrived(part=part, chip=chip):
            rows_p = rows_of(chip, place.c, part)
            pltpu.make_async_remote_copy(
                src_ref=slots.at[rows_p], dst_ref=slots.at[rows_p], send_sem=ssem.at[0, part, chip],
                recv_sem=rsem.at[part, chip], device_id=place.neighbour(X_), device_id_type=MESH,
            ).wait_recv()

        when(there, arrived)
        for kind in routes(part, dt, dz, dy) + [4]:
            push(there, part, chip, kind)
        if number == 4:
            sort(cot_o, cot)
        if number >= 6 and done < steps:
            encode(done)
            done += 1
    for i in range(done, steps):
        encode(i)

    def from_sibling(chip, _):
        for part in range(2):
            rows_p = rows_of(chip, 1 - place.c, part)
            pltpu.make_async_remote_copy(
                src_ref=slots.at[rows_p], dst_ref=slots.at[rows_p], send_sem=sibsem.at[part, chip],
                recv_sem=sibrecv.at[part, chip], device_id=place.sibling(), device_id_type=MESH,
            ).wait_recv()
        return 0

    lax.fori_loop(0, 4 * Z_CHIPS, from_sibling, 0)
    for condition, copy in sends:
        when(condition, copy.wait_send)
    for swap in swaps:
        swap.wait()
    keep.wait()


IMG_ROWS = 192
ENC_ROWS = 192


def run_gather(images, lengths, picks, tokens, cot, img, master, norms, total_rows):
    rows = tokens.shape[0]
    dma = pltpu.SemaphoreType.DMA
    low = jax.ShapeDtypeStruct((rows, D), BF)
    return pl.pallas_call(
        functools.partial(gather_kernel, images),
        out_shape=(
            jax.ShapeDtypeStruct((total_rows, D), BF),
            low,
            jax.ShapeDtypeStruct((8, 128), jnp.int32),
            low,
            jax.ShapeDtypeStruct(img.shape, BF),
            jax.ShapeDtypeStruct((8, rows), jnp.int32),
        ),
        in_specs=[SM, SM, VM, VM, VM, VM, VM],
        out_specs=(ANY, ANY, ANY, VM, VM, VM),
        scratch_shapes=[
            pltpu.VMEM(master.shape, BF),
            pltpu.VMEM((rows, D), BF),
            pltpu.VMEM((8, 128), jnp.int32),
            pltpu.SMEM((lengths.shape[1],), jnp.int32),
            pltpu.SMEM((lengths.shape[1],), jnp.int32),
            pltpu.SMEM((images + 1,), jnp.int32),
            dma((4, 2, 16)),
            dma((2, 16)),
            dma((2, 16)),
            dma((2, 16)),
            dma((2, 2)),
            dma,
        ],
        compiler_params=pltpu.CompilerParams(
            vmem_limit_bytes=VLIM, has_side_effects=True, collective_id=0
        ),
    )(lengths, picks, tokens, cot, img, master, norms)


def sum_kernel(
    grads, norm_terms, place_row, gt, out_back, dk_h, dv_h, w_h, img_h, norms,
    red_o, norm_o, gt_o, lay_o, gi_h,
    wkv, ebuf, obuf, ng, esem, osem, wksem, acc, sib, ya, xa, ba, aa, zb_b, zb_a, yb, xb, gtr, nbuf, nrecv,
    lsem, sibsem, sibrecv, ssem, rsem, gsem, nsend, nrs,
):
    place = Place()
    rows = gt.shape[0]
    greet(place, True)
    order = list(signed_arrivals())[::-1] + [(0, 0, 0, 0), (1, 0, 0, 0)]
    sends = []

    def local(part, chip):
        off = pl.ds(PART_OFF[part], PART_ROWS[part])
        return pltpu.make_async_copy(
            grads.at[rows_of(chip, place.c, part)], acc.at[chip, off], lsem.at[part, chip]
        )

    def across(part, chip):
        off = pl.ds(PART_OFF[part], PART_ROWS[part])
        return pltpu.make_async_remote_copy(
            src_ref=grads.at[rows_of(chip, 1 - place.c, part)], dst_ref=sib.at[chip, off],
            send_sem=sibsem.at[part, chip], recv_sem=sibrecv.at[part, chip],
            device_id=place.sibling(), device_id_type=MESH,
        )

    for part, dt, dz, dy in order:
        chip = place.chip(dt, dz, dy)

        def begin(part=part, chip=chip):
            across(part, chip).start()
            local(part, chip).start()

        when(place.exists(dz), begin)
    back = pltpu.make_async_remote_copy(
        src_ref=gt, dst_ref=gtr, send_sem=gsem.at[0], recv_sem=gsem.at[1],
        device_id=place.neighbour(X_), device_id_type=MESH,
    )
    back.start()

    def landing(part, kind, chip):
        t, z = chip // 8, (chip // 2) % Z_CHIPS
        if part == 0:
            ref, index = {X_: (xa, z), Y_: (ya, t * Z_CHIPS + z), UP_: (ba, z), DN_: (aa, z)}[kind]
        else:
            ref, index = {X_: (xb, 0), Y_: (yb, t), UP_: (zb_b, chip), DN_: (zb_a, chip)}[kind]
        return ref.at[index]

    def flow(part, kind, chip):
        off = pl.ds(PART_OFF[part], PART_ROWS[part])
        return pltpu.make_async_remote_copy(
            src_ref=acc.at[chip, off], dst_ref=landing(part, kind, chip),
            send_sem=ssem.at[part, chip], recv_sem=rsem.at[kind, part, chip],
            device_id=place.neighbour(kind), device_id_type=MESH,
        )

    def add(part, chip, other, final):
        def body(i, _):
            at = pl.ds(pl.multiple_of(PART_OFF[part] + i * 64, 64), 64)
            value = acc[chip, at, :].astype(F32)
            for ref in other:
                value = value + ref(part, pl.ds(pl.multiple_of(i * 64, 64), 64), at).astype(F32)
            if final:
                red_o[at, :] = value
            else:
                acc[chip, at, :] = value.astype(BF)
            return 0

        lax.fori_loop(0, PART_ROWS[part] // 64, body, 0)

    def norm_round(i, target):
        return pltpu.make_async_remote_copy(
            src_ref=nbuf.at[i], dst_ref=nrecv.at[i], send_sem=nsend.at[i], recv_sem=nrs.at[i],
            device_id=target, device_id_type=MESH,
        )

    def norm_line(k, target):
        return pltpu.make_async_remote_copy(
            src_ref=nbuf.at[3], dst_ref=nrecv.at[3 + place.z], send_sem=nsend.at[3 + k],
            recv_sem=nrs.at[3 + place.z], device_id=target, device_id_type=MESH,
        )

    def norm_from(z):
        return pltpu.make_async_remote_copy(
            src_ref=nbuf.at[3], dst_ref=nrecv.at[3 + z], send_sem=nsend.at[3], recv_sem=nrs.at[3 + z],
            device_id=place.neighbour(X_), device_id_type=MESH,
        )

    line = [norm_line(k, target) for k, target in enumerate(place.line())]
    rounds = [place.sibling(), place.neighbour(X_), place.neighbour(Y_)]
    keys = pltpu.make_async_copy(w_h, wkv, wksem)
    keys.start()
    steps = dk_h.shape[0] // ENC_ROWS
    ng[...] = jnp.zeros_like(ng)

    def fetch(i):
        at = pl.ds(i * ENC_ROWS, ENC_ROWS)
        return [
            pltpu.make_async_copy(ref.at[at], ebuf.at[j, i % 2], esem.at[j, i % 2])
            for j, ref in enumerate((dk_h, dv_h, img_h))
        ]

    def put(i):
        at = pl.ds(i * ENC_ROWS, ENC_ROWS)
        return [pltpu.make_async_copy(obuf.at[i % 2], gi_h.at[at], osem.at[i % 2])]

    def encoder_back(i):
        wait(fetch(i))
        if i >= 2:
            wait(put(i - 2))
        out = obuf.at[i % 2]
        out[...] = nt(ebuf[0, i % 2], wkv[0]) + nt(ebuf[1, i % 2], wkv[1])

        def body(j, _):
            normed, inv_std = normalise(ebuf[2, i % 2, blk(j, 64), :].astype(F32))
            grad = out[blk(j, 64), :].astype(BF).astype(F32)
            ng[0:1, :] += jnp.sum(grad * normed, axis=0, keepdims=True)
            ng[1:2, :] += jnp.sum(grad, axis=0, keepdims=True)
            out[blk(j, 64), :] = norm_back(grad, normed, inv_std, norms[3:4, :])
            return 0

        lax.fori_loop(0, ENC_ROWS // 64, body, 0)
        start(put(i))
        if i + 2 < steps:
            start(fetch(i + 2))

    start(fetch(0))
    start(fetch(1))

    def unsort(out, array):
        def body(b, _):
            target = lax.broadcasted_iota(jnp.int32, (rows, QB), 0)
            onehot = (target == place_row[0:1, blk(b)]).astype(F32).astype(BF)
            out[blk(b), :] = tn(onehot, array[...]).astype(out.dtype)
            return 0

        lax.fori_loop(0, rows // QB, body, 0)

    for number, (part, dt, dz, dy) in enumerate(order):
        chip = place.chip(dt, dz, dy)
        there = place.exists(dz)
        final = (dt, dz, dy) == (0, 0, 0)
        kinds = routes(part, dt, dz, dy)

        def step(part=part, chip=chip, kinds=kinds, final=final, dt=dt, dz=dz, dy=dy):
            local(part, chip).wait()
            across(part, chip).wait_recv()
            refs = [lambda p, i, at: sib[chip, at, :]]
            fixed = [kind for kind in kinds if kind in (X_, Y_)]
            edge = [kind for kind in kinds if kind in (UP_, DN_)]
            for kind in fixed:
                flow(part, OPPOSITE[kind], chip).wait_recv()
                refs.append(
                    lambda p, i, at, kind=kind: landing(part, OPPOSITE[kind], chip)[i, :]
                )
            for kind in edge:

                def one(kind=kind):
                    flow(part, OPPOSITE[kind], chip).wait_recv()
                    add(part, chip, [lambda p, i, at: landing(part, OPPOSITE[kind], chip)[i, :]], False)

                pl.when(place.has(kind))(one)
            add(part, chip, refs, final)
            if not final:
                flow(part, source(part, dt, dz, dy), chip).start()

        when(there, step)
        if not final:
            sends.append((there, part, chip, source(part, dt, dz, dy)))
        if 2 <= number < 2 + 2 * steps and number % 2 == 0:
            if number == 2:
                keys.wait()
            encoder_back(number // 2 - 1)
        if number == 27:
            nbuf[0] = norm_terms[...]
            nbuf[0, 3:4, :] = ng[0:1, :]
            nbuf[0, 7:8, :] = ng[1:2, :]
            norm_round(0, rounds[0]).start()
        if number in (31, 35, 39):
            i = (31, 35, 39).index(number)
            norm_round(i, rounds[i]).wait()
            nbuf[i + 1] = nbuf[i] + nrecv[i]
            if i < 2:
                norm_round(i + 1, rounds[i + 1]).start()
            else:
                for copy in line:
                    copy.start()
        if number == 28:
            unsort(lay_o, out_back)
        if number == 40:
            back.wait()
            unsort(gt_o, gtr)

    for z in range(Z_CHIPS):

        @pl.when(place.z != z)
        def _(z=z):
            norm_from(z).wait_recv()

        @pl.when(place.z == z)
        def _(z=z):
            nrecv[3 + z] = nbuf[3]

    wait(put(steps - 2) + put(steps - 1))
    norm_o[...] = (nrecv[3] + nrecv[4]) + (nrecv[5] + nrecv[6])
    for copy in line:
        copy.wait_send()
    for there, part, chip, kind in sends:
        when(there, flow(part, kind, chip).wait_send)

    def sent(chip, _):
        for part in range(2):
            across(part, chip).wait_send()
        return 0

    lax.fori_loop(0, 4 * Z_CHIPS, sent, 0)


def run_sum(grads, norm_terms, place_row, gt, out_back, dk, dv, kv_weights, img, norms):
    rows = gt.shape[0]
    dma = pltpu.SemaphoreType.DMA
    a, b = PART_ROWS
    shard = a + b
    line = 4 * Z_CHIPS
    return pl.pallas_call(
        sum_kernel,
        out_shape=(
            jax.ShapeDtypeStruct((shard, D), F32),
            jax.ShapeDtypeStruct((8, D), F32),
            jax.ShapeDtypeStruct((rows, D), F32),
            jax.ShapeDtypeStruct((rows, D), BF),
            jax.ShapeDtypeStruct(img.shape, F32),
        ),
        in_specs=[ANY, VM, VM, ANY, VM, ANY, ANY, ANY, ANY, VM],
        out_specs=(VM,) * 4 + (ANY,),
        scratch_shapes=[
            pltpu.VMEM((2, D, D), BF),
            pltpu.VMEM((3, 2, ENC_ROWS, D), BF),
            pltpu.VMEM((2, ENC_ROWS, D), F32),
            pltpu.VMEM((8, D), F32),
            dma((3, 2)),
            dma((2,)),
            dma,
            pltpu.VMEM((line, shard, D), BF),
            pltpu.VMEM((line, shard, D), BF),
            pltpu.VMEM((2 * Z_CHIPS, a, D), BF),
            pltpu.VMEM((Z_CHIPS, a, D), BF),
            pltpu.VMEM((Z_CHIPS, a, D), BF),
            pltpu.VMEM((Z_CHIPS, a, D), BF),
            pltpu.VMEM((line, b, D), BF),
            pltpu.VMEM((line, b, D), BF),
            pltpu.VMEM((2, b, D), BF),
            pltpu.VMEM((1, b, D), BF),
            pltpu.VMEM((rows, D), BF),
            pltpu.VMEM((4, 8, D), F32),
            pltpu.VMEM((7, 8, D), F32),
            dma((2, line)),
            dma((2, line)),
            dma((2, line)),
            dma((2, line)),
            dma((4, 2, line)),
            dma((2,)),
            dma((7,)),
            dma((7,)),
        ],
        compiler_params=pltpu.CompilerParams(
            vmem_limit_bytes=VLIM, has_side_effects=True, collective_id=1
        ),
    )(grads, norm_terms, place_row, gt, out_back, dk, dv, kv_weights, img, norms)


def from_partner(block, axis):
    half = lax.axis_size(axis) // 2
    count = lax.axis_size(axis)
    return lax.ppermute(block, axis, [(i, (i + half) % count) for i in range(count)])


def adamw_update(weight, moment, second, grad_in, rate, decay_rate):
    new_moment = beta_one * moment + (1.0 - beta_one) * grad_in
    new_second = beta_two * second + (1.0 - beta_two) * grad_in * grad_in
    moment_hat = new_moment / (1.0 - beta_one**STEP)
    second_hat = new_second / (1.0 - beta_two**STEP)
    new_weight = weight - rate * (
        moment_hat / (jnp.sqrt(second_hat) + epsilon) + decay_rate * weight
    )
    return (new_weight, new_moment, new_second)


def caption_plan(lengths, picks, rows, images):
    ends = jnp.cumsum(lengths)
    starts = ends - lengths
    rank = picks * lengths.shape[0] + jnp.arange(lengths.shape[0], dtype=jnp.int32)
    ahead = rank[None, :] < rank[:, None]
    sorted_starts = jnp.sum(jnp.where(ahead, lengths[None, :], 0), axis=1)
    token = jnp.arange(rows, dtype=jnp.int32)
    inside = (token[:, None] >= starts[None, :]) & (token[:, None] < ends[None, :])
    place = token + jnp.sum(jnp.where(inside, (sorted_starts - starts)[None, :], 0), axis=1)
    edges = jnp.arange(images + 1, dtype=jnp.int32)
    bounds = jnp.sum(jnp.where(picks[None, :] < edges[:, None], lengths[None, :], 0), axis=1)
    return place, sorted_starts, bounds


def per_device(
    kernels,
    tokens,
    cotangent,
    caption_lengths,
    image_index,
    image_states,
    master_weights,
    first_moments,
    second_moments,
    owner_list,
    norm_params,
    norm_first,
    norm_second,
):
    rows = tokens.shape[0]
    groups = owner_list.shape[0]
    total_rows = 8 * D + 2 * FF
    group_rows = total_rows // groups
    images = image_states.shape[0]
    captions = caption_lengths.shape[1]
    axes = ("tower", "dp")
    direct = group_rows == GROUP
    ids = jnp.arange(groups, dtype=jnp.int32)
    inverse = jnp.sum(jnp.where(owner_list[None, :] == ids[:, None], ids[None, :], 0), axis=1)
    img = image_states.reshape(-1, D)
    if kernels:
        gathered, x, meta, sent_cot, enc, place_row = run_gather(
            images, caption_lengths, image_index, tokens, cotangent, img, master_weights,
            norm_params, total_rows,
        )
    else:
        gathered = lax.all_gather(master_weights.astype(BF), axes, axis=0, tiled=True)
        place, starts, bounds = caption_plan(caption_lengths[0], image_index[0], rows, images)
        into = (place[None, :] == jnp.arange(rows, dtype=jnp.int32)[:, None]).astype(BF)
        meta = jnp.zeros((8, 128), jnp.int32)
        meta = meta.at[0, :captions].set(starts)
        meta = meta.at[0, BOUND_LANE : BOUND_LANE + images + 1].set(bounds)
        meta = from_partner(meta, "tower")
        x = from_partner(nn(into, tokens).astype(BF), "tower")
        sent_cot = nn(into, cotangent).astype(BF)
        normed, _i = normalise(img.astype(F32))
        enc = (normed * norm_params[3] + norm_params[7]).astype(BF)
    if direct:
        slots = gathered.reshape(groups, GROUP, D)
        inv = inverse
    else:
        slots = gathered.reshape(groups, group_rows, D)[inverse].reshape(-1, GROUP, D)
        inv = jnp.arange(total_rows // GROUP, dtype=jnp.int32)
    cot = from_partner(sent_cot, "tower")
    *kept, kv_weights, r2 = run_attention_forward(
        captions, images, inv, meta, x, enc, norm_params, slots
    )
    out, g2, ng3, grads = run_feed_forward(inv, r2, cot, norm_params, slots)
    out_back = from_partner(out, "tower")
    gt, ng, dk, dv, grads = run_attention_backward(
        captions, images, inv, meta, g2, x, kept, enc, norm_params, slots, grads
    )
    none = jnp.zeros((1, D), F32)
    norm_terms = jnp.concatenate(
        [ng[0:1], ng[2:3], ng3[0:1], none, ng[1:2], ng[3:4], ng3[1:2], none]
    )
    if kernels:
        reduced, norm_grads, grad_tokens, layer_out, grad_images = run_sum(
            grads.reshape(total_rows, D), norm_terms, place_row, gt, out_back, dk, dv, kv_weights,
            img, norm_params,
        )
    else:
        layer_out = tn(into, out_back).astype(BF)
        grad_tokens = tn(into, from_partner(gt, "tower"))
        grad_enc = (nt(dk, kv_weights[0]) + nt(dv, kv_weights[1])).astype(BF).astype(F32)
        normed, inv_std = normalise(img.astype(F32))
        grad_images = norm_back(grad_enc, normed, inv_std, norm_params[3:4])
        norm_terms = norm_terms.at[3].set(jnp.sum(grad_enc * normed, axis=0))
        norm_terms = norm_terms.at[7].set(jnp.sum(grad_enc, axis=0))
        if direct:
            arranged = grads.reshape(total_rows, D)
        else:
            arranged = grads.reshape(groups, group_rows, D)[owner_list].reshape(total_rows, D)
        reduced = lax.psum_scatter(arranged, axes, scatter_dimension=0, tiled=True).astype(F32)
        norm_grads = lax.psum(norm_terms, axes)
    new_weights, new_first, new_second = adamw_update(
        master_weights, first_moments, second_moments, reduced, learn_rate, weight_decay
    )
    norm_new, norm_first_new, norm_second_new = adamw_update(
        norm_params, norm_first, norm_second, norm_grads, norm_rate, 0.0
    )
    return (
        layer_out,
        grad_tokens,
        grad_images.reshape(image_states.shape),
        new_weights,
        new_first,
        new_second,
        new_weights.astype(BF),
        norm_new,
        norm_first_new,
        norm_second_new,
    )


def solution(mesh):
    split = P(("tower", "dp"), None)
    wide = P(("tower", "dp"), None, None)
    in_specs = (split,) * 4 + (wide,) + (split,) * 3 + (P(),) * 4
    out_specs = (split, split, wide) + (split,) * 4 + (P(),) * 3
    shape = dict(mesh.shape)
    kernels = shape["tower"] == 2 and shape["dp"] == 4 * Z_CHIPS
    return jax.shard_map(
        functools.partial(per_device, kernels),
        mesh=mesh,
        in_specs=in_specs,
        out_specs=out_specs,
        check_vma=False,
    )
```

```python
import functools

import jax
import jax.numpy as jnp
from jax import lax
from jax.experimental import pallas as pl
from jax.experimental.pallas import tpu as pltpu
from jax.sharding import PartitionSpec as P

D = 768
HEADS = 12
HDIM = 64
FF = 3072
STEP = 5
PAIRS = HEADS // 2
LANES = 2 * HDIM
QB = 128
HEAD_ROWS = 16
PAIR_GROUPS = ((0, 1, 2), (3, 4, 5))
GROUP = 192
BOUND_LANE = 64
PER = D // GROUP
SCALE = HDIM ** (-0.5)

beta_one = 0.5
beta_two = 0.6
learn_rate = 0.03
norm_rate = 0.4
weight_decay = 0.01
epsilon = 1e-08
norm_eps = 1e-05
masked_score = -1000000000.0

W_Q, W_K, W_V, W_O, C_Q, C_K, C_V, C_O, UP, DOWN = 0, 1, 2, 3, 4, 5, 6, 7, 8, 12

BF = jnp.bfloat16
F32 = jnp.float32
VM = pl.BlockSpec(memory_space=pltpu.VMEM)
SM = pl.BlockSpec(memory_space=pltpu.SMEM)
ANY = pl.BlockSpec(memory_space=pl.ANY)
VLIM = 58 * 2**20


def nn(a, b):
    return lax.dot_general(a, b, (((1,), (0,)), ((), ())), preferred_element_type=F32)


def nt(a, b):
    return lax.dot_general(a, b, (((1,), (1,)), ((), ())), preferred_element_type=F32)


def tn(a, b):
    return lax.dot_general(a, b, (((0,), (0,)), ((), ())), preferred_element_type=F32)


def blk(i, size=QB):
    return pl.ds(pl.multiple_of(i * size, size), size)


def lanes(p):
    return slice(p * LANES, (p + 1) * LANES)


def normalise(x):
    centred = x - jnp.mean(x, axis=-1, keepdims=True)
    inv = lax.rsqrt(jnp.mean(centred * centred, axis=-1, keepdims=True) + norm_eps)
    return centred * inv, inv


def norm_back(grad, normed, inv, gain):
    gn = grad * gain
    m1 = jnp.mean(gn, axis=-1, keepdims=True)
    m2 = jnp.mean(gn * normed, axis=-1, keepdims=True)
    return inv * (gn - m1 - normed * m2)


def head_masks():
    low = (lax.broadcasted_iota(jnp.int32, (1, LANES), 1) < HDIM).astype(F32)
    return low.astype(BF), (1.0 - low).astype(BF)


def two_heads(x, masks):
    return jnp.concatenate([x * masks[0], x * masks[1]], axis=0)


def merge_heads(both):
    return jnp.concatenate([both[:HDIM, :QB], both[HDIM:, QB:]], axis=0)


def weight_copies(slots, inv, buf, sem, matrix, slot):
    return [
        pltpu.make_async_copy(
            slots.at[inv[matrix * PER + j]], buf.at[slot, pl.ds(j * GROUP, GROUP)], sem.at[slot, j]
        )
        for j in range(PER)
    ]


def grad_copies(grads, inv, buf, sem, matrix, slot):
    return [
        pltpu.make_async_copy(
            buf.at[slot, pl.ds(j * GROUP, GROUP)], grads.at[inv[matrix * PER + j]], sem.at[slot, j]
        )
        for j in range(PER)
    ]


def start(copies):
    for copy in copies:
        copy.start()


def wait(copies):
    for copy in copies:
        copy.wait()


def causal_mask(meta, captions, b):
    query = lax.broadcasted_iota(jnp.int32, (1, QB), 1) + b * QB
    first = jnp.zeros((1, QB), jnp.int32)
    for c in range(captions):
        first = jnp.maximum(first, jnp.where(query >= meta[0, c], meta[0, c], 0))
    key = lax.broadcasted_iota(jnp.int32, (2 * QB, QB), 0) + (b - 1) * QB
    allowed = (key >= first) & (key <= query)
    return jnp.concatenate([allowed, allowed], axis=1)


def column_softmax(scores):
    top = jnp.max(scores, axis=0, keepdims=True)
    exponent = jnp.exp(scores - top)
    total = jnp.sum(exponent, axis=0, keepdims=True)
    return exponent, 1.0 / total, top + jnp.log(total)


def head_products(grad, out):
    prod = grad.astype(F32) * out
    high = prod.astype(BF)
    low = (prod - high.astype(F32)).astype(BF)
    head = lax.broadcasted_iota(jnp.int32, (HEAD_ROWS, D), 0)
    lane = lax.broadcasted_iota(jnp.int32, (HEAD_ROWS, D), 1)
    pick = ((lane >= head * HDIM) & (lane < (head + 1) * HDIM)).astype(F32).astype(BF)
    return nt(pick, high) + nt(pick, low)


def pair_row(table, p):
    return jnp.concatenate([table[2 * p : 2 * p + 1], table[2 * p + 1 : 2 * p + 2]], axis=1)


def call(body, out_shape, in_specs, out_specs, scratch, aliases=None, effects=False):
    return pl.pallas_call(
        body,
        out_shape=out_shape,
        in_specs=in_specs,
        out_specs=out_specs,
        scratch_shapes=scratch,
        input_output_aliases=aliases or {},
        compiler_params=pltpu.CompilerParams(vmem_limit_bytes=VLIM, has_side_effects=effects),
    )


def image_blocks(meta, i):
    low, high = meta[0, BOUND_LANE + i], meta[0, BOUND_LANE + i + 1]
    first = low // QB
    last = jnp.where(high > low, (high + QB - 1) // QB, first)
    return low, high, first, last


def blk_of(i, size):
    return pl.ds(pl.multiple_of(i * size, 64), size)


def attention_forward(
    captions, images, inv, meta, x, enc_h, norms, slots,
    q_h, k_h, v_h, att_h, r1_h, cq_h, kk_h, vv_h, cross_h, atf_h, crf_h, fst_h, snd_h, slse_o, clse_o, w_h, r2_o,
    wbuf, low, second, q, kpad, vpad, att, atf, r1, cq, enc, kk, vv, cross, acc, wsem, esem, osem,
):
    rows = x.shape[0]
    patches = enc.shape[0] // images
    loads = [weight_copies(slots, inv, wbuf, wsem, m, m) for m in range(8)]
    for load in loads[:3]:
        start(load)
    enc_copy = pltpu.make_async_copy(enc_h, enc, esem)
    enc_copy.start()
    for m in (C_K, C_V, W_O, C_Q, C_O):
        start(loads[m])
    masks = head_masks()
    copies = []

    def store(i, vmem, hbm):
        copies.append(pltpu.make_async_copy(vmem, hbm, osem.at[i]))
        copies[-1].start()

    def norm_one(i, _):
        normed, _i = normalise(x[blk(i), :].astype(F32))
        low[blk(i), :] = (normed * norms[0:1, :] + norms[4:5, :]).astype(BF)
        return 0

    lax.fori_loop(0, rows // QB, norm_one, 0, unroll=True)
    store(12, low, fst_h)
    kpad[pl.ds(0, QB), :] = jnp.zeros((QB, D), BF)
    vpad[pl.ds(0, QB), :] = jnp.zeros((QB, D), BF)
    wait(loads[W_Q])
    q[...] = (nn(low[...], wbuf[W_Q]) * SCALE).astype(BF)
    store(0, q, q_h)
    wait(loads[W_K])
    kpad[pl.ds(QB, rows), :] = nn(low[...], wbuf[W_K]).astype(BF)
    store(1, kpad.at[pl.ds(QB, rows)], k_h)
    wait(loads[W_V])
    vpad[pl.ds(QB, rows), :] = nn(low[...], wbuf[W_V]).astype(BF)
    store(2, vpad.at[pl.ds(QB, rows)], v_h)
    enc_copy.wait()
    wait(loads[C_K])
    wait(loads[C_V])
    store(3, wbuf.at[pl.ds(C_K, 2)], w_h)

    def attend(b, _):
        allowed = causal_mask(meta, captions, b)
        span = pl.ds(pl.multiple_of(b * QB, QB), 2 * QB)
        scores = [
            nt(kpad[span, lanes(p)], two_heads(q[blk(b), lanes(p)], masks)) for p in range(PAIRS)
        ]
        soft = [column_softmax(jnp.where(allowed, score, masked_score)) for score in scores]
        for p in range(PAIRS):
            exponent, scale, lse = soft[p]
            out = merge_heads(tn(vpad[span, lanes(p)], exponent.astype(BF)) * scale).T
            atf[blk(b), lanes(p)] = out
            att[blk(b), lanes(p)] = out.astype(BF)
            slse_o[b, p : p + 1, :] = lse
        return 0

    lax.fori_loop(0, rows // QB, attend, 0)
    store(4, att, att_h)
    store(10, atf, atf_h)

    def project(c, _):
        kk[blk(c, D), :] = nn(enc[blk(c, D), :], wbuf[C_K]).astype(BF)
        vv[blk(c, D), :] = nn(enc[blk(c, D), :], wbuf[C_V]).astype(BF)
        return 0

    lax.fori_loop(0, enc.shape[0] // D, project, 0)
    store(5, kk, kk_h)
    store(6, vv, vv_h)
    wait(loads[W_O])
    r1[...] = x[...].astype(F32) + nn(att[...], wbuf[W_O])
    store(7, r1, r1_h)

    def norm_two(i, _):
        normed, _i = normalise(r1[blk(i), :])
        second[blk(i), :] = (normed * norms[1:2, :] + norms[5:6, :]).astype(BF)
        return 0

    lax.fori_loop(0, rows // QB, norm_two, 0, unroll=True)
    store(13, second, snd_h)
    wait(loads[C_Q])
    cq[...] = (nn(second[...], wbuf[C_Q]) * SCALE).astype(BF)
    store(8, cq, cq_h)
    acc[...] = jnp.zeros_like(acc)
    clse_o[...] = jnp.zeros_like(clse_o)

    def image(i, _):
        first_row, end_row, first, last = image_blocks(meta, i)

        def attend_image(b, _):
            token = lax.broadcasted_iota(jnp.int32, (1, QB), 1) + b * QB
            here = ((token >= first_row) & (token < end_row)).astype(F32)
            here = jnp.concatenate([here, here], axis=1)
            at = blk_of(i, patches)
            scores = [
                nt(kk[at, lanes(p)], two_heads(cq[blk(b), lanes(p)], masks)) for p in range(PAIRS)
            ]
            soft = [column_softmax(score) for score in scores]
            for p in range(PAIRS):
                exponent, scale, lse = soft[p]
                clse_o[b, p : p + 1, :] = jnp.where(here > 0, lse, clse_o[b, p : p + 1, :])
                out = tn(vv[at, lanes(p)], exponent.astype(BF)) * (scale * here)
                acc[blk(b), lanes(p)] += merge_heads(out).T
            return 0

        lax.fori_loop(first, last, attend_image, 0)
        return 0

    lax.fori_loop(0, images, image, 0)
    cross[...] = acc[...].astype(BF)
    store(9, cross, cross_h)
    store(11, acc, crf_h)
    wait(loads[C_O])
    r2_o[...] = r1[...] + nn(cross[...], wbuf[C_O])
    for copy in copies:
        copy.wait()


def run_attention_forward(captions, images, inv, meta, x, enc, norms, slots):
    rows = x.shape[0]
    one = jax.ShapeDtypeStruct((rows, D), BF)
    full = jax.ShapeDtypeStruct((rows, D), F32)
    kv = jax.ShapeDtypeStruct(enc.shape, BF)
    lse = jax.ShapeDtypeStruct((rows // QB, 8, 2 * QB), F32)
    low = pltpu.VMEM((rows, D), BF)
    pad = pltpu.VMEM((rows + QB, D), BF)
    big = pltpu.VMEM((rows, D), F32)
    wide = pltpu.VMEM(enc.shape, BF)
    return call(
        functools.partial(attention_forward, captions, images),
        (one, one, one, one, full, one, kv, kv, one, full, full, one, one, lse, lse)
        + (jax.ShapeDtypeStruct((2, D, D), BF), full),
        [SM, SM, VM, ANY, VM, ANY],
        (ANY,) * 13 + (VM, VM, ANY, VM),
        [
            pltpu.VMEM((8, D, D), BF), low, low, low, pad, pad, low, big, big, low, wide, wide, wide,
            low, big, pltpu.SemaphoreType.DMA((8, PER)), pltpu.SemaphoreType.DMA,
            pltpu.SemaphoreType.DMA((14,)),
        ],
    )(inv, meta, x, enc, norms, slots)


GELU_A = 0.7978845608028654
GELU_B = GELU_A * 0.044715


GELU_ROWS = 32
HID_COLS = 256


def feed_forward(
    inv, r2, cot, norms, slots, out_o, g2_o, ng_o, grads,
    wup, wdown, third, pre, gh, hid, gpre, acc, gthird, gup, gdown, usem, dsem, gusem, gdsem,
):
    rows = r2.shape[0]
    chunks = FF // D

    def loads(c):
        slot = c % 3
        return weight_copies(slots, inv, wup, usem, UP + c, slot) + weight_copies(
            slots, inv, wdown, dsem, DOWN + c, slot
        )

    def stores(c):
        return grad_copies(grads, inv, gup, gusem, UP + c, c % 2) + grad_copies(
            grads, inv, gdown, gdsem, DOWN + c, c % 2
        )

    def gelu(c, i):
        at = pl.ds(i * GELU_ROWS, GELU_ROWS)
        x = pre[c % 2, at, :]
        x2 = x * x
        t = jnp.tanh(x * (GELU_A + GELU_B * x2))
        half = 0.5 + 0.5 * t
        value = x * half
        hid[at, :] = value.astype(BF)
        slope = half + value * (1.0 - t) * (GELU_A + 3.0 * GELU_B * x2)
        gpre[at, :] = (gh[c % 2, at, :] * slope).astype(BF)

    def into_hidden(c, j):
        cols = pl.ds(j * HID_COLS, HID_COLS)
        pre[c % 2, :, cols] = nt(third[...], wup[c % 3, cols, :])
        gh[c % 2, :, cols] = nt(cot[...], wdown[c % 3, cols, :])

    start(loads(0))
    start(loads(1))

    def norm_three(i, _):
        normed, _i = normalise(r2[blk(i), :])
        third[blk(i), :] = (normed * norms[2:3, :] + norms[6:7, :]).astype(BF)
        return 0

    lax.fori_loop(0, rows // QB, norm_three, 0, unroll=True)
    wait(loads(0))
    for j in range(D // HID_COLS):
        into_hidden(0, j)
    parts = D // HID_COLS
    share = rows // GELU_ROWS // parts
    for c in range(chunks):
        if c + 2 < chunks:
            start(loads(c + 2))
        if c + 1 < chunks:
            wait(loads(c + 1))
        for j in range(parts):
            if c + 1 < chunks:
                into_hidden(c + 1, j)
            for i in range(j * share, (j + 1) * share):
                gelu(c, i)
        if c >= 2:
            wait(stores(c - 2))
        if c == 0:
            acc[...] = r2[...] + nn(hid[...], wdown[c % 3])
            gthird[...] = nn(gpre[...], wup[c % 3])
        else:
            acc[...] += nn(hid[...], wdown[c % 3])
            gthird[...] += nn(gpre[...], wup[c % 3])
        gdown[c % 2] = tn(hid[...], cot[...]).astype(BF)
        gup[c % 2] = tn(gpre[...], third[...]).astype(BF)
        start(stores(c))
    out_o[...] = acc[...].astype(BF)
    ng_o[...] = jnp.zeros_like(ng_o)

    def back(i, _):
        normed, inv_std = normalise(r2[blk(i), :])
        grad = gthird[blk(i), :]
        ng_o[0:1, :] += jnp.sum(grad * normed, axis=0, keepdims=True)
        ng_o[1:2, :] += jnp.sum(grad, axis=0, keepdims=True)
        g2_o[blk(i), :] = cot[blk(i), :].astype(F32) + norm_back(
            grad, normed, inv_std, norms[2:3, :]
        )
        return 0

    lax.fori_loop(0, rows // QB, back, 0, unroll=True)
    for c in range(chunks - 2, chunks):
        wait(stores(c))


def run_feed_forward(inv, r2, cot, norms, slots):
    rows = r2.shape[0]
    big = pltpu.VMEM((rows, D), F32)
    bigs = pltpu.VMEM((2, rows, D), F32)
    low = pltpu.VMEM((rows, D), BF)
    two = pltpu.VMEM((2, D, D), BF)
    three = pltpu.VMEM((3, D, D), BF)
    sem = pltpu.SemaphoreType.DMA((2, PER))
    sem3 = pltpu.SemaphoreType.DMA((3, PER))
    return call(
        feed_forward,
        (
            jax.ShapeDtypeStruct((rows, D), BF),
            jax.ShapeDtypeStruct((rows, D), F32),
            jax.ShapeDtypeStruct((2, D), F32),
            jax.ShapeDtypeStruct(slots.shape, BF),
        ),
        [SM, VM, VM, VM, ANY],
        (VM, VM, VM, ANY),
        [three, three, low, bigs, bigs, low, low, big, big, two, two, sem3, sem3, sem, sem],
    )(inv, r2, cot, norms, slots)


def attention_backward(
    captions, images,
    inv, meta, g2, x_h, q_h, k_h, v_h, att_h, r1_h, cq_h, kk_h, vv_h, cross, atf_h, crf_h, fst_h, snd_h,
    slse, clse, enc_h, norms, slots, grads_in,
    gt_o, ng_o, dk_h, dv_h, grads,
    wbuf, gbuf, x, q, kpad, vpad, att, r1, cq, kk, vv, enc, gca, dq, acck, accv, big, out32,
    low_n, delta, wsem, gsem, isem, osem,
):
    rows = g2.shape[0]
    patches = enc.shape[0] // images
    names = (C_O, C_Q, W_O, W_Q, W_K, W_V)
    loads = [weight_copies(slots, inv, wbuf, wsem, m, i) for i, m in enumerate(names)]
    body = pl.ds(QB, rows)
    inputs = [
        pltpu.make_async_copy(hbm, vmem, isem.at[i])
        for i, (hbm, vmem) in enumerate(
            (
                (crf_h, out32), (cq_h, cq), (kk_h, kk), (vv_h, vv), (enc_h, enc), (r1_h, r1),
                (snd_h, low_n), (att_h, att), (q_h, q), (k_h, kpad.at[body]),
                (v_h, vpad.at[body]), (x_h, x), (atf_h, out32), (fst_h, low_n),
            )
        )
    ]
    start(loads[0])
    start(inputs[:5])
    start(loads[1])
    start(inputs[5:12])
    for load in loads[2:]:
        start(load)

    def store(matrix, slot):
        copies = grad_copies(grads, inv, gbuf, gsem, matrix, slot)
        start(copies)
        return copies

    masks = head_masks()
    ng_o[...] = jnp.zeros_like(ng_o)
    low = dq
    low[...] = g2[...].astype(BF)
    gbuf[0] = tn(cross[...], low[...]).astype(BF)
    store_co = store(C_O, 0)
    wait(loads[0])
    gca[...] = nt(low[...], wbuf[0]).astype(BF)
    dq[...] = jnp.zeros_like(dq)
    wait(inputs[:4])

    def deltas(b, _):
        delta[b] = head_products(gca[blk(b), :], out32[blk(b), :])
        return 0

    lax.fori_loop(0, rows // QB, deltas, 0)
    start(inputs[12:13])

    def image(i, _):
        first_row, end_row, first, last = image_blocks(meta, i)
        ik = acck.at[pl.ds(0, patches)]
        iv = accv.at[pl.ds(0, patches)]
        ik[...] = jnp.zeros_like(ik)
        iv[...] = jnp.zeros_like(iv)

        def attend_image(b, _):
            token = lax.broadcasted_iota(jnp.int32, (QB, LANES), 0) + b * QB
            here = ((token >= first_row) & (token < end_row)).astype(F32).astype(BF)
            column = lax.broadcasted_iota(jnp.int32, (1, QB), 1) + b * QB
            inside = (column >= first_row) & (column < end_row)
            inside = jnp.concatenate([inside, inside], axis=1)
            at = blk_of(i, patches)
            table = delta[b]
            for group in PAIR_GROUPS:
                q2 = [two_heads(cq[blk(b), lanes(p)], masks) for p in group]
                go2 = [two_heads(gca[blk(b), lanes(p)] * here, masks) for p in group]
                scores = [nt(kk[at, lanes(p)], one) for p, one in zip(group, q2)]
                gps = [nt(vv[at, lanes(p)], go) for p, go in zip(group, go2)]
                probs = [
                    jnp.exp(score - jnp.where(inside, clse[b, p : p + 1, :], -masked_score))
                    for p, score in zip(group, scores)
                ]
                for p, prob, go in zip(group, probs, go2):
                    iv[:, lanes(p)] += nn(prob.astype(BF), go)
                gss = [
                    (prob * (gp - pair_row(table, p))).astype(BF)
                    for p, prob, gp in zip(group, probs, gps)
                ]
                for p, gs, one in zip(group, gss, q2):
                    ik[:, lanes(p)] += nn(gs, one)
                for p, gs in zip(group, gss):
                    gq = merge_heads(tn(kk[at, lanes(p)], gs)).T * SCALE
                    dq[blk(b), lanes(p)] += gq.astype(BF)
            return 0

        lax.fori_loop(first, last, attend_image, 0)
        kk[blk_of(i, patches), :] = ik[...].astype(BF)
        vv[blk_of(i, patches), :] = iv[...].astype(BF)
        return 0

    lax.fori_loop(0, images, image, 0)
    dk, dv = kk, vv
    out_k = pltpu.make_async_copy(dk, dk_h, osem.at[0])
    out_v = pltpu.make_async_copy(dv, dv_h, osem.at[1])
    start([out_k, out_v])
    wait(inputs[4:5])
    stores = []
    for slot, matrix, grad in ((1, C_K, dk), (2, C_V, dv)):
        gbuf[slot] = tn(enc[...], grad[...]).astype(BF)
        stores.append(store(matrix, slot))
    wait(inputs[5:7])
    gbuf[3] = tn(low_n[...], dq[...]).astype(BF)
    start(inputs[13:])
    stores.append(store(C_Q, 3))
    wait(loads[1])
    big[...] = nt(dq[...], wbuf[1])

    def back_two(i, _):
        normed, inv_std = normalise(r1[blk(i), :])
        grad = big[blk(i), :]
        ng_o[2:3, :] += jnp.sum(grad * normed, axis=0, keepdims=True)
        ng_o[3:4, :] += jnp.sum(grad, axis=0, keepdims=True)
        total = g2[blk(i), :] + norm_back(grad, normed, inv_std, norms[1:2, :])
        r1[blk(i), :] = total
        low[blk(i), :] = total.astype(BF)
        return 0

    lax.fori_loop(0, rows // QB, back_two, 0, unroll=True)
    g1 = r1
    wait(inputs[7:13])
    wait(store_co)
    gbuf[0] = tn(att[...], low[...]).astype(BF)
    stores.append(store(W_O, 0))
    wait(loads[2])
    gca[...] = nt(low[...], wbuf[2]).astype(BF)
    kpad[pl.ds(0, QB), :] = jnp.zeros((QB, D), BF)
    vpad[pl.ds(0, QB), :] = jnp.zeros((QB, D), BF)
    acck[...] = jnp.zeros_like(acck)
    accv[...] = jnp.zeros_like(accv)
    lax.fori_loop(0, rows // QB, deltas, 0)
    wait([out_k, out_v])

    def attend(b, _):
        allowed = causal_mask(meta, captions, b)
        span = pl.ds(pl.multiple_of(b * QB, QB), 2 * QB)
        group = range(PAIRS)
        q2 = [two_heads(q[blk(b), lanes(p)], masks) for p in group]
        go2 = [two_heads(gca[blk(b), lanes(p)], masks) for p in group]
        scores = [nt(kpad[span, lanes(p)], q2[p]) for p in group]
        gps = [nt(vpad[span, lanes(p)], go2[p]) for p in group]
        table = delta[b]
        probs = [
            jnp.where(allowed, jnp.exp(scores[p] - slse[b, p : p + 1, :]), 0.0) for p in group
        ]
        for p in group:
            accv[span, lanes(p)] += nn(probs[p].astype(BF), go2[p])
        gss = [(probs[p] * (gps[p] - pair_row(table, p))).astype(BF) for p in group]
        for p in group:
            acck[span, lanes(p)] += nn(gss[p], q2[p])
        for p in group:
            gq = merge_heads(tn(kpad[span, lanes(p)], gss[p])).T * SCALE
            dq[blk(b), lanes(p)] = gq.astype(BF)
        return 0

    lax.fori_loop(0, rows // QB, attend, 0)
    sk, sv = dk.at[pl.ds(0, rows)], dv.at[pl.ds(0, rows)]
    sk[...] = acck[body, :].astype(BF)
    sv[...] = accv[body, :].astype(BF)

    for done in stores[:3]:
        wait(done)
    wait(inputs[13:])
    for slot, matrix, grad in ((1, W_Q, dq), (2, W_K, sk), (3, W_V, sv)):
        gbuf[slot] = tn(low_n[...], grad[...]).astype(BF)
        stores.append(store(matrix, slot))
    for load in loads[3:]:
        wait(load)
    big[...] = nt(dq[...], wbuf[3]) + nt(sk[...], wbuf[4]) + nt(sv[...], wbuf[5])

    def back_one(i, _):
        normed, inv_std = normalise(x[blk(i), :].astype(F32))
        grad = big[blk(i), :]
        ng_o[0:1, :] += jnp.sum(grad * normed, axis=0, keepdims=True)
        ng_o[1:2, :] += jnp.sum(grad, axis=0, keepdims=True)
        gt_o[blk(i), :] = (g1[blk(i), :] + norm_back(grad, normed, inv_std, norms[0:1, :])).astype(
            BF
        )
        return 0

    lax.fori_loop(0, rows // QB, back_one, 0, unroll=True)
    for done in stores[3:]:
        wait(done)


def run_attention_backward(captions, images, inv, meta, g2, x, kept, enc, norms, slots, grads):
    rows = g2.shape[0]
    low = pltpu.VMEM((rows, D), BF)
    pad = pltpu.VMEM((rows + QB, D), BF)
    padf = pltpu.VMEM((rows + QB, D), F32)
    big = pltpu.VMEM((rows, D), F32)
    wide = pltpu.VMEM(enc.shape, BF)
    kv = jax.ShapeDtypeStruct(enc.shape, BF)
    dma = pltpu.SemaphoreType.DMA
    return call(
        functools.partial(attention_backward, captions, images),
        (
            jax.ShapeDtypeStruct((rows, D), BF),
            jax.ShapeDtypeStruct((4, D), F32),
            kv,
            kv,
            jax.ShapeDtypeStruct(slots.shape, BF),
        ),
        [SM, SM, VM] + [ANY] * 9 + [VM, ANY, ANY, ANY, ANY, VM, VM, ANY, VM, ANY, ANY],
        (VM, VM, ANY, ANY, ANY),
        [
            pltpu.VMEM((6, D, D), BF), pltpu.VMEM((4, D, D), BF), low, low, pad, pad, low, big, low,
            wide, wide, wide, low, low, padf, padf, big, big, low,
            pltpu.VMEM((rows // QB, HEAD_ROWS, QB), F32),
            dma((6, PER)), dma((4, PER)), dma((14,)), dma((2,)),
        ],
        aliases={22: 4},
    )(inv, meta, g2, x, *kept, enc, norms, slots, grads)


MESH = pl.DeviceIdType.MESH
X_, Y_, UP_, DN_ = 0, 1, 2, 3
OPPOSITE = (X_, Y_, DN_, UP_)
Z_CHIPS = 4
DIMS = {"x": 2, "y": 2, "z": Z_CHIPS}


class Plan:
    def __init__(self, parts, arrivals):
        self.rows = [rows for rows, _ in parts]
        self.order = [order for _, order in parts]
        self.off = [sum(self.rows[:i]) for i in range(len(parts))]
        self.count = len(parts)
        self.shard = sum(self.rows)
        self.pieces = [
            (part, dt, step, dy)
            for part, dt, dz, dy in arrivals
            for step in ((-dz, dz) if dz else (0,))
        ]

    def last_axis(self, part, dt, dz, dy):
        moved = {"x": dt, "y": dy, "z": dz}
        return max((i for i, axis in enumerate(self.order[part]) if moved[axis]), default=-1)

    def routes(self, part, dt, dz, dy):
        order = self.order[part]
        last = self.last_axis(part, dt, dz, dy)
        kinds = []
        if last >= 0 and order[last] == "z":
            kinds.append(UP_ if dz < 0 else DN_)
        for axis in order[last + 1 :]:
            kinds += {"x": [X_], "y": [Y_], "z": [UP_, DN_]}[axis]
        return kinds

    def source(self, part, dt, dz, dy):
        axis = self.order[part][self.last_axis(part, dt, dz, dy)]
        return {"x": X_, "y": Y_, "z": UP_ if dz > 0 else DN_}[axis]

    def landing_spots(self, part, kind):
        axis = "xyzz"[kind]
        ahead = self.order[part]
        ahead = ahead[: ahead.index(axis)] + ("z" if axis == "z" else "")
        spots = 1
        for name in ahead:
            spots *= DIMS[name]
        return ahead, spots

    def slot_rows(self, chip, core, part):
        first = (chip * 2 + core) * self.shard + self.off[part]
        return pl.ds(pl.multiple_of(first, 32), self.rows[part])


G_PLAN = Plan(
    ((64, "xyz"), (64, "zxy"), (128, "zyx"), (128, "xzy")),
    (
        (0, 0, 1, 0), (3, 1, 0, 0), (2, 0, 0, 1), (0, 1, 0, 0), (1, 0, 0, 1), (1, 0, 1, 0),
        (0, 0, 0, 1), (3, 0, 1, 0), (2, 0, 1, 0), (2, 1, 0, 0), (1, 1, 0, 0), (3, 0, 0, 1),
        (0, 0, 2, 0), (3, 1, 1, 0), (3, 1, 0, 1), (0, 1, 1, 0), (0, 1, 0, 1), (1, 0, 2, 0),
        (0, 0, 1, 1), (1, 0, 1, 1), (3, 0, 2, 0), (2, 0, 1, 1), (3, 0, 1, 1), (2, 0, 2, 0),
        (1, 1, 1, 0), (1, 1, 0, 1), (0, 1, 1, 1), (3, 1, 2, 0), (0, 0, 3, 0), (0, 1, 2, 0),
        (2, 1, 0, 1), (0, 0, 2, 1), (1, 0, 3, 0), (3, 1, 1, 1), (1, 0, 2, 1), (2, 1, 1, 0),
        (3, 0, 3, 0), (2, 0, 2, 1), (3, 0, 2, 1), (1, 1, 1, 1), (2, 0, 3, 0), (0, 1, 2, 1),
        (1, 0, 3, 1), (1, 1, 2, 0), (3, 1, 2, 1), (2, 1, 1, 1), (3, 0, 3, 1), (2, 1, 2, 0),
        (2, 0, 3, 1), (3, 1, 3, 0), (0, 1, 3, 0), (1, 1, 3, 0), (0, 0, 3, 1), (1, 1, 2, 1),
        (2, 1, 3, 0), (2, 1, 2, 1), (0, 1, 3, 1), (1, 1, 3, 1), (3, 1, 3, 1), (2, 1, 3, 1),
    ),
)
OWN_SENDS = ((3, 0), (0, 2), (0, 0), (1, 3), (3, 2), (2, 1), (1, 1), (2, 0), (2, 2), (0, 3), (0, 1), (1, 2), (2, 3), (1, 0), (3, 3), (3, 1))
S_PLAN = Plan(
    ((160, "zxy"), (96, "zyx"), (128, "xyz")),
    (
        (1, 1, 3, 1), (2, 1, 3, 1), (2, 0, 3, 1), (2, 0, 3, 0), (0, 1, 2, 1), (2, 1, 3, 0),
        (0, 1, 3, 1), (0, 0, 3, 1), (2, 1, 2, 1), (1, 0, 3, 1), (2, 0, 2, 1), (1, 1, 3, 0),
        (0, 1, 3, 0), (0, 1, 1, 1), (2, 1, 2, 0), (1, 1, 2, 0), (2, 1, 1, 1), (0, 1, 0, 1),
        (1, 1, 2, 1), (2, 0, 1, 1), (1, 0, 3, 0), (0, 0, 1, 1), (0, 0, 2, 1), (0, 0, 3, 0),
        (1, 1, 0, 1), (0, 1, 2, 0), (2, 0, 2, 0), (1, 1, 1, 1), (2, 1, 1, 0), (2, 1, 0, 1),
        (0, 1, 1, 0), (1, 0, 2, 1), (1, 1, 1, 0), (0, 0, 2, 0), (2, 0, 1, 0), (0, 1, 0, 0),
        (1, 0, 1, 1), (0, 0, 0, 1), (1, 1, 0, 0), (1, 0, 2, 0), (2, 0, 0, 1), (1, 0, 0, 1),
        (0, 0, 1, 0), (2, 1, 0, 0), (1, 0, 1, 0),
    ),
)
GT_AT = 3


class Place:
    def __init__(self):
        self.t = lax.axis_index("tower")
        d = lax.axis_index("dp")
        self.z, self.y, self.c = d // 4, (d // 2) % 2, d % 2

    def device(self, t, z, y, c):
        return (t, z * 4 + y * 2 + c)

    def neighbour(self, kind):
        t, z, y, c = self.t, self.z, self.y, self.c
        return (
            self.device(1 - t, z, y, c),
            self.device(t, z, 1 - y, c),
            self.device(t, jnp.minimum(z + 1, Z_CHIPS - 1), y, c),
            self.device(t, jnp.maximum(z - 1, 0), y, c),
        )[kind]

    def line(self):
        return [
            self.device(self.t, lax.rem(self.z + k, Z_CHIPS), self.y, self.c)
            for k in range(1, Z_CHIPS)
        ]

    def sibling(self):
        return self.device(self.t, self.z, self.y, 1 - self.c)

    def has(self, kind):
        return {UP_: self.z < Z_CHIPS - 1, DN_: self.z > 0}.get(kind)

    def chip(self, dt=0, dz=0, dy=0):
        t = 1 - self.t if dt else self.t
        y = 1 - self.y if dy else self.y
        return t * 8 + (self.z + dz) * 2 + y

    def exists(self, dz):
        return None if dz == 0 else self.z >= -dz if dz < 0 else self.z < Z_CHIPS - dz


def both(first, second):
    return second if first is None else first if second is None else first & second


def when(condition, body):
    if condition is None:
        body()
    else:
        pl.when(condition)(body)


def greet(place, whole_line):
    barrier = pltpu.get_barrier_semaphore()
    targets = [place.neighbour(X_), place.neighbour(Y_), place.sibling()]
    if whole_line:
        targets += place.line()
    for target in targets:
        pl.semaphore_signal(barrier, inc=1, device_id=target, device_id_type=MESH)
    if whole_line:
        pl.semaphore_wait(barrier, len(targets))
        return
    for kind in (UP_, DN_):

        @pl.when(place.has(kind))
        def _(kind=kind):
            pl.semaphore_signal(
                barrier, inc=1, device_id=place.neighbour(kind), device_id_type=MESH
            )

    inner = (place.z > 0) & (place.z < Z_CHIPS - 1)
    pl.semaphore_wait(barrier, jnp.where(inner, len(targets) + 2, len(targets) + 1))


def plan_captions(lengths, picks, start_s, sorted_s, bound_s, images):
    captions = lengths.shape[1]

    def begin(c, run):
        start_s[c] = run
        return run + lengths[0, c]

    lax.fori_loop(0, captions, begin, jnp.int32(0))

    def image(i, run):
        bound_s[i] = run

        def caption(c, run):
            hit = picks[0, c] == i
            sorted_s[c] = jnp.where(hit, run, sorted_s[c])
            return run + jnp.where(hit, lengths[0, c], 0)

        return lax.fori_loop(0, captions, caption, run)

    def clear(c, run):
        sorted_s[c] = 0
        return run

    lax.fori_loop(0, captions, clear, 0)
    bound_s[images] = lax.fori_loop(0, images, image, jnp.int32(0))


def gather_kernel(
    images, lengths, picks, tokens, cot, img, master, norms,
    slots, x_o, meta_o, cot_o, enc_o, place_o,
    own, xs, metas, start_s, sorted_s, bound_s,
    ssem, rsem, sibsem, sibrecv, xsem, lsem,
):
    place = Place()
    rows = tokens.shape[0]
    captions = lengths.shape[1]
    own[...] = master[...].astype(BF)
    greet(place, False)
    sends = []

    def push(condition, part, chip, kind, mine=False):
        target = place.sibling() if kind == 4 else place.neighbour(kind)
        if kind < 4:
            condition = both(condition, place.has(kind))
        rows_p = G_PLAN.slot_rows(chip, place.c, part)
        src = own.at[pl.ds(G_PLAN.off[part], G_PLAN.rows[part])] if mine else slots.at[rows_p]
        sem = sibrecv if kind == 4 else rsem
        out = sibsem.at[part, chip] if kind == 4 else ssem.at[kind, part, chip]
        copy = pltpu.make_async_remote_copy(
            src_ref=src, dst_ref=slots.at[rows_p], send_sem=out, recv_sem=sem.at[part, chip],
            device_id=target, device_id_type=MESH,
        )
        when(condition, copy.start)
        sends.append((condition, copy))

    me = place.chip()
    for part, kind in OWN_SENDS + tuple((part, 4) for part in range(G_PLAN.count)):
        push(None, part, me, kind, mine=True)
    keep = pltpu.make_async_copy(
        own, slots.at[pl.ds(pl.multiple_of((me * 2 + place.c) * own.shape[0], 128), own.shape[0])], lsem
    )
    keep.start()

    plan_captions(lengths, picks, start_s, sorted_s, bound_s, images)
    token = lax.broadcasted_iota(jnp.int32, (1, rows), 1)

    def locate(c, where_to):
        inside = (token >= start_s[c]) & (token < start_s[c] + lengths[0, c])
        return jnp.where(inside, token + (sorted_s[c] - start_s[c]), where_to)

    where_to = lax.fori_loop(0, captions, locate, token)
    place_o[...] = jnp.broadcast_to(where_to, place_o.shape)
    lane = lax.broadcasted_iota(jnp.int32, metas.shape, 1)

    def note(c, row):
        return jnp.where(lane == c, sorted_s[c], row)

    row = lax.fori_loop(0, captions, note, jnp.zeros(metas.shape, jnp.int32))
    for i in range(images + 1):
        row = jnp.where(lane == BOUND_LANE + i, bound_s[i], row)
    metas[...] = row

    def sort(out, array):
        def body(b, _):
            target = lax.broadcasted_iota(jnp.int32, (QB, rows), 0) + b * QB
            onehot = (target == place_o[0:1, :]).astype(F32).astype(BF)
            out[blk(b), :] = nn(onehot, array[...]).astype(BF)
            return 0

        lax.fori_loop(0, rows // QB, body, 0)

    sort(xs, tokens)
    swaps = []
    for i, (src, dst) in enumerate(((metas, meta_o), (xs, x_o))):
        swaps.append(
            pltpu.make_async_remote_copy(
                src_ref=src, dst_ref=dst, send_sem=xsem.at[0, i], recv_sem=xsem.at[1, i],
                device_id=place.neighbour(X_), device_id_type=MESH,
            )
        )
        swaps[-1].start()

    def encode(i):
        def body(j, _):
            at = pl.ds(pl.multiple_of(i * IMG_ROWS + j * 64, 64), 64)
            normed, _i = normalise(img[at, :].astype(F32))
            enc_o[at, :] = (normed * norms[3:4, :] + norms[7:8, :]).astype(BF)
            return 0

        lax.fori_loop(0, IMG_ROWS // 64, body, 0)

    steps = img.shape[0] // IMG_ROWS
    done = 0
    for number, (part, dt, dz, dy) in enumerate(G_PLAN.pieces):
        there = place.exists(dz)
        chip = place.chip(dt, dz, dy)

        def arrived(part=part, chip=chip):
            rows_p = G_PLAN.slot_rows(chip, place.c, part)
            pltpu.make_async_remote_copy(
                src_ref=slots.at[rows_p], dst_ref=slots.at[rows_p], send_sem=ssem.at[0, part, chip],
                recv_sem=rsem.at[part, chip], device_id=place.neighbour(X_), device_id_type=MESH,
            ).wait_recv()

        when(there, arrived)
        for kind in G_PLAN.routes(part, dt, dz, dy) + [4]:
            push(there, part, chip, kind)
        if number == 4:
            sort(cot_o, cot)
        if number >= 6 and done < steps:
            encode(done)
            done += 1
    for i in range(done, steps):
        encode(i)

    def from_sibling(chip, _):
        for part in range(G_PLAN.count):
            rows_p = G_PLAN.slot_rows(chip, 1 - place.c, part)
            pltpu.make_async_remote_copy(
                src_ref=slots.at[rows_p], dst_ref=slots.at[rows_p], send_sem=sibsem.at[part, chip],
                recv_sem=sibrecv.at[part, chip], device_id=place.sibling(), device_id_type=MESH,
            ).wait_recv()
        return 0

    lax.fori_loop(0, 4 * Z_CHIPS, from_sibling, 0)
    for condition, copy in sends:
        when(condition, copy.wait_send)
    for swap in swaps:
        swap.wait()
    keep.wait()


IMG_ROWS = 192
ENC_ROWS = 192


def run_gather(images, lengths, picks, tokens, cot, img, master, norms, total_rows):
    rows = tokens.shape[0]
    dma = pltpu.SemaphoreType.DMA
    low = jax.ShapeDtypeStruct((rows, D), BF)
    return pl.pallas_call(
        functools.partial(gather_kernel, images),
        out_shape=(
            jax.ShapeDtypeStruct((total_rows, D), BF),
            low,
            jax.ShapeDtypeStruct((8, 128), jnp.int32),
            low,
            jax.ShapeDtypeStruct(img.shape, BF),
            jax.ShapeDtypeStruct((8, rows), jnp.int32),
        ),
        in_specs=[SM, SM, VM, VM, VM, VM, VM],
        out_specs=(ANY, ANY, ANY, VM, VM, VM),
        scratch_shapes=[
            pltpu.VMEM(master.shape, BF),
            pltpu.VMEM((rows, D), BF),
            pltpu.VMEM((8, 128), jnp.int32),
            pltpu.SMEM((lengths.shape[1],), jnp.int32),
            pltpu.SMEM((lengths.shape[1],), jnp.int32),
            pltpu.SMEM((images + 1,), jnp.int32),
            dma((4, G_PLAN.count, 16)),
            dma((G_PLAN.count, 16)),
            dma((G_PLAN.count, 16)),
            dma((G_PLAN.count, 16)),
            dma((2, 2)),
            dma,
        ],
        compiler_params=pltpu.CompilerParams(
            vmem_limit_bytes=VLIM, has_side_effects=True, collective_id=0
        ),
    )(lengths, picks, tokens, cot, img, master, norms)


def sum_kernel(
    grads, norm_terms, place_row, gt, out_back, dk_h, dv_h, w_h, img_h, norms,
    red_o, norm_o, gt_o, lay_o, gi_h,
    wkv, ebuf, obuf, ng, esem, osem, wksem, acc, sib, gtr, nbuf, nrecv,
    lsem, sibsem, sibrecv, ssem, rsem, gsem, nsend, nrs, *land,
):
    place = Place()
    rows = gt.shape[0]
    greet(place, True)
    order = S_PLAN.pieces + [(part, 0, 0, 0) for part in range(S_PLAN.count)]
    sends = []

    def local(part, chip):
        off = pl.ds(S_PLAN.off[part], S_PLAN.rows[part])
        return pltpu.make_async_copy(
            grads.at[S_PLAN.slot_rows(chip, place.c, part)], acc.at[chip, off], lsem.at[part, chip]
        )

    def across(part, chip):
        off = pl.ds(S_PLAN.off[part], S_PLAN.rows[part])
        return pltpu.make_async_remote_copy(
            src_ref=grads.at[S_PLAN.slot_rows(chip, 1 - place.c, part)], dst_ref=sib.at[chip, off],
            send_sem=sibsem.at[part, chip], recv_sem=sibrecv.at[part, chip],
            device_id=place.sibling(), device_id_type=MESH,
        )

    for part, dt, dz, dy in order:
        chip = place.chip(dt, dz, dy)

        def begin(part=part, chip=chip):
            across(part, chip).start()
            local(part, chip).start()

        when(place.exists(dz), begin)
    back = pltpu.make_async_remote_copy(
        src_ref=gt, dst_ref=gtr, send_sem=gsem.at[0], recv_sem=gsem.at[1],
        device_id=place.neighbour(X_), device_id_type=MESH,
    )

    def landing(part, kind, chip):
        at = {"x": chip // 8, "z": (chip // 2) % Z_CHIPS, "y": chip % 2}
        spot = 0
        for name in S_PLAN.landing_spots(part, kind)[0]:
            spot = spot * DIMS[name] + at[name]
        return land[part * 4 + kind].at[spot]

    def flow(part, kind, chip):
        off = pl.ds(S_PLAN.off[part], S_PLAN.rows[part])
        return pltpu.make_async_remote_copy(
            src_ref=acc.at[chip, off], dst_ref=landing(part, kind, chip),
            send_sem=ssem.at[part, chip], recv_sem=rsem.at[kind, part, chip],
            device_id=place.neighbour(kind), device_id_type=MESH,
        )

    def add(part, chip, other, final):
        def body(i, _):
            at = pl.ds(pl.multiple_of(S_PLAN.off[part] + i * 32, 32), 32)
            value = acc[chip, at, :].astype(F32)
            for ref in other:
                value = value + ref(part, pl.ds(pl.multiple_of(i * 32, 32), 32), at).astype(F32)
            if final:
                red_o[at, :] = value
            else:
                acc[chip, at, :] = value.astype(BF)
            return 0

        lax.fori_loop(0, S_PLAN.rows[part] // 32, body, 0)

    def norm_round(i, target):
        return pltpu.make_async_remote_copy(
            src_ref=nbuf.at[i], dst_ref=nrecv.at[i], send_sem=nsend.at[i], recv_sem=nrs.at[i],
            device_id=target, device_id_type=MESH,
        )

    def norm_line(k, target):
        return pltpu.make_async_remote_copy(
            src_ref=nbuf.at[3], dst_ref=nrecv.at[3 + place.z], send_sem=nsend.at[3 + k],
            recv_sem=nrs.at[3 + place.z], device_id=target, device_id_type=MESH,
        )

    def norm_from(z):
        return pltpu.make_async_remote_copy(
            src_ref=nbuf.at[3], dst_ref=nrecv.at[3 + z], send_sem=nsend.at[3], recv_sem=nrs.at[3 + z],
            device_id=place.neighbour(X_), device_id_type=MESH,
        )

    line = [norm_line(k, target) for k, target in enumerate(place.line())]
    rounds = [place.sibling(), place.neighbour(X_), place.neighbour(Y_)]
    keys = pltpu.make_async_copy(w_h, wkv, wksem)
    keys.start()
    steps = dk_h.shape[0] // ENC_ROWS
    ng[...] = jnp.zeros_like(ng)

    def fetch(i):
        at = pl.ds(i * ENC_ROWS, ENC_ROWS)
        return [
            pltpu.make_async_copy(ref.at[at], ebuf.at[j, i % 2], esem.at[j, i % 2])
            for j, ref in enumerate((dk_h, dv_h, img_h))
        ]

    def put(i):
        at = pl.ds(i * ENC_ROWS, ENC_ROWS)
        return [pltpu.make_async_copy(obuf.at[i % 2], gi_h.at[at], osem.at[i % 2])]

    def encoder_back(i):
        wait(fetch(i))
        if i >= 2:
            wait(put(i - 2))
        out = obuf.at[i % 2]
        out[...] = nt(ebuf[0, i % 2], wkv[0]) + nt(ebuf[1, i % 2], wkv[1])

        def body(j, _):
            normed, inv_std = normalise(ebuf[2, i % 2, blk(j, 64), :].astype(F32))
            grad = out[blk(j, 64), :].astype(BF).astype(F32)
            ng[0:1, :] += jnp.sum(grad * normed, axis=0, keepdims=True)
            ng[1:2, :] += jnp.sum(grad, axis=0, keepdims=True)
            out[blk(j, 64), :] = norm_back(grad, normed, inv_std, norms[3:4, :])
            return 0

        lax.fori_loop(0, ENC_ROWS // 64, body, 0)
        start(put(i))
        if i + 2 < steps:
            start(fetch(i + 2))

    start(fetch(0))
    start(fetch(1))

    def unsort(out, array):
        def body(b, _):
            target = lax.broadcasted_iota(jnp.int32, (rows, QB), 0)
            onehot = (target == place_row[0:1, blk(b)]).astype(F32).astype(BF)
            out[blk(b), :] = tn(onehot, array[...]).astype(out.dtype)
            return 0

        lax.fori_loop(0, rows // QB, body, 0)

    span = len(order) // 2 - 4
    enc_at = [2 + i * span // steps for i in range(steps)]
    norm_at = [span + 3 + (i * len(order)) // 14 for i in range(4)]
    for number, (part, dt, dz, dy) in enumerate(order):
        chip = place.chip(dt, dz, dy)
        if number == GT_AT:
            back.start()
        there = place.exists(dz)
        final = (dt, dz, dy) == (0, 0, 0)
        kinds = S_PLAN.routes(part, dt, dz, dy)

        def step(part=part, chip=chip, kinds=kinds, final=final, dt=dt, dz=dz, dy=dy):
            local(part, chip).wait()
            across(part, chip).wait_recv()
            refs = [lambda p, i, at: sib[chip, at, :]]
            fixed = [kind for kind in kinds if kind in (X_, Y_)]
            edge = [kind for kind in kinds if kind in (UP_, DN_)]
            for kind in fixed:
                flow(part, OPPOSITE[kind], chip).wait_recv()
                refs.append(
                    lambda p, i, at, kind=kind: landing(part, OPPOSITE[kind], chip)[i, :]
                )
            for kind in edge:

                def one(kind=kind):
                    flow(part, OPPOSITE[kind], chip).wait_recv()
                    add(part, chip, [lambda p, i, at: landing(part, OPPOSITE[kind], chip)[i, :]], False)

                pl.when(place.has(kind))(one)
            add(part, chip, refs, final)
            if not final:
                flow(part, S_PLAN.source(part, dt, dz, dy), chip).start()

        when(there, step)
        if not final:
            sends.append((there, part, chip, S_PLAN.source(part, dt, dz, dy)))
        if number in enc_at:
            if number == enc_at[0]:
                keys.wait()
            encoder_back(enc_at.index(number))
        if number == norm_at[0]:
            nbuf[0] = norm_terms[...]
            nbuf[0, 3:4, :] = ng[0:1, :]
            nbuf[0, 7:8, :] = ng[1:2, :]
            norm_round(0, rounds[0]).start()
        if number in norm_at[1:]:
            i = norm_at.index(number) - 1
            norm_round(i, rounds[i]).wait()
            nbuf[i + 1] = nbuf[i] + nrecv[i]
            if i < 2:
                norm_round(i + 1, rounds[i + 1]).start()
            else:
                for copy in line:
                    copy.start()
        if number == norm_at[0] + 1:
            unsort(lay_o, out_back)
        if number == norm_at[3] + 1:
            back.wait()
            unsort(gt_o, gtr)

    for z in range(Z_CHIPS):

        @pl.when(place.z != z)
        def _(z=z):
            norm_from(z).wait_recv()

        @pl.when(place.z == z)
        def _(z=z):
            nrecv[3 + z] = nbuf[3]

    wait(put(steps - 2) + put(steps - 1))
    norm_o[...] = (nrecv[3] + nrecv[4]) + (nrecv[5] + nrecv[6])
    for copy in line:
        copy.wait_send()
    for there, part, chip, kind in sends:
        when(there, flow(part, kind, chip).wait_send)

    def sent(chip, _):
        for part in range(S_PLAN.count):
            across(part, chip).wait_send()
        return 0

    lax.fori_loop(0, 4 * Z_CHIPS, sent, 0)


def run_sum(grads, norm_terms, place_row, gt, out_back, dk, dv, kv_weights, img, norms):
    rows = gt.shape[0]
    dma = pltpu.SemaphoreType.DMA
    shard = S_PLAN.shard
    line = 4 * Z_CHIPS
    return pl.pallas_call(
        sum_kernel,
        out_shape=(
            jax.ShapeDtypeStruct((shard, D), F32),
            jax.ShapeDtypeStruct((8, D), F32),
            jax.ShapeDtypeStruct((rows, D), F32),
            jax.ShapeDtypeStruct((rows, D), BF),
            jax.ShapeDtypeStruct(img.shape, F32),
        ),
        in_specs=[ANY, VM, VM, ANY, VM, ANY, ANY, ANY, ANY, VM],
        out_specs=(VM,) * 4 + (ANY,),
        scratch_shapes=[
            pltpu.VMEM((2, D, D), BF),
            pltpu.VMEM((3, 2, ENC_ROWS, D), BF),
            pltpu.VMEM((2, ENC_ROWS, D), F32),
            pltpu.VMEM((8, D), F32),
            dma((3, 2)),
            dma((2,)),
            dma,
            pltpu.VMEM((line, shard, D), BF),
            pltpu.VMEM((line, shard, D), BF),
            pltpu.VMEM((rows, D), BF),
            pltpu.VMEM((4, 8, D), F32),
            pltpu.VMEM((7, 8, D), F32),
            dma((S_PLAN.count, line)),
            dma((S_PLAN.count, line)),
            dma((S_PLAN.count, line)),
            dma((S_PLAN.count, line)),
            dma((4, S_PLAN.count, line)),
            dma((2,)),
            dma((7,)),
            dma((7,)),
        ]
        + [
            pltpu.VMEM((S_PLAN.landing_spots(part, kind)[1], S_PLAN.rows[part], D), BF)
            for part in range(S_PLAN.count)
            for kind in range(4)
        ],
        compiler_params=pltpu.CompilerParams(
            vmem_limit_bytes=VLIM, has_side_effects=True, collective_id=1
        ),
    )(grads, norm_terms, place_row, gt, out_back, dk, dv, kv_weights, img, norms)


def from_partner(block, axis):
    half = lax.axis_size(axis) // 2
    count = lax.axis_size(axis)
    return lax.ppermute(block, axis, [(i, (i + half) % count) for i in range(count)])


def adamw_update(weight, moment, second, grad_in, rate, decay_rate):
    new_moment = beta_one * moment + (1.0 - beta_one) * grad_in
    new_second = beta_two * second + (1.0 - beta_two) * grad_in * grad_in
    moment_hat = new_moment / (1.0 - beta_one**STEP)
    second_hat = new_second / (1.0 - beta_two**STEP)
    new_weight = weight - rate * (
        moment_hat / (jnp.sqrt(second_hat) + epsilon) + decay_rate * weight
    )
    return (new_weight, new_moment, new_second)


def caption_plan(lengths, picks, rows, images):
    ends = jnp.cumsum(lengths)
    starts = ends - lengths
    rank = picks * lengths.shape[0] + jnp.arange(lengths.shape[0], dtype=jnp.int32)
    ahead = rank[None, :] < rank[:, None]
    sorted_starts = jnp.sum(jnp.where(ahead, lengths[None, :], 0), axis=1)
    token = jnp.arange(rows, dtype=jnp.int32)
    inside = (token[:, None] >= starts[None, :]) & (token[:, None] < ends[None, :])
    place = token + jnp.sum(jnp.where(inside, (sorted_starts - starts)[None, :], 0), axis=1)
    edges = jnp.arange(images + 1, dtype=jnp.int32)
    bounds = jnp.sum(jnp.where(picks[None, :] < edges[:, None], lengths[None, :], 0), axis=1)
    return place, sorted_starts, bounds


def per_device(
    kernels,
    tokens,
    cotangent,
    caption_lengths,
    image_index,
    image_states,
    master_weights,
    first_moments,
    second_moments,
    owner_list,
    norm_params,
    norm_first,
    norm_second,
):
    rows = tokens.shape[0]
    groups = owner_list.shape[0]
    total_rows = 8 * D + 2 * FF
    group_rows = total_rows // groups
    images = image_states.shape[0]
    captions = caption_lengths.shape[1]
    axes = ("tower", "dp")
    direct = group_rows == GROUP
    ids = jnp.arange(groups, dtype=jnp.int32)
    inverse = jnp.sum(jnp.where(owner_list[None, :] == ids[:, None], ids[None, :], 0), axis=1)
    img = image_states.reshape(-1, D)
    if kernels:
        gathered, x, meta, sent_cot, enc, place_row = run_gather(
            images, caption_lengths, image_index, tokens, cotangent, img, master_weights,
            norm_params, total_rows,
        )
    else:
        gathered = lax.all_gather(master_weights.astype(BF), axes, axis=0, tiled=True)
        place, starts, bounds = caption_plan(caption_lengths[0], image_index[0], rows, images)
        into = (place[None, :] == jnp.arange(rows, dtype=jnp.int32)[:, None]).astype(BF)
        meta = jnp.zeros((8, 128), jnp.int32)
        meta = meta.at[0, :captions].set(starts)
        meta = meta.at[0, BOUND_LANE : BOUND_LANE + images + 1].set(bounds)
        meta = from_partner(meta, "tower")
        x = from_partner(nn(into, tokens).astype(BF), "tower")
        sent_cot = nn(into, cotangent).astype(BF)
        normed, _i = normalise(img.astype(F32))
        enc = (normed * norm_params[3] + norm_params[7]).astype(BF)
    if direct:
        slots = gathered.reshape(groups, GROUP, D)
        inv = inverse
    else:
        slots = gathered.reshape(groups, group_rows, D)[inverse].reshape(-1, GROUP, D)
        inv = jnp.arange(total_rows // GROUP, dtype=jnp.int32)
    cot = from_partner(sent_cot, "tower")
    *kept, kv_weights, r2 = run_attention_forward(
        captions, images, inv, meta, x, enc, norm_params, slots
    )
    out, g2, ng3, grads = run_feed_forward(inv, r2, cot, norm_params, slots)
    out_back = from_partner(out, "tower")
    gt, ng, dk, dv, grads = run_attention_backward(
        captions, images, inv, meta, g2, x, kept, enc, norm_params, slots, grads
    )
    none = jnp.zeros((1, D), F32)
    norm_terms = jnp.concatenate(
        [ng[0:1], ng[2:3], ng3[0:1], none, ng[1:2], ng[3:4], ng3[1:2], none]
    )
    if kernels:
        reduced, norm_grads, grad_tokens, layer_out, grad_images = run_sum(
            grads.reshape(total_rows, D), norm_terms, place_row, gt, out_back, dk, dv, kv_weights,
            img, norm_params,
        )
    else:
        layer_out = tn(into, out_back).astype(BF)
        grad_tokens = tn(into, from_partner(gt, "tower"))
        grad_enc = (nt(dk, kv_weights[0]) + nt(dv, kv_weights[1])).astype(BF).astype(F32)
        normed, inv_std = normalise(img.astype(F32))
        grad_images = norm_back(grad_enc, normed, inv_std, norm_params[3:4])
        norm_terms = norm_terms.at[3].set(jnp.sum(grad_enc * normed, axis=0))
        norm_terms = norm_terms.at[7].set(jnp.sum(grad_enc, axis=0))
        if direct:
            arranged = grads.reshape(total_rows, D)
        else:
            arranged = grads.reshape(groups, group_rows, D)[owner_list].reshape(total_rows, D)
        reduced = lax.psum_scatter(arranged, axes, scatter_dimension=0, tiled=True).astype(F32)
        norm_grads = lax.psum(norm_terms, axes)
    new_weights, new_first, new_second = adamw_update(
        master_weights, first_moments, second_moments, reduced, learn_rate, weight_decay
    )
    norm_new, norm_first_new, norm_second_new = adamw_update(
        norm_params, norm_first, norm_second, norm_grads, norm_rate, 0.0
    )
    return (
        layer_out,
        grad_tokens,
        grad_images.reshape(image_states.shape),
        new_weights,
        new_first,
        new_second,
        new_weights.astype(BF),
        norm_new,
        norm_first_new,
        norm_second_new,
    )


def solution(mesh):
    split = P(("tower", "dp"), None)
    wide = P(("tower", "dp"), None, None)
    in_specs = (split,) * 4 + (wide,) + (split,) * 3 + (P(),) * 4
    out_specs = (split, split, wide) + (split,) * 4 + (P(),) * 3
    shape = dict(mesh.shape)
    kernels = shape["tower"] == 2 and shape["dp"] == 4 * Z_CHIPS
    return jax.shard_map(
        functools.partial(per_device, kernels),
        mesh=mesh,
        in_specs=in_specs,
        out_specs=out_specs,
        check_vma=False,
    )
```

```python
import functools

import jax
import jax.numpy as jnp
from jax import lax
from jax.experimental import pallas as pl
from jax.experimental.pallas import tpu as pltpu
from jax.sharding import PartitionSpec as P

D = 768
HEADS = 12
HDIM = 64
FF = 3072
STEP = 5
PAIRS = HEADS // 2
LANES = 2 * HDIM
QB = 128
HEAD_ROWS = 16
PAIR_GROUPS = ((0, 1, 2), (3, 4, 5))
GROUP = 192
BOUND_LANE = 64
PER = D // GROUP
SCALE = HDIM ** (-0.5)

beta_one = 0.5
beta_two = 0.6
learn_rate = 0.03
norm_rate = 0.4
weight_decay = 0.01
epsilon = 1e-08
norm_eps = 1e-05
masked_score = -1000000000.0

W_Q, W_K, W_V, W_O, C_Q, C_K, C_V, C_O, UP, DOWN = 0, 1, 2, 3, 4, 5, 6, 7, 8, 12

BF = jnp.bfloat16
F32 = jnp.float32
VM = pl.BlockSpec(memory_space=pltpu.VMEM)
SM = pl.BlockSpec(memory_space=pltpu.SMEM)
ANY = pl.BlockSpec(memory_space=pl.ANY)
VLIM = 58 * 2**20


def nn(a, b):
    return lax.dot_general(a, b, (((1,), (0,)), ((), ())), preferred_element_type=F32)


def nt(a, b):
    return lax.dot_general(a, b, (((1,), (1,)), ((), ())), preferred_element_type=F32)


def tn(a, b):
    return lax.dot_general(a, b, (((0,), (0,)), ((), ())), preferred_element_type=F32)


def blk(i, size=QB):
    return pl.ds(pl.multiple_of(i * size, size), size)


def lanes(p):
    return slice(p * LANES, (p + 1) * LANES)


def normalise(x):
    centred = x - jnp.mean(x, axis=-1, keepdims=True)
    inv = lax.rsqrt(jnp.mean(centred * centred, axis=-1, keepdims=True) + norm_eps)
    return centred * inv, inv


def norm_back(grad, normed, inv, gain):
    gn = grad * gain
    m1 = jnp.mean(gn, axis=-1, keepdims=True)
    m2 = jnp.mean(gn * normed, axis=-1, keepdims=True)
    return inv * (gn - m1 - normed * m2)


def head_masks():
    low = (lax.broadcasted_iota(jnp.int32, (1, LANES), 1) < HDIM).astype(F32)
    return low.astype(BF), (1.0 - low).astype(BF)


def two_heads(x, masks):
    return jnp.concatenate([x * masks[0], x * masks[1]], axis=0)


def merge_heads(both):
    return jnp.concatenate([both[:HDIM, :QB], both[HDIM:, QB:]], axis=0)


def weight_copies(slots, inv, buf, sem, matrix, slot):
    return [
        pltpu.make_async_copy(
            slots.at[inv[matrix * PER + j]], buf.at[slot, pl.ds(j * GROUP, GROUP)], sem.at[slot, j]
        )
        for j in range(PER)
    ]


def grad_copies(grads, inv, buf, sem, matrix, slot):
    return [
        pltpu.make_async_copy(
            buf.at[slot, pl.ds(j * GROUP, GROUP)], grads.at[inv[matrix * PER + j]], sem.at[slot, j]
        )
        for j in range(PER)
    ]


def start(copies):
    for copy in copies:
        copy.start()


def wait(copies):
    for copy in copies:
        copy.wait()


def causal_mask(meta, captions, b):
    query = lax.broadcasted_iota(jnp.int32, (1, QB), 1) + b * QB
    first = jnp.zeros((1, QB), jnp.int32)
    for c in range(captions):
        first = jnp.maximum(first, jnp.where(query >= meta[0, c], meta[0, c], 0))
    key = lax.broadcasted_iota(jnp.int32, (2 * QB, QB), 0) + (b - 1) * QB
    allowed = (key >= first) & (key <= query)
    return jnp.concatenate([allowed, allowed], axis=1)


def column_softmax(scores):
    top = jnp.max(scores, axis=0, keepdims=True)
    exponent = jnp.exp(scores - top)
    total = jnp.sum(exponent, axis=0, keepdims=True)
    return exponent, 1.0 / total, top + jnp.log(total)


def head_products(grad, out):
    prod = grad.astype(F32) * out
    high = prod.astype(BF)
    low = (prod - high.astype(F32)).astype(BF)
    head = lax.broadcasted_iota(jnp.int32, (HEAD_ROWS, D), 0)
    lane = lax.broadcasted_iota(jnp.int32, (HEAD_ROWS, D), 1)
    pick = ((lane >= head * HDIM) & (lane < (head + 1) * HDIM)).astype(F32).astype(BF)
    return nt(pick, high) + nt(pick, low)


def pair_row(table, p):
    return jnp.concatenate([table[2 * p : 2 * p + 1], table[2 * p + 1 : 2 * p + 2]], axis=1)


def call(body, out_shape, in_specs, out_specs, scratch, aliases=None, effects=False):
    return pl.pallas_call(
        body,
        out_shape=out_shape,
        in_specs=in_specs,
        out_specs=out_specs,
        scratch_shapes=scratch,
        input_output_aliases=aliases or {},
        compiler_params=pltpu.CompilerParams(vmem_limit_bytes=VLIM, has_side_effects=effects),
    )


def image_blocks(meta, i):
    low, high = meta[0, BOUND_LANE + i], meta[0, BOUND_LANE + i + 1]
    first = low // QB
    last = jnp.where(high > low, (high + QB - 1) // QB, first)
    return low, high, first, last


def blk_of(i, size):
    return pl.ds(pl.multiple_of(i * size, 64), size)


def attention_forward(
    captions, images, inv, meta, x, enc_h, norms, slots,
    q_h, k_h, v_h, att_h, r1_h, cq_h, kk_h, vv_h, cross_h, atf_h, crf_h, fst_h, snd_h, slse_o, clse_o, w_h, r2_o,
    wbuf, low, second, q, kpad, vpad, att, atf, r1, cq, enc, kk, vv, cross, acc, wsem, esem, osem,
):
    rows = x.shape[0]
    patches = enc.shape[0] // images
    loads = [weight_copies(slots, inv, wbuf, wsem, m, m) for m in range(8)]
    for load in loads[:3]:
        start(load)
    enc_copy = pltpu.make_async_copy(enc_h, enc, esem)
    enc_copy.start()
    for m in (C_K, C_V, W_O, C_Q, C_O):
        start(loads[m])
    masks = head_masks()
    copies = []

    def store(i, vmem, hbm):
        copies.append(pltpu.make_async_copy(vmem, hbm, osem.at[i]))
        copies[-1].start()

    def norm_one(i, _):
        normed, _i = normalise(x[blk(i), :].astype(F32))
        low[blk(i), :] = (normed * norms[0:1, :] + norms[4:5, :]).astype(BF)
        return 0

    lax.fori_loop(0, rows // QB, norm_one, 0, unroll=True)
    store(12, low, fst_h)
    kpad[pl.ds(0, QB), :] = jnp.zeros((QB, D), BF)
    vpad[pl.ds(0, QB), :] = jnp.zeros((QB, D), BF)
    wait(loads[W_Q])
    q[...] = (nn(low[...], wbuf[W_Q]) * SCALE).astype(BF)
    store(0, q, q_h)
    wait(loads[W_K])
    kpad[pl.ds(QB, rows), :] = nn(low[...], wbuf[W_K]).astype(BF)
    store(1, kpad.at[pl.ds(QB, rows)], k_h)
    wait(loads[W_V])
    vpad[pl.ds(QB, rows), :] = nn(low[...], wbuf[W_V]).astype(BF)
    store(2, vpad.at[pl.ds(QB, rows)], v_h)
    enc_copy.wait()
    wait(loads[C_K])
    wait(loads[C_V])
    store(3, wbuf.at[pl.ds(C_K, 2)], w_h)

    def attend(b, _):
        allowed = causal_mask(meta, captions, b)
        span = pl.ds(pl.multiple_of(b * QB, QB), 2 * QB)
        scores = [
            nt(kpad[span, lanes(p)], two_heads(q[blk(b), lanes(p)], masks)) for p in range(PAIRS)
        ]
        soft = [column_softmax(jnp.where(allowed, score, masked_score)) for score in scores]
        for p in range(PAIRS):
            exponent, scale, lse = soft[p]
            out = merge_heads(tn(vpad[span, lanes(p)], exponent.astype(BF)) * scale).T
            atf[blk(b), lanes(p)] = out
            att[blk(b), lanes(p)] = out.astype(BF)
            slse_o[b, p : p + 1, :] = lse
        return 0

    lax.fori_loop(0, rows // QB, attend, 0)
    store(4, att, att_h)
    store(10, atf, atf_h)

    def project(c, _):
        kk[blk(c, D), :] = nn(enc[blk(c, D), :], wbuf[C_K]).astype(BF)
        vv[blk(c, D), :] = nn(enc[blk(c, D), :], wbuf[C_V]).astype(BF)
        return 0

    lax.fori_loop(0, enc.shape[0] // D, project, 0)
    store(5, kk, kk_h)
    store(6, vv, vv_h)
    wait(loads[W_O])
    r1[...] = x[...].astype(F32) + nn(att[...], wbuf[W_O])
    store(7, r1, r1_h)

    def norm_two(i, _):
        normed, _i = normalise(r1[blk(i), :])
        second[blk(i), :] = (normed * norms[1:2, :] + norms[5:6, :]).astype(BF)
        return 0

    lax.fori_loop(0, rows // QB, norm_two, 0, unroll=True)
    store(13, second, snd_h)
    wait(loads[C_Q])
    cq[...] = (nn(second[...], wbuf[C_Q]) * SCALE).astype(BF)
    store(8, cq, cq_h)
    acc[...] = jnp.zeros_like(acc)
    clse_o[...] = jnp.zeros_like(clse_o)

    def image(i, _):
        first_row, end_row, first, last = image_blocks(meta, i)

        def attend_image(b, _):
            token = lax.broadcasted_iota(jnp.int32, (1, QB), 1) + b * QB
            here = ((token >= first_row) & (token < end_row)).astype(F32)
            here = jnp.concatenate([here, here], axis=1)
            at = blk_of(i, patches)
            scores = [
                nt(kk[at, lanes(p)], two_heads(cq[blk(b), lanes(p)], masks)) for p in range(PAIRS)
            ]
            soft = [column_softmax(score) for score in scores]
            for p in range(PAIRS):
                exponent, scale, lse = soft[p]
                clse_o[b, p : p + 1, :] = jnp.where(here > 0, lse, clse_o[b, p : p + 1, :])
                out = tn(vv[at, lanes(p)], exponent.astype(BF)) * (scale * here)
                acc[blk(b), lanes(p)] += merge_heads(out).T
            return 0

        lax.fori_loop(first, last, attend_image, 0)
        return 0

    lax.fori_loop(0, images, image, 0)
    cross[...] = acc[...].astype(BF)
    store(9, cross, cross_h)
    store(11, acc, crf_h)
    wait(loads[C_O])
    r2_o[...] = r1[...] + nn(cross[...], wbuf[C_O])
    for copy in copies:
        copy.wait()


def run_attention_forward(captions, images, inv, meta, x, enc, norms, slots):
    rows = x.shape[0]
    one = jax.ShapeDtypeStruct((rows, D), BF)
    full = jax.ShapeDtypeStruct((rows, D), F32)
    kv = jax.ShapeDtypeStruct(enc.shape, BF)
    lse = jax.ShapeDtypeStruct((rows // QB, 8, 2 * QB), F32)
    low = pltpu.VMEM((rows, D), BF)
    pad = pltpu.VMEM((rows + QB, D), BF)
    big = pltpu.VMEM((rows, D), F32)
    wide = pltpu.VMEM(enc.shape, BF)
    return call(
        functools.partial(attention_forward, captions, images),
        (one, one, one, one, full, one, kv, kv, one, full, full, one, one, lse, lse)
        + (jax.ShapeDtypeStruct((2, D, D), BF), full),
        [SM, SM, VM, ANY, VM, ANY],
        (ANY,) * 13 + (VM, VM, ANY, VM),
        [
            pltpu.VMEM((8, D, D), BF), low, low, low, pad, pad, low, big, big, low, wide, wide, wide,
            low, big, pltpu.SemaphoreType.DMA((8, PER)), pltpu.SemaphoreType.DMA,
            pltpu.SemaphoreType.DMA((14,)),
        ],
    )(inv, meta, x, enc, norms, slots)


GELU_A = 0.7978845608028654
GELU_B = GELU_A * 0.044715


def feed_forward(
    inv, r2, cot_h, norms, slots, out_o, g2_o, ng_o, grads,
    cot, csem, wup, wdown, third, pre, gh, hid, gpre, acc, gthird, gup, gdown, usem, dsem, gusem, gdsem,
):
    rows = r2.shape[0]
    chunks = FF // D

    def loads(c, slot):
        return weight_copies(slots, inv, wup, usem, UP + c, slot) + weight_copies(
            slots, inv, wdown, dsem, DOWN + c, slot
        )

    def stores(c, slot):
        return grad_copies(grads, inv, gup, gusem, UP + c, slot) + grad_copies(
            grads, inv, gdown, gdsem, DOWN + c, slot
        )

    start(loads(0, 0))
    cot_copy = pltpu.make_async_copy(cot_h, cot, csem)
    cot_copy.start()

    def norm_three(i, _):
        normed, _i = normalise(r2[blk(i), :])
        third[blk(i), :] = (normed * norms[2:3, :] + norms[6:7, :]).astype(BF)
        return 0

    lax.fori_loop(0, rows // QB, norm_three, 0, unroll=2)
    cot_copy.wait()
    acc[...] = r2[...]
    gthird[...] = jnp.zeros_like(gthird)

    def chunk(c, _):
        slot = c % 2

        @pl.when(c + 1 < chunks)
        def _():
            start(loads(c + 1, 1 - slot))

        wait(loads(c, slot))
        pre[...] = nt(third[...], wup[slot])
        gh[...] = nt(cot[...], wdown[slot])

        def gelu(i, _):
            x = pre[blk(i, 64), :]
            x2 = x * x
            t = jnp.tanh(x * (GELU_A + GELU_B * x2))
            half = 0.5 + 0.5 * t
            value = x * half
            hid[blk(i, 64), :] = value.astype(BF)
            slope = half + value * (1.0 - t) * (GELU_A + 3.0 * GELU_B * x2)
            gpre[blk(i, 64), :] = (gh[blk(i, 64), :] * slope).astype(BF)
            return 0

        lax.fori_loop(0, rows // 64, gelu, 0)

        @pl.when(c >= 2)
        def _():
            wait(stores(c - 2, slot))

        acc[...] += nn(hid[...], wdown[slot])
        gdown[slot] = tn(hid[...], cot[...]).astype(BF)
        gup[slot] = tn(gpre[...], third[...]).astype(BF)
        start(stores(c, slot))
        gthird[...] += nn(gpre[...], wup[slot])
        return 0

    lax.fori_loop(0, chunks, chunk, 0)
    out_o[...] = acc[...].astype(BF)
    ng_o[...] = jnp.zeros_like(ng_o)

    def back(i, _):
        normed, inv_std = normalise(r2[blk(i), :])
        grad = gthird[blk(i), :]
        ng_o[0:1, :] += jnp.sum(grad * normed, axis=0, keepdims=True)
        ng_o[1:2, :] += jnp.sum(grad, axis=0, keepdims=True)
        g2_o[blk(i), :] = cot[blk(i), :].astype(F32) + norm_back(
            grad, normed, inv_std, norms[2:3, :]
        )
        return 0

    lax.fori_loop(0, rows // QB, back, 0)
    for c in range(chunks - 2, chunks):
        wait(stores(c, c % 2))


def run_feed_forward(inv, r2, cot, norms, slots):
    rows = r2.shape[0]
    big = pltpu.VMEM((rows, D), F32)
    low = pltpu.VMEM((rows, D), BF)
    two = pltpu.VMEM((2, D, D), BF)
    sem = pltpu.SemaphoreType.DMA((2, PER))
    return call(
        feed_forward,
        (
            jax.ShapeDtypeStruct((rows, D), BF),
            jax.ShapeDtypeStruct((rows, D), F32),
            jax.ShapeDtypeStruct((2, D), F32),
            jax.ShapeDtypeStruct(slots.shape, BF),
        ),
        [SM, VM, ANY, VM, ANY],
        (VM, VM, VM, ANY),
        [low, pltpu.SemaphoreType.DMA, two, two, low, big, big, low, low, big, big, two, two, sem, sem, sem, sem],
    )(inv, r2, cot, norms, slots)


def attention_backward(
    captions, images,
    inv, meta, g2, x_h, q_h, k_h, v_h, att_h, r1_h, cq_h, kk_h, vv_h, cross, atf_h, crf_h, fst_h, snd_h,
    slse, clse, enc_h, norms, slots, grads_in, ng3,
    gt_o, ng_o, dk_h, dv_h, grads,
    wbuf, gbuf, x, q, kpad, vpad, att, r1, cq, kk, vv, enc, gca, dq, acck, accv, big, out32,
    low_n, delta, wsem, gsem, isem, osem,
):
    rows = g2.shape[0]
    patches = enc.shape[0] // images
    names = (C_O, C_Q, W_O, W_Q, W_K, W_V)
    loads = [weight_copies(slots, inv, wbuf, wsem, m, i) for i, m in enumerate(names)]
    body = pl.ds(QB, rows)
    inputs = [
        pltpu.make_async_copy(hbm, vmem, isem.at[i])
        for i, (hbm, vmem) in enumerate(
            (
                (crf_h, out32), (cq_h, cq), (kk_h, kk), (vv_h, vv), (enc_h, enc), (r1_h, r1),
                (snd_h, low_n), (att_h, att), (q_h, q), (k_h, kpad.at[body]),
                (v_h, vpad.at[body]), (x_h, x), (atf_h, out32), (fst_h, low_n),
            )
        )
    ]
    start(loads[0])
    start(inputs[:5])
    start(loads[1])
    start(inputs[5:12])
    for load in loads[2:]:
        start(load)

    def store(matrix, slot):
        copies = grad_copies(grads, inv, gbuf, gsem, matrix, slot)
        start(copies)
        return copies

    masks = head_masks()
    ng_o[...] = jnp.zeros_like(ng_o)
    ng_o[2:3, :] = ng3[0:1, :]
    ng_o[6:7, :] = ng3[1:2, :]
    low = dq
    low[...] = g2[...].astype(BF)
    gbuf[0] = tn(cross[...], low[...]).astype(BF)
    store_co = store(C_O, 0)
    wait(loads[0])
    gca[...] = nt(low[...], wbuf[0]).astype(BF)
    dq[...] = jnp.zeros_like(dq)
    wait(inputs[:4])

    def deltas(b, _):
        delta[b] = head_products(gca[blk(b), :], out32[blk(b), :])
        return 0

    lax.fori_loop(0, rows // QB, deltas, 0)
    start(inputs[12:13])

    def image(i, _):
        first_row, end_row, first, last = image_blocks(meta, i)
        ik = acck.at[pl.ds(0, patches)]
        iv = accv.at[pl.ds(0, patches)]
        ik[...] = jnp.zeros_like(ik)
        iv[...] = jnp.zeros_like(iv)

        def attend_image(b, _):
            token = lax.broadcasted_iota(jnp.int32, (QB, LANES), 0) + b * QB
            here = ((token >= first_row) & (token < end_row)).astype(F32).astype(BF)
            column = lax.broadcasted_iota(jnp.int32, (1, QB), 1) + b * QB
            inside = (column >= first_row) & (column < end_row)
            inside = jnp.concatenate([inside, inside], axis=1)
            at = blk_of(i, patches)
            table = delta[b]
            for group in PAIR_GROUPS:
                q2 = [two_heads(cq[blk(b), lanes(p)], masks) for p in group]
                go2 = [two_heads(gca[blk(b), lanes(p)] * here, masks) for p in group]
                scores = [nt(kk[at, lanes(p)], one) for p, one in zip(group, q2)]
                gps = [nt(vv[at, lanes(p)], go) for p, go in zip(group, go2)]
                probs = [
                    jnp.exp(score - jnp.where(inside, clse[b, p : p + 1, :], -masked_score))
                    for p, score in zip(group, scores)
                ]
                for p, prob, go in zip(group, probs, go2):
                    iv[:, lanes(p)] += nn(prob.astype(BF), go)
                gss = [
                    (prob * (gp - pair_row(table, p))).astype(BF)
                    for p, prob, gp in zip(group, probs, gps)
                ]
                for p, gs, one in zip(group, gss, q2):
                    ik[:, lanes(p)] += nn(gs, one)
                for p, gs in zip(group, gss):
                    gq = merge_heads(tn(kk[at, lanes(p)], gs)).T * SCALE
                    dq[blk(b), lanes(p)] += gq.astype(BF)
            return 0

        lax.fori_loop(first, last, attend_image, 0)
        kk[blk_of(i, patches), :] = ik[...].astype(BF)
        vv[blk_of(i, patches), :] = iv[...].astype(BF)
        return 0

    lax.fori_loop(0, images, image, 0)
    dk, dv = kk, vv
    out_k = pltpu.make_async_copy(dk, dk_h, osem.at[0])
    out_v = pltpu.make_async_copy(dv, dv_h, osem.at[1])
    start([out_k, out_v])
    wait(inputs[4:5])
    stores = []
    for slot, matrix, grad in ((1, C_K, dk), (2, C_V, dv)):
        gbuf[slot] = tn(enc[...], grad[...]).astype(BF)
        stores.append(store(matrix, slot))
    wait(inputs[5:7])
    gbuf[3] = tn(low_n[...], dq[...]).astype(BF)
    start(inputs[13:])
    stores.append(store(C_Q, 3))
    wait(loads[1])
    big[...] = nt(dq[...], wbuf[1])

    def back_two(i, _):
        normed, inv_std = normalise(r1[blk(i), :])
        grad = big[blk(i), :]
        ng_o[1:2, :] += jnp.sum(grad * normed, axis=0, keepdims=True)
        ng_o[5:6, :] += jnp.sum(grad, axis=0, keepdims=True)
        total = g2[blk(i), :] + norm_back(grad, normed, inv_std, norms[1:2, :])
        r1[blk(i), :] = total
        low[blk(i), :] = total.astype(BF)
        return 0

    lax.fori_loop(0, rows // QB, back_two, 0, unroll=True)
    g1 = r1
    wait(inputs[7:13])
    wait(store_co)
    gbuf[0] = tn(att[...], low[...]).astype(BF)
    stores.append(store(W_O, 0))
    wait(loads[2])
    gca[...] = nt(low[...], wbuf[2]).astype(BF)
    kpad[pl.ds(0, QB), :] = jnp.zeros((QB, D), BF)
    vpad[pl.ds(0, QB), :] = jnp.zeros((QB, D), BF)
    acck[...] = jnp.zeros_like(acck)
    accv[...] = jnp.zeros_like(accv)
    lax.fori_loop(0, rows // QB, deltas, 0)
    wait([out_k, out_v])

    def attend(b, _):
        allowed = causal_mask(meta, captions, b)
        span = pl.ds(pl.multiple_of(b * QB, QB), 2 * QB)
        group = range(PAIRS)
        q2 = [two_heads(q[blk(b), lanes(p)], masks) for p in group]
        go2 = [two_heads(gca[blk(b), lanes(p)], masks) for p in group]
        scores = [nt(kpad[span, lanes(p)], q2[p]) for p in group]
        gps = [nt(vpad[span, lanes(p)], go2[p]) for p in group]
        table = delta[b]
        probs = [
            jnp.where(allowed, jnp.exp(scores[p] - slse[b, p : p + 1, :]), 0.0) for p in group
        ]
        for p in group:
            accv[span, lanes(p)] += nn(probs[p].astype(BF), go2[p])
        gss = [(probs[p] * (gps[p] - pair_row(table, p))).astype(BF) for p in group]
        for p in group:
            acck[span, lanes(p)] += nn(gss[p], q2[p])
        for p in group:
            gq = merge_heads(tn(kpad[span, lanes(p)], gss[p])).T * SCALE
            dq[blk(b), lanes(p)] = gq.astype(BF)
        return 0

    lax.fori_loop(0, rows // QB, attend, 0)
    sk, sv = dk.at[pl.ds(0, rows)], dv.at[pl.ds(0, rows)]
    sk[...] = acck[body, :].astype(BF)
    sv[...] = accv[body, :].astype(BF)

    for done in stores[:3]:
        wait(done)
    wait(inputs[13:])
    for slot, matrix, grad in ((1, W_Q, dq), (2, W_K, sk), (3, W_V, sv)):
        gbuf[slot] = tn(low_n[...], grad[...]).astype(BF)
        stores.append(store(matrix, slot))
    for load in loads[3:]:
        wait(load)
    big[...] = nt(dq[...], wbuf[3]) + nt(sk[...], wbuf[4]) + nt(sv[...], wbuf[5])

    def back_one(i, _):
        normed, inv_std = normalise(x[blk(i), :].astype(F32))
        grad = big[blk(i), :]
        ng_o[0:1, :] += jnp.sum(grad * normed, axis=0, keepdims=True)
        ng_o[4:5, :] += jnp.sum(grad, axis=0, keepdims=True)
        gt_o[blk(i), :] = (g1[blk(i), :] + norm_back(grad, normed, inv_std, norms[0:1, :])).astype(
            BF
        )
        return 0

    lax.fori_loop(0, rows // QB, back_one, 0, unroll=True)
    for done in stores[3:]:
        wait(done)


def run_attention_backward(captions, images, inv, meta, g2, x, kept, enc, norms, slots, grads, ng3):
    rows = g2.shape[0]
    low = pltpu.VMEM((rows, D), BF)
    pad = pltpu.VMEM((rows + QB, D), BF)
    padf = pltpu.VMEM((rows + QB, D), F32)
    big = pltpu.VMEM((rows, D), F32)
    wide = pltpu.VMEM(enc.shape, BF)
    kv = jax.ShapeDtypeStruct(enc.shape, BF)
    dma = pltpu.SemaphoreType.DMA
    return call(
        functools.partial(attention_backward, captions, images),
        (
            jax.ShapeDtypeStruct((rows, D), BF),
            jax.ShapeDtypeStruct((8, D), F32),
            kv,
            kv,
            jax.ShapeDtypeStruct(slots.shape, BF),
        ),
        [SM, SM, VM] + [ANY] * 9 + [VM, ANY, ANY, ANY, ANY, VM, VM, ANY, VM, ANY, ANY, VM],
        (VM, VM, ANY, ANY, ANY),
        [
            pltpu.VMEM((6, D, D), BF), pltpu.VMEM((4, D, D), BF), low, low, pad, pad, low, big, low,
            wide, wide, wide, low, low, padf, padf, big, big, low,
            pltpu.VMEM((rows // QB, HEAD_ROWS, QB), F32),
            dma((6, PER)), dma((4, PER)), dma((14,)), dma((2,)),
        ],
        aliases={22: 4},
    )(inv, meta, g2, x, *kept, enc, norms, slots, grads, ng3)


MESH = pl.DeviceIdType.MESH
X_, Y_, UP_, DN_ = 0, 1, 2, 3
OPPOSITE = (X_, Y_, DN_, UP_)
Z_CHIPS = 4
DIMS = {"x": 2, "y": 2, "z": Z_CHIPS}


class Plan:
    def __init__(self, parts, arrivals):
        self.rows = [rows for rows, _ in parts]
        self.order = [order for _, order in parts]
        self.off = [sum(self.rows[:i]) for i in range(len(parts))]
        self.count = len(parts)
        self.shard = sum(self.rows)
        self.pieces = [
            (part, dt, step, dy)
            for part, dt, dz, dy in arrivals
            for step in ((-dz, dz) if dz else (0,))
        ]

    def last_axis(self, part, dt, dz, dy):
        moved = {"x": dt, "y": dy, "z": dz}
        return max((i for i, axis in enumerate(self.order[part]) if moved[axis]), default=-1)

    def routes(self, part, dt, dz, dy):
        order = self.order[part]
        last = self.last_axis(part, dt, dz, dy)
        kinds = []
        if last >= 0 and order[last] == "z":
            kinds.append(UP_ if dz < 0 else DN_)
        for axis in order[last + 1 :]:
            kinds += {"x": [X_], "y": [Y_], "z": [UP_, DN_]}[axis]
        return kinds

    def source(self, part, dt, dz, dy):
        axis = self.order[part][self.last_axis(part, dt, dz, dy)]
        return {"x": X_, "y": Y_, "z": UP_ if dz > 0 else DN_}[axis]

    def landing_spots(self, part, kind):
        axis = "xyzz"[kind]
        ahead = self.order[part]
        ahead = ahead[: ahead.index(axis)] + ("z" if axis == "z" else "")
        spots = 1
        for name in ahead:
            spots *= DIMS[name]
        return ahead, spots

    def slot_rows(self, chip, core, part):
        first = (chip * 2 + core) * self.shard + self.off[part]
        return pl.ds(pl.multiple_of(first, 32), self.rows[part])


G_PLAN = Plan(
    ((64, "xyz"), (64, "zxy"), (128, "zyx"), (128, "xzy")),
    (
        (0, 0, 1, 0), (3, 1, 0, 0), (2, 0, 0, 1), (0, 1, 0, 0), (1, 0, 0, 1), (1, 0, 1, 0),
        (0, 0, 0, 1), (3, 0, 1, 0), (2, 0, 1, 0), (2, 1, 0, 0), (1, 1, 0, 0), (3, 0, 0, 1),
        (0, 0, 2, 0), (3, 1, 1, 0), (3, 1, 0, 1), (0, 1, 1, 0), (0, 1, 0, 1), (1, 0, 2, 0),
        (0, 0, 1, 1), (1, 0, 1, 1), (3, 0, 2, 0), (2, 0, 1, 1), (3, 0, 1, 1), (2, 0, 2, 0),
        (1, 1, 1, 0), (1, 1, 0, 1), (0, 1, 1, 1), (3, 1, 2, 0), (0, 0, 3, 0), (0, 1, 2, 0),
        (2, 1, 0, 1), (0, 0, 2, 1), (1, 0, 3, 0), (3, 1, 1, 1), (1, 0, 2, 1), (2, 1, 1, 0),
        (3, 0, 3, 0), (2, 0, 2, 1), (3, 0, 2, 1), (1, 1, 1, 1), (2, 0, 3, 0), (0, 1, 2, 1),
        (1, 0, 3, 1), (1, 1, 2, 0), (3, 1, 2, 1), (2, 1, 1, 1), (3, 0, 3, 1), (2, 1, 2, 0),
        (2, 0, 3, 1), (3, 1, 3, 0), (0, 1, 3, 0), (1, 1, 3, 0), (0, 0, 3, 1), (1, 1, 2, 1),
        (2, 1, 3, 0), (2, 1, 2, 1), (0, 1, 3, 1), (1, 1, 3, 1), (3, 1, 3, 1), (2, 1, 3, 1),
    ),
)
OWN_SENDS = ((3, 0), (0, 2), (0, 0), (1, 3), (3, 2), (2, 1), (1, 1), (2, 0), (2, 2), (0, 3), (0, 1), (1, 2), (2, 3), (1, 0), (3, 3), (3, 1))
S_PLAN = Plan(
    ((160, "zxy"), (96, "zyx"), (128, "xyz")),
    (
        (1, 1, 3, 1), (2, 1, 3, 1), (2, 0, 3, 1), (2, 0, 3, 0), (0, 1, 2, 1), (2, 1, 3, 0),
        (0, 1, 3, 1), (0, 0, 3, 1), (2, 1, 2, 1), (1, 0, 3, 1), (2, 0, 2, 1), (1, 1, 3, 0),
        (0, 1, 3, 0), (0, 1, 1, 1), (2, 1, 2, 0), (1, 1, 2, 0), (2, 1, 1, 1), (0, 1, 0, 1),
        (1, 1, 2, 1), (2, 0, 1, 1), (1, 0, 3, 0), (0, 0, 1, 1), (0, 0, 2, 1), (0, 0, 3, 0),
        (1, 1, 0, 1), (0, 1, 2, 0), (2, 0, 2, 0), (1, 1, 1, 1), (2, 1, 1, 0), (2, 1, 0, 1),
        (0, 1, 1, 0), (1, 0, 2, 1), (1, 1, 1, 0), (0, 0, 2, 0), (2, 0, 1, 0), (0, 1, 0, 0),
        (1, 0, 1, 1), (0, 0, 0, 1), (1, 1, 0, 0), (1, 0, 2, 0), (2, 0, 0, 1), (1, 0, 0, 1),
        (0, 0, 1, 0), (2, 1, 0, 0), (1, 0, 1, 0),
    ),
)
GT_AT = 3


class Place:
    def __init__(self):
        self.t = lax.axis_index("tower")
        d = lax.axis_index("dp")
        self.z, self.y, self.c = d // 4, (d // 2) % 2, d % 2

    def device(self, t, z, y, c):
        return (t, z * 4 + y * 2 + c)

    def neighbour(self, kind):
        t, z, y, c = self.t, self.z, self.y, self.c
        return (
            self.device(1 - t, z, y, c),
            self.device(t, z, 1 - y, c),
            self.device(t, jnp.minimum(z + 1, Z_CHIPS - 1), y, c),
            self.device(t, jnp.maximum(z - 1, 0), y, c),
        )[kind]

    def line(self):
        return [
            self.device(self.t, lax.rem(self.z + k, Z_CHIPS), self.y, self.c)
            for k in range(1, Z_CHIPS)
        ]

    def sibling(self):
        return self.device(self.t, self.z, self.y, 1 - self.c)

    def has(self, kind):
        return {UP_: self.z < Z_CHIPS - 1, DN_: self.z > 0}.get(kind)

    def chip(self, dt=0, dz=0, dy=0):
        t = 1 - self.t if dt else self.t
        y = 1 - self.y if dy else self.y
        return t * 8 + (self.z + dz) * 2 + y

    def exists(self, dz):
        return None if dz == 0 else self.z >= -dz if dz < 0 else self.z < Z_CHIPS - dz


def both(first, second):
    return second if first is None else first if second is None else first & second


def when(condition, body):
    if condition is None:
        body()
    else:
        pl.when(condition)(body)


def greet(place, whole_line):
    barrier = pltpu.get_barrier_semaphore()
    targets = [place.neighbour(X_), place.neighbour(Y_), place.sibling()]
    if whole_line:
        targets += place.line()
    for target in targets:
        pl.semaphore_signal(barrier, inc=1, device_id=target, device_id_type=MESH)
    if whole_line:
        pl.semaphore_wait(barrier, len(targets))
        return
    for kind in (UP_, DN_):

        @pl.when(place.has(kind))
        def _(kind=kind):
            pl.semaphore_signal(
                barrier, inc=1, device_id=place.neighbour(kind), device_id_type=MESH
            )

    inner = (place.z > 0) & (place.z < Z_CHIPS - 1)
    pl.semaphore_wait(barrier, jnp.where(inner, len(targets) + 2, len(targets) + 1))


def plan_captions(lengths, picks, start_s, sorted_s, bound_s, images):
    captions = lengths.shape[1]

    def begin(c, run):
        start_s[c] = run
        return run + lengths[0, c]

    lax.fori_loop(0, captions, begin, jnp.int32(0))

    def image(i, run):
        bound_s[i] = run

        def caption(c, run):
            hit = picks[0, c] == i
            sorted_s[c] = jnp.where(hit, run, sorted_s[c])
            return run + jnp.where(hit, lengths[0, c], 0)

        return lax.fori_loop(0, captions, caption, run)

    def clear(c, run):
        sorted_s[c] = 0
        return run

    lax.fori_loop(0, captions, clear, 0)
    bound_s[images] = lax.fori_loop(0, images, image, jnp.int32(0))


def gather_kernel(
    images, lengths, picks, tokens, cot, img, master, norms,
    slots, x_o, meta_o, cot_o, enc_o, place_o,
    own, xs, metas, start_s, sorted_s, bound_s,
    ssem, rsem, sibsem, sibrecv, xsem, lsem,
):
    place = Place()
    rows = tokens.shape[0]
    captions = lengths.shape[1]
    own[...] = master[...].astype(BF)
    greet(place, False)
    sends = []

    def push(condition, part, chip, kind, mine=False):
        target = place.sibling() if kind == 4 else place.neighbour(kind)
        if kind < 4:
            condition = both(condition, place.has(kind))
        rows_p = G_PLAN.slot_rows(chip, place.c, part)
        src = own.at[pl.ds(G_PLAN.off[part], G_PLAN.rows[part])] if mine else slots.at[rows_p]
        sem = sibrecv if kind == 4 else rsem
        out = sibsem.at[part, chip] if kind == 4 else ssem.at[kind, part, chip]
        copy = pltpu.make_async_remote_copy(
            src_ref=src, dst_ref=slots.at[rows_p], send_sem=out, recv_sem=sem.at[part, chip],
            device_id=target, device_id_type=MESH,
        )
        when(condition, copy.start)
        sends.append((condition, copy))

    me = place.chip()
    for part, kind in OWN_SENDS + tuple((part, 4) for part in range(G_PLAN.count)):
        push(None, part, me, kind, mine=True)
    keep = pltpu.make_async_copy(
        own, slots.at[pl.ds(pl.multiple_of((me * 2 + place.c) * own.shape[0], 128), own.shape[0])], lsem
    )
    keep.start()

    plan_captions(lengths, picks, start_s, sorted_s, bound_s, images)
    token = lax.broadcasted_iota(jnp.int32, (1, rows), 1)

    def locate(c, where_to):
        inside = (token >= start_s[c]) & (token < start_s[c] + lengths[0, c])
        return jnp.where(inside, token + (sorted_s[c] - start_s[c]), where_to)

    where_to = lax.fori_loop(0, captions, locate, token)
    place_o[...] = jnp.broadcast_to(where_to, place_o.shape)
    lane = lax.broadcasted_iota(jnp.int32, metas.shape, 1)

    def note(c, row):
        return jnp.where(lane == c, sorted_s[c], row)

    row = lax.fori_loop(0, captions, note, jnp.zeros(metas.shape, jnp.int32))
    for i in range(images + 1):
        row = jnp.where(lane == BOUND_LANE + i, bound_s[i], row)
    metas[...] = row

    def sort(out, array):
        def body(b, _):
            target = lax.broadcasted_iota(jnp.int32, (QB, rows), 0) + b * QB
            onehot = (target == place_o[0:1, :]).astype(F32).astype(BF)
            out[blk(b), :] = nn(onehot, array[...]).astype(BF)
            return 0

        lax.fori_loop(0, rows // QB, body, 0)

    sort(xs, tokens)
    swaps = []
    for i, (src, dst) in enumerate(((metas, meta_o), (xs, x_o))):
        swaps.append(
            pltpu.make_async_remote_copy(
                src_ref=src, dst_ref=dst, send_sem=xsem.at[0, i], recv_sem=xsem.at[1, i],
                device_id=place.neighbour(X_), device_id_type=MESH,
            )
        )
        swaps[-1].start()

    def encode(i):
        def body(j, _):
            at = pl.ds(pl.multiple_of(i * IMG_ROWS + j * 64, 64), 64)
            normed, _i = normalise(img[at, :].astype(F32))
            enc_o[at, :] = (normed * norms[3:4, :] + norms[7:8, :]).astype(BF)
            return 0

        lax.fori_loop(0, IMG_ROWS // 64, body, 0)

    steps = img.shape[0] // IMG_ROWS
    done = 0
    for number, (part, dt, dz, dy) in enumerate(G_PLAN.pieces):
        there = place.exists(dz)
        chip = place.chip(dt, dz, dy)

        def arrived(part=part, chip=chip):
            rows_p = G_PLAN.slot_rows(chip, place.c, part)
            pltpu.make_async_remote_copy(
                src_ref=slots.at[rows_p], dst_ref=slots.at[rows_p], send_sem=ssem.at[0, part, chip],
                recv_sem=rsem.at[part, chip], device_id=place.neighbour(X_), device_id_type=MESH,
            ).wait_recv()

        when(there, arrived)
        for kind in G_PLAN.routes(part, dt, dz, dy) + [4]:
            push(there, part, chip, kind)
        if number == 4:
            sort(cot_o, cot)
        if number >= 6 and done < steps:
            encode(done)
            done += 1
    for i in range(done, steps):
        encode(i)

    def from_sibling(chip, _):
        for part in range(G_PLAN.count):
            rows_p = G_PLAN.slot_rows(chip, 1 - place.c, part)
            pltpu.make_async_remote_copy(
                src_ref=slots.at[rows_p], dst_ref=slots.at[rows_p], send_sem=sibsem.at[part, chip],
                recv_sem=sibrecv.at[part, chip], device_id=place.sibling(), device_id_type=MESH,
            ).wait_recv()
        return 0

    lax.fori_loop(0, 4 * Z_CHIPS, from_sibling, 0)
    for condition, copy in sends:
        when(condition, copy.wait_send)
    for swap in swaps:
        swap.wait()
    keep.wait()


IMG_ROWS = 192
ENC_ROWS = 192


def run_gather(images, lengths, picks, tokens, cot, img, master, norms, total_rows):
    rows = tokens.shape[0]
    dma = pltpu.SemaphoreType.DMA
    low = jax.ShapeDtypeStruct((rows, D), BF)
    return pl.pallas_call(
        functools.partial(gather_kernel, images),
        out_shape=(
            jax.ShapeDtypeStruct((total_rows, D), BF),
            low,
            jax.ShapeDtypeStruct((8, 128), jnp.int32),
            low,
            jax.ShapeDtypeStruct(img.shape, BF),
            jax.ShapeDtypeStruct((8, rows), jnp.int32),
        ),
        in_specs=[SM, SM, VM, VM, VM, VM, VM],
        out_specs=(ANY, ANY, ANY, VM, VM, VM),
        scratch_shapes=[
            pltpu.VMEM(master.shape, BF),
            pltpu.VMEM((rows, D), BF),
            pltpu.VMEM((8, 128), jnp.int32),
            pltpu.SMEM((lengths.shape[1],), jnp.int32),
            pltpu.SMEM((lengths.shape[1],), jnp.int32),
            pltpu.SMEM((images + 1,), jnp.int32),
            dma((4, G_PLAN.count, 16)),
            dma((G_PLAN.count, 16)),
            dma((G_PLAN.count, 16)),
            dma((G_PLAN.count, 16)),
            dma((2, 2)),
            dma,
        ],
        compiler_params=pltpu.CompilerParams(
            vmem_limit_bytes=VLIM, has_side_effects=True, collective_id=0
        ),
    )(lengths, picks, tokens, cot, img, master, norms)


def sum_kernel(
    grads, norm_terms, place_row, gt, out_back, dk_h, dv_h, w_h, img_h, norms,
    red_o, norm_o, gt_o, lay_o, gi_h,
    out_b, obsem, wkv, ebuf, obuf, ng, esem, osem, wksem, acc, sib, gtr, nbuf, nrecv,
    lsem, sibsem, sibrecv, ssem, rsem, gsem, nsend, nrs, *land,
):
    place = Place()
    rows = gt.shape[0]
    greet(place, True)
    order = S_PLAN.pieces + [(part, 0, 0, 0) for part in range(S_PLAN.count)]
    sends = []

    def local(part, chip):
        off = pl.ds(S_PLAN.off[part], S_PLAN.rows[part])
        return pltpu.make_async_copy(
            grads.at[S_PLAN.slot_rows(chip, place.c, part)], acc.at[chip, off], lsem.at[part, chip]
        )

    def across(part, chip):
        off = pl.ds(S_PLAN.off[part], S_PLAN.rows[part])
        return pltpu.make_async_remote_copy(
            src_ref=grads.at[S_PLAN.slot_rows(chip, 1 - place.c, part)], dst_ref=sib.at[chip, off],
            send_sem=sibsem.at[part, chip], recv_sem=sibrecv.at[part, chip],
            device_id=place.sibling(), device_id_type=MESH,
        )

    for part, dt, dz, dy in order:
        chip = place.chip(dt, dz, dy)

        def begin(part=part, chip=chip):
            across(part, chip).start()
            local(part, chip).start()

        when(place.exists(dz), begin)
    back = pltpu.make_async_remote_copy(
        src_ref=gt, dst_ref=gtr, send_sem=gsem.at[0], recv_sem=gsem.at[1],
        device_id=place.neighbour(X_), device_id_type=MESH,
    )

    def landing(part, kind, chip):
        at = {"x": chip // 8, "z": (chip // 2) % Z_CHIPS, "y": chip % 2}
        spot = 0
        for name in S_PLAN.landing_spots(part, kind)[0]:
            spot = spot * DIMS[name] + at[name]
        return land[part * 4 + kind].at[spot]

    def flow(part, kind, chip):
        off = pl.ds(S_PLAN.off[part], S_PLAN.rows[part])
        return pltpu.make_async_remote_copy(
            src_ref=acc.at[chip, off], dst_ref=landing(part, kind, chip),
            send_sem=ssem.at[part, chip], recv_sem=rsem.at[kind, part, chip],
            device_id=place.neighbour(kind), device_id_type=MESH,
        )

    def add(part, chip, other, final):
        def body(i, _):
            at = pl.ds(pl.multiple_of(S_PLAN.off[part] + i * 32, 32), 32)
            value = acc[chip, at, :].astype(F32)
            for ref in other:
                value = value + ref(part, pl.ds(pl.multiple_of(i * 32, 32), 32), at).astype(F32)
            if final:
                red_o[at, :] = value
            else:
                acc[chip, at, :] = value.astype(BF)
            return 0

        lax.fori_loop(0, S_PLAN.rows[part] // 32, body, 0)

    def norm_round(i, target):
        return pltpu.make_async_remote_copy(
            src_ref=nbuf.at[i], dst_ref=nrecv.at[i], send_sem=nsend.at[i], recv_sem=nrs.at[i],
            device_id=target, device_id_type=MESH,
        )

    def norm_line(k, target):
        return pltpu.make_async_remote_copy(
            src_ref=nbuf.at[3], dst_ref=nrecv.at[3 + place.z], send_sem=nsend.at[3 + k],
            recv_sem=nrs.at[3 + place.z], device_id=target, device_id_type=MESH,
        )

    def norm_from(z):
        return pltpu.make_async_remote_copy(
            src_ref=nbuf.at[3], dst_ref=nrecv.at[3 + z], send_sem=nsend.at[3], recv_sem=nrs.at[3 + z],
            device_id=place.neighbour(X_), device_id_type=MESH,
        )

    line = [norm_line(k, target) for k, target in enumerate(place.line())]
    rounds = [place.sibling(), place.neighbour(X_), place.neighbour(Y_)]
    keys = pltpu.make_async_copy(w_h, wkv, wksem)
    keys.start()
    out_copy = pltpu.make_async_copy(out_back, out_b, obsem)
    out_copy.start()
    steps = dk_h.shape[0] // ENC_ROWS
    ng[...] = jnp.zeros_like(ng)

    def fetch(i):
        at = pl.ds(i * ENC_ROWS, ENC_ROWS)
        return [
            pltpu.make_async_copy(ref.at[at], ebuf.at[j, i % 2], esem.at[j, i % 2])
            for j, ref in enumerate((dk_h, dv_h, img_h))
        ]

    def put(i):
        at = pl.ds(i * ENC_ROWS, ENC_ROWS)
        return [pltpu.make_async_copy(obuf.at[i % 2], gi_h.at[at], osem.at[i % 2])]

    def encoder_back(i):
        wait(fetch(i))
        if i >= 2:
            wait(put(i - 2))
        out = obuf.at[i % 2]
        out[...] = nt(ebuf[0, i % 2], wkv[0]) + nt(ebuf[1, i % 2], wkv[1])

        def body(j, _):
            normed, inv_std = normalise(ebuf[2, i % 2, blk(j, 64), :].astype(F32))
            grad = out[blk(j, 64), :].astype(BF).astype(F32)
            ng[0:1, :] += jnp.sum(grad * normed, axis=0, keepdims=True)
            ng[1:2, :] += jnp.sum(grad, axis=0, keepdims=True)
            out[blk(j, 64), :] = norm_back(grad, normed, inv_std, norms[3:4, :])
            return 0

        lax.fori_loop(0, ENC_ROWS // 64, body, 0)
        start(put(i))
        if i + 2 < steps:
            start(fetch(i + 2))

    start(fetch(0))
    start(fetch(1))

    def unsort(out, array):
        def body(b, _):
            target = lax.broadcasted_iota(jnp.int32, (rows, QB), 0)
            onehot = (target == place_row[0:1, blk(b)]).astype(F32).astype(BF)
            out[blk(b), :] = tn(onehot, array[...]).astype(out.dtype)
            return 0

        lax.fori_loop(0, rows // QB, body, 0)

    span = len(order) // 2 - 4
    enc_at = [2 + i * span // steps for i in range(steps)]
    norm_at = [span + 3 + (i * len(order)) // 14 for i in range(4)]
    for number, (part, dt, dz, dy) in enumerate(order):
        chip = place.chip(dt, dz, dy)
        if number == GT_AT:
            back.start()
        there = place.exists(dz)
        final = (dt, dz, dy) == (0, 0, 0)
        kinds = S_PLAN.routes(part, dt, dz, dy)

        def step(part=part, chip=chip, kinds=kinds, final=final, dt=dt, dz=dz, dy=dy):
            local(part, chip).wait()
            across(part, chip).wait_recv()
            refs = [lambda p, i, at: sib[chip, at, :]]
            fixed = [kind for kind in kinds if kind in (X_, Y_)]
            edge = [kind for kind in kinds if kind in (UP_, DN_)]
            for kind in fixed:
                flow(part, OPPOSITE[kind], chip).wait_recv()
                refs.append(
                    lambda p, i, at, kind=kind: landing(part, OPPOSITE[kind], chip)[i, :]
                )
            for kind in edge:

                def one(kind=kind):
                    flow(part, OPPOSITE[kind], chip).wait_recv()
                    add(part, chip, [lambda p, i, at: landing(part, OPPOSITE[kind], chip)[i, :]], False)

                pl.when(place.has(kind))(one)
            add(part, chip, refs, final)
            if not final:
                flow(part, S_PLAN.source(part, dt, dz, dy), chip).start()

        when(there, step)
        if not final:
            sends.append((there, part, chip, S_PLAN.source(part, dt, dz, dy)))
        if number in enc_at:
            if number == enc_at[0]:
                keys.wait()
            encoder_back(enc_at.index(number))
        if number == norm_at[0]:
            nbuf[0] = norm_terms[...]
            nbuf[0, 3:4, :] = ng[0:1, :]
            nbuf[0, 7:8, :] = ng[1:2, :]
            norm_round(0, rounds[0]).start()
        if number in norm_at[1:]:
            i = norm_at.index(number) - 1
            norm_round(i, rounds[i]).wait()
            nbuf[i + 1] = nbuf[i] + nrecv[i]
            if i < 2:
                norm_round(i + 1, rounds[i + 1]).start()
            else:
                for copy in line:
                    copy.start()
        if number == norm_at[0] + 1:
            out_copy.wait()
            unsort(lay_o, out_b)
        if number == norm_at[3] + 1:
            back.wait()
            unsort(gt_o, gtr)

    for z in range(Z_CHIPS):

        @pl.when(place.z != z)
        def _(z=z):
            norm_from(z).wait_recv()

        @pl.when(place.z == z)
        def _(z=z):
            nrecv[3 + z] = nbuf[3]

    wait(put(steps - 2) + put(steps - 1))
    norm_o[...] = (nrecv[3] + nrecv[4]) + (nrecv[5] + nrecv[6])
    for copy in line:
        copy.wait_send()
    for there, part, chip, kind in sends:
        when(there, flow(part, kind, chip).wait_send)

    def sent(chip, _):
        for part in range(S_PLAN.count):
            across(part, chip).wait_send()
        return 0

    lax.fori_loop(0, 4 * Z_CHIPS, sent, 0)


def run_sum(grads, norm_terms, place_row, gt, out_back, dk, dv, kv_weights, img, norms):
    rows = gt.shape[0]
    dma = pltpu.SemaphoreType.DMA
    shard = S_PLAN.shard
    line = 4 * Z_CHIPS
    return pl.pallas_call(
        sum_kernel,
        out_shape=(
            jax.ShapeDtypeStruct((shard, D), F32),
            jax.ShapeDtypeStruct((8, D), F32),
            jax.ShapeDtypeStruct((rows, D), F32),
            jax.ShapeDtypeStruct((rows, D), BF),
            jax.ShapeDtypeStruct(img.shape, F32),
        ),
        in_specs=[ANY, VM, VM, ANY, ANY, ANY, ANY, ANY, ANY, VM],
        out_specs=(VM,) * 4 + (ANY,),
        scratch_shapes=[
            pltpu.VMEM((rows, D), BF),
            dma,
            pltpu.VMEM((2, D, D), BF),
            pltpu.VMEM((3, 2, ENC_ROWS, D), BF),
            pltpu.VMEM((2, ENC_ROWS, D), F32),
            pltpu.VMEM((8, D), F32),
            dma((3, 2)),
            dma((2,)),
            dma,
            pltpu.VMEM((line, shard, D), BF),
            pltpu.VMEM((line, shard, D), BF),
            pltpu.VMEM((rows, D), BF),
            pltpu.VMEM((4, 8, D), F32),
            pltpu.VMEM((7, 8, D), F32),
            dma((S_PLAN.count, line)),
            dma((S_PLAN.count, line)),
            dma((S_PLAN.count, line)),
            dma((S_PLAN.count, line)),
            dma((4, S_PLAN.count, line)),
            dma((2,)),
            dma((7,)),
            dma((7,)),
        ]
        + [
            pltpu.VMEM((S_PLAN.landing_spots(part, kind)[1], S_PLAN.rows[part], D), BF)
            for part in range(S_PLAN.count)
            for kind in range(4)
        ],
        compiler_params=pltpu.CompilerParams(
            vmem_limit_bytes=VLIM, has_side_effects=True, collective_id=1
        ),
    )(grads, norm_terms, place_row, gt, out_back, dk, dv, kv_weights, img, norms)


def from_partner(block, axis):
    half = lax.axis_size(axis) // 2
    count = lax.axis_size(axis)
    return lax.ppermute(block, axis, [(i, (i + half) % count) for i in range(count)])


def adamw_update(weight, moment, second, grad_in, rate, decay_rate):
    new_moment = beta_one * moment + (1.0 - beta_one) * grad_in
    new_second = beta_two * second + (1.0 - beta_two) * grad_in * grad_in
    moment_hat = new_moment / (1.0 - beta_one**STEP)
    second_hat = new_second / (1.0 - beta_two**STEP)
    new_weight = weight - rate * (
        moment_hat / (jnp.sqrt(second_hat) + epsilon) + decay_rate * weight
    )
    return (new_weight, new_moment, new_second)


def caption_plan(lengths, picks, rows, images):
    ends = jnp.cumsum(lengths)
    starts = ends - lengths
    rank = picks * lengths.shape[0] + jnp.arange(lengths.shape[0], dtype=jnp.int32)
    ahead = rank[None, :] < rank[:, None]
    sorted_starts = jnp.sum(jnp.where(ahead, lengths[None, :], 0), axis=1)
    token = jnp.arange(rows, dtype=jnp.int32)
    inside = (token[:, None] >= starts[None, :]) & (token[:, None] < ends[None, :])
    place = token + jnp.sum(jnp.where(inside, (sorted_starts - starts)[None, :], 0), axis=1)
    edges = jnp.arange(images + 1, dtype=jnp.int32)
    bounds = jnp.sum(jnp.where(picks[None, :] < edges[:, None], lengths[None, :], 0), axis=1)
    return place, sorted_starts, bounds


def per_device(
    kernels,
    tokens,
    cotangent,
    caption_lengths,
    image_index,
    image_states,
    master_weights,
    first_moments,
    second_moments,
    owner_list,
    norm_params,
    norm_first,
    norm_second,
):
    rows = tokens.shape[0]
    groups = owner_list.shape[0]
    total_rows = 8 * D + 2 * FF
    group_rows = total_rows // groups
    images = image_states.shape[0]
    captions = caption_lengths.shape[1]
    axes = ("tower", "dp")
    direct = group_rows == GROUP
    ids = jnp.arange(groups, dtype=jnp.int32)
    inverse = jnp.sum(jnp.where(owner_list[None, :] == ids[:, None], ids[None, :], 0), axis=1)
    img = image_states.reshape(-1, D)
    if kernels:
        gathered, x, meta, sent_cot, enc, place_row = run_gather(
            images, caption_lengths, image_index, tokens, cotangent, img, master_weights,
            norm_params, total_rows,
        )
    else:
        gathered = lax.all_gather(master_weights.astype(BF), axes, axis=0, tiled=True)
        place, starts, bounds = caption_plan(caption_lengths[0], image_index[0], rows, images)
        into = (place[None, :] == jnp.arange(rows, dtype=jnp.int32)[:, None]).astype(BF)
        meta = jnp.zeros((8, 128), jnp.int32)
        meta = meta.at[0, :captions].set(starts)
        meta = meta.at[0, BOUND_LANE : BOUND_LANE + images + 1].set(bounds)
        meta = from_partner(meta, "tower")
        x = from_partner(nn(into, tokens).astype(BF), "tower")
        sent_cot = nn(into, cotangent).astype(BF)
        normed, _i = normalise(img.astype(F32))
        enc = (normed * norm_params[3] + norm_params[7]).astype(BF)
    if direct:
        slots = gathered.reshape(groups, GROUP, D)
        inv = inverse
    else:
        slots = gathered.reshape(groups, group_rows, D)[inverse].reshape(-1, GROUP, D)
        inv = jnp.arange(total_rows // GROUP, dtype=jnp.int32)
    cot = from_partner(sent_cot, "tower")
    *kept, kv_weights, r2 = run_attention_forward(
        captions, images, inv, meta, x, enc, norm_params, slots
    )
    out, g2, ng3, grads = run_feed_forward(inv, r2, cot, norm_params, slots)
    out_back = from_partner(out, "tower")
    gt, norm_terms, dk, dv, grads = run_attention_backward(
        captions, images, inv, meta, g2, x, kept, enc, norm_params, slots, grads, ng3
    )
    if kernels:
        reduced, norm_grads, grad_tokens, layer_out, grad_images = run_sum(
            grads.reshape(total_rows, D), norm_terms, place_row, gt, out_back, dk, dv, kv_weights,
            img, norm_params,
        )
    else:
        layer_out = tn(into, out_back).astype(BF)
        grad_tokens = tn(into, from_partner(gt, "tower"))
        grad_enc = (nt(dk, kv_weights[0]) + nt(dv, kv_weights[1])).astype(BF).astype(F32)
        normed, inv_std = normalise(img.astype(F32))
        grad_images = norm_back(grad_enc, normed, inv_std, norm_params[3:4])
        norm_terms = norm_terms.at[3].set(jnp.sum(grad_enc * normed, axis=0))
        norm_terms = norm_terms.at[7].set(jnp.sum(grad_enc, axis=0))
        if direct:
            arranged = grads.reshape(total_rows, D)
        else:
            arranged = grads.reshape(groups, group_rows, D)[owner_list].reshape(total_rows, D)
        reduced = lax.psum_scatter(arranged, axes, scatter_dimension=0, tiled=True).astype(F32)
        norm_grads = lax.psum(norm_terms, axes)
    new_weights, new_first, new_second = adamw_update(
        master_weights, first_moments, second_moments, reduced, learn_rate, weight_decay
    )
    norm_new, norm_first_new, norm_second_new = adamw_update(
        norm_params, norm_first, norm_second, norm_grads, norm_rate, 0.0
    )
    return (
        layer_out,
        grad_tokens,
        grad_images.reshape(image_states.shape),
        new_weights,
        new_first,
        new_second,
        new_weights.astype(BF),
        norm_new,
        norm_first_new,
        norm_second_new,
    )


def solution(mesh):
    split = P(("tower", "dp"), None)
    wide = P(("tower", "dp"), None, None)
    in_specs = (split,) * 4 + (wide,) + (split,) * 3 + (P(),) * 4
    out_specs = (split, split, wide) + (split,) * 4 + (P(),) * 3
    shape = dict(mesh.shape)
    kernels = shape["tower"] == 2 and shape["dp"] == 4 * Z_CHIPS
    return jax.shard_map(
        functools.partial(per_device, kernels),
        mesh=mesh,
        in_specs=in_specs,
        out_specs=out_specs,
        check_vma=False,
    )
```

```python
import functools

import jax
import jax.numpy as jnp
from jax import lax
from jax.experimental import pallas as pl
from jax.experimental.pallas import tpu as pltpu
from jax.sharding import PartitionSpec as P

D = 768
HEADS = 12
HDIM = 64
FF = 3072
STEP = 5
PAIRS = HEADS // 2
LANES = 2 * HDIM
QB = 128
HEAD_ROWS = 16
PAIR_GROUPS = ((0, 1, 2), (3, 4, 5))
GROUP = 192
BOUND_LANE = 64
PER = D // GROUP
SCALE = HDIM ** (-0.5)

beta_one = 0.5
beta_two = 0.6
learn_rate = 0.03
norm_rate = 0.4
weight_decay = 0.01
epsilon = 1e-08
norm_eps = 1e-05
masked_score = -1000000000.0

W_Q, W_K, W_V, W_O, C_Q, C_K, C_V, C_O, UP, DOWN = 0, 1, 2, 3, 4, 5, 6, 7, 8, 12

BF = jnp.bfloat16
F32 = jnp.float32
VM = pl.BlockSpec(memory_space=pltpu.VMEM)
SM = pl.BlockSpec(memory_space=pltpu.SMEM)
ANY = pl.BlockSpec(memory_space=pl.ANY)
VLIM = 58 * 2**20


def nn(a, b):
    return lax.dot_general(a, b, (((1,), (0,)), ((), ())), preferred_element_type=F32)


def nt(a, b):
    return lax.dot_general(a, b, (((1,), (1,)), ((), ())), preferred_element_type=F32)


def tn(a, b):
    return lax.dot_general(a, b, (((0,), (0,)), ((), ())), preferred_element_type=F32)


def blk(i, size=QB):
    return pl.ds(pl.multiple_of(i * size, size), size)


def lanes(p):
    return slice(p * LANES, (p + 1) * LANES)


def normalise(x):
    centred = x - jnp.mean(x, axis=-1, keepdims=True)
    inv = lax.rsqrt(jnp.mean(centred * centred, axis=-1, keepdims=True) + norm_eps)
    return centred * inv, inv


def norm_back(grad, normed, inv, gain):
    gn = grad * gain
    m1 = jnp.mean(gn, axis=-1, keepdims=True)
    m2 = jnp.mean(gn * normed, axis=-1, keepdims=True)
    return inv * (gn - m1 - normed * m2)


def head_masks():
    low = (lax.broadcasted_iota(jnp.int32, (1, LANES), 1) < HDIM).astype(F32)
    return low.astype(BF), (1.0 - low).astype(BF)


def two_heads(x, masks):
    return jnp.concatenate([x * masks[0], x * masks[1]], axis=0)


def merge_heads(both):
    return jnp.concatenate([both[:HDIM, :QB], both[HDIM:, QB:]], axis=0)


def weight_copies(slots, inv, buf, sem, matrix, slot):
    return [
        pltpu.make_async_copy(
            slots.at[inv[matrix * PER + j]], buf.at[slot, pl.ds(j * GROUP, GROUP)], sem.at[slot, j]
        )
        for j in range(PER)
    ]


def grad_copies(grads, inv, buf, sem, matrix, slot):
    return [
        pltpu.make_async_copy(
            buf.at[slot, pl.ds(j * GROUP, GROUP)], grads.at[inv[matrix * PER + j]], sem.at[slot, j]
        )
        for j in range(PER)
    ]


def start(copies):
    for copy in copies:
        copy.start()


def wait(copies):
    for copy in copies:
        copy.wait()


def causal_mask(meta, captions, b):
    query = lax.broadcasted_iota(jnp.int32, (1, QB), 1) + b * QB
    first = jnp.zeros((1, QB), jnp.int32)
    for c in range(captions):
        first = jnp.maximum(first, jnp.where(query >= meta[0, c], meta[0, c], 0))
    key = lax.broadcasted_iota(jnp.int32, (2 * QB, QB), 0) + (b - 1) * QB
    allowed = (key >= first) & (key <= query)
    return jnp.concatenate([allowed, allowed], axis=1)


def column_softmax(scores):
    top = jnp.max(scores, axis=0, keepdims=True)
    exponent = jnp.exp(scores - top)
    total = jnp.sum(exponent, axis=0, keepdims=True)
    return exponent, 1.0 / total, top + jnp.log(total)


def head_products(grad, out):
    prod = grad.astype(F32) * out
    high = prod.astype(BF)
    low = (prod - high.astype(F32)).astype(BF)
    head = lax.broadcasted_iota(jnp.int32, (HEAD_ROWS, D), 0)
    lane = lax.broadcasted_iota(jnp.int32, (HEAD_ROWS, D), 1)
    pick = ((lane >= head * HDIM) & (lane < (head + 1) * HDIM)).astype(F32).astype(BF)
    return nt(pick, high) + nt(pick, low)


def pair_row(table, p):
    return jnp.concatenate([table[2 * p : 2 * p + 1], table[2 * p + 1 : 2 * p + 2]], axis=1)


def call(body, out_shape, in_specs, out_specs, scratch, aliases=None, effects=False):
    return pl.pallas_call(
        body,
        out_shape=out_shape,
        in_specs=in_specs,
        out_specs=out_specs,
        scratch_shapes=scratch,
        input_output_aliases=aliases or {},
        compiler_params=pltpu.CompilerParams(vmem_limit_bytes=VLIM, has_side_effects=effects),
    )


def image_blocks(meta, i):
    low, high = meta[0, BOUND_LANE + i], meta[0, BOUND_LANE + i + 1]
    first = low // QB
    last = jnp.where(high > low, (high + QB - 1) // QB, first)
    return low, high, first, last


def blk_of(i, size):
    return pl.ds(pl.multiple_of(i * size, 64), size)


def attention_forward(
    captions, images, inv, meta, x, enc_h, norms, slots,
    q_h, k_h, v_h, att_h, r1_h, cq_h, kk_h, vv_h, cross_h, atf_h, crf_h, fst_h, snd_h, slse_o, clse_o, w_h, r2_o,
    wbuf, low, second, q, kpad, vpad, att, atf, r1, cq, enc, kv, cross, acc, wsem, esem, osem,
):
    rows = x.shape[0]
    patches = enc.shape[0] // images
    loads = [weight_copies(slots, inv, wbuf, wsem, m, m) for m in range(8)]
    for load in loads[:3]:
        start(load)
    enc_copy = pltpu.make_async_copy(enc_h, enc, esem)
    enc_copy.start()
    for m in (C_K, C_V, W_O, C_Q, C_O):
        start(loads[m])
    masks = head_masks()
    kk, vv = kv.at[0], kv.at[1]
    pieces = enc.shape[0] // D
    copies = []

    def store(i, vmem, hbm):
        copies.append(pltpu.make_async_copy(vmem, hbm, osem.at[i]))
        copies[-1].start()

    def norm_one(i, _):
        normed, _i = normalise(x[blk(i), :].astype(F32))
        low[blk(i), :] = (normed * norms[0:1, :] + norms[4:5, :]).astype(BF)
        return 0

    lax.fori_loop(0, rows // QB, norm_one, 0, unroll=True)
    store(12, low, fst_h)
    kpad[pl.ds(0, QB), :] = jnp.zeros((QB, D), BF)
    vpad[pl.ds(0, QB), :] = jnp.zeros((QB, D), BF)
    wait(loads[W_Q])
    q[...] = (nn(low[...], wbuf[W_Q]) * SCALE).astype(BF)
    store(0, q, q_h)
    wait(loads[W_K])
    kpad[pl.ds(QB, rows), :] = nn(low[...], wbuf[W_K]).astype(BF)
    store(1, kpad.at[pl.ds(QB, rows)], k_h)
    wait(loads[W_V])
    vpad[pl.ds(QB, rows), :] = nn(low[...], wbuf[W_V]).astype(BF)
    store(2, vpad.at[pl.ds(QB, rows)], v_h)
    enc_copy.wait()
    wait(loads[C_K])
    wait(loads[C_V])
    store(3, wbuf.at[pl.ds(C_K, 2)], w_h)

    def attend(b, _):
        allowed = causal_mask(meta, captions, b)
        span = pl.ds(pl.multiple_of(b * QB, QB), 2 * QB)
        scores = [
            nt(kpad[span, lanes(p)], two_heads(q[blk(b), lanes(p)], masks)) for p in range(PAIRS)
        ]
        piece = blk(b % pieces, D)
        kv[b // pieces, piece, :] = nn(enc[piece, :], wbuf[C_K + b // pieces]).astype(BF)
        soft = [column_softmax(jnp.where(allowed, score, masked_score)) for score in scores]
        for p in range(PAIRS):
            exponent, scale, lse = soft[p]
            out = merge_heads(tn(vpad[span, lanes(p)], exponent.astype(BF)) * scale).T
            atf[blk(b), lanes(p)] = out
            att[blk(b), lanes(p)] = out.astype(BF)
            slse_o[b, p : p + 1, :] = lse
        return 0

    assert rows // QB == 2 * pieces
    lax.fori_loop(0, rows // QB, attend, 0)
    store(4, att, att_h)
    store(10, atf, atf_h)

    store(5, kk, kk_h)
    store(6, vv, vv_h)
    wait(loads[W_O])
    r1[...] = x[...].astype(F32) + nn(att[...], wbuf[W_O])
    store(7, r1, r1_h)

    def norm_two(i, _):
        normed, _i = normalise(r1[blk(i), :])
        second[blk(i), :] = (normed * norms[1:2, :] + norms[5:6, :]).astype(BF)
        return 0

    lax.fori_loop(0, rows // QB, norm_two, 0, unroll=True)
    store(13, second, snd_h)
    wait(loads[C_Q])
    cq[...] = (nn(second[...], wbuf[C_Q]) * SCALE).astype(BF)
    store(8, cq, cq_h)
    acc[...] = jnp.zeros_like(acc)
    clse_o[...] = jnp.zeros_like(clse_o)

    def image(i, _):
        first_row, end_row, first, last = image_blocks(meta, i)

        def attend_image(b, _):
            token = lax.broadcasted_iota(jnp.int32, (1, QB), 1) + b * QB
            here = ((token >= first_row) & (token < end_row)).astype(F32)
            here = jnp.concatenate([here, here], axis=1)
            at = blk_of(i, patches)
            scores = [
                nt(kk[at, lanes(p)], two_heads(cq[blk(b), lanes(p)], masks)) for p in range(PAIRS)
            ]
            soft = [column_softmax(score) for score in scores]
            for p in range(PAIRS):
                exponent, scale, lse = soft[p]
                clse_o[b, p : p + 1, :] = jnp.where(here > 0, lse, clse_o[b, p : p + 1, :])
                out = tn(vv[at, lanes(p)], exponent.astype(BF)) * (scale * here)
                acc[blk(b), lanes(p)] += merge_heads(out).T
            return 0

        lax.fori_loop(first, last, attend_image, 0)
        return 0

    lax.fori_loop(0, images, image, 0)
    cross[...] = acc[...].astype(BF)
    store(9, cross, cross_h)
    store(11, acc, crf_h)
    wait(loads[C_O])
    r2_o[...] = r1[...] + nn(cross[...], wbuf[C_O])
    for copy in copies:
        copy.wait()


def run_attention_forward(captions, images, inv, meta, x, enc, norms, slots):
    rows = x.shape[0]
    one = jax.ShapeDtypeStruct((rows, D), BF)
    full = jax.ShapeDtypeStruct((rows, D), F32)
    kv = jax.ShapeDtypeStruct(enc.shape, BF)
    lse = jax.ShapeDtypeStruct((rows // QB, 8, 2 * QB), F32)
    low = pltpu.VMEM((rows, D), BF)
    pad = pltpu.VMEM((rows + QB, D), BF)
    big = pltpu.VMEM((rows, D), F32)
    wide = pltpu.VMEM(enc.shape, BF)
    return call(
        functools.partial(attention_forward, captions, images),
        (one, one, one, one, full, one, kv, kv, one, full, full, one, one, lse, lse)
        + (jax.ShapeDtypeStruct((2, D, D), BF), full),
        [SM, SM, VM, ANY, VM, ANY],
        (ANY,) * 13 + (VM, VM, ANY, VM),
        [
            pltpu.VMEM((8, D, D), BF), low, low, low, pad, pad, low, big, big, low, wide,
            pltpu.VMEM((2,) + enc.shape, BF), low, big, pltpu.SemaphoreType.DMA((8, PER)), pltpu.SemaphoreType.DMA,
            pltpu.SemaphoreType.DMA((14,)),
        ],
    )(inv, meta, x, enc, norms, slots)


GELU_A = 0.7978845608028654
GELU_B = GELU_A * 0.044715


def feed_forward(
    inv, r2, cot_h, norms, slots, out_o, g2_o, ng_o, grads,
    cot, csem, wup, wdown, third, pre, gh, hid, gpre, acc, gthird, gup, gdown, usem, dsem, gusem, gdsem,
):
    rows = r2.shape[0]
    chunks = FF // D

    def loads(c, slot):
        return weight_copies(slots, inv, wup, usem, UP + c, slot) + weight_copies(
            slots, inv, wdown, dsem, DOWN + c, slot
        )

    def stores(c, slot):
        return grad_copies(grads, inv, gup, gusem, UP + c, slot) + grad_copies(
            grads, inv, gdown, gdsem, DOWN + c, slot
        )

    start(loads(0, 0))
    cot_copy = pltpu.make_async_copy(cot_h, cot, csem)
    cot_copy.start()

    def norm_three(i, _):
        normed, _i = normalise(r2[blk(i), :])
        third[blk(i), :] = (normed * norms[2:3, :] + norms[6:7, :]).astype(BF)
        return 0

    lax.fori_loop(0, rows // QB, norm_three, 0, unroll=2)
    cot_copy.wait()
    acc[...] = r2[...]
    gthird[...] = jnp.zeros_like(gthird)

    def chunk(c, _):
        slot = c % 2

        @pl.when(c + 1 < chunks)
        def _():
            start(loads(c + 1, 1 - slot))

        wait(loads(c, slot))
        pre[...] = nt(third[...], wup[slot])
        gh[...] = nt(cot[...], wdown[slot])

        def gelu(i, _):
            x = pre[blk(i, 64), :]
            x2 = x * x
            t = jnp.tanh(x * (GELU_A + GELU_B * x2))
            half = 0.5 + 0.5 * t
            value = x * half
            hid[blk(i, 64), :] = value.astype(BF)
            slope = half + value * (1.0 - t) * (GELU_A + 3.0 * GELU_B * x2)
            gpre[blk(i, 64), :] = (gh[blk(i, 64), :] * slope).astype(BF)
            return 0

        lax.fori_loop(0, rows // 64, gelu, 0)

        @pl.when(c >= 2)
        def _():
            wait(stores(c - 2, slot))

        acc[...] += nn(hid[...], wdown[slot])
        gdown[slot] = tn(hid[...], cot[...]).astype(BF)
        gup[slot] = tn(gpre[...], third[...]).astype(BF)
        start(stores(c, slot))
        gthird[...] += nn(gpre[...], wup[slot])
        return 0

    lax.fori_loop(0, chunks, chunk, 0)
    out_o[...] = acc[...].astype(BF)
    ng_o[...] = jnp.zeros_like(ng_o)

    def back(i, _):
        normed, inv_std = normalise(r2[blk(i), :])
        grad = gthird[blk(i), :]
        ng_o[0:1, :] += jnp.sum(grad * normed, axis=0, keepdims=True)
        ng_o[1:2, :] += jnp.sum(grad, axis=0, keepdims=True)
        g2_o[blk(i), :] = cot[blk(i), :].astype(F32) + norm_back(
            grad, normed, inv_std, norms[2:3, :]
        )
        return 0

    lax.fori_loop(0, rows // QB, back, 0)
    for c in range(chunks - 2, chunks):
        wait(stores(c, c % 2))


def run_feed_forward(inv, r2, cot, norms, slots):
    rows = r2.shape[0]
    big = pltpu.VMEM((rows, D), F32)
    low = pltpu.VMEM((rows, D), BF)
    two = pltpu.VMEM((2, D, D), BF)
    sem = pltpu.SemaphoreType.DMA((2, PER))
    return call(
        feed_forward,
        (
            jax.ShapeDtypeStruct((rows, D), BF),
            jax.ShapeDtypeStruct((rows, D), F32),
            jax.ShapeDtypeStruct((2, D), F32),
            jax.ShapeDtypeStruct(slots.shape, BF),
        ),
        [SM, VM, ANY, VM, ANY],
        (VM, VM, VM, ANY),
        [low, pltpu.SemaphoreType.DMA, two, two, low, big, big, low, low, big, big, two, two, sem, sem, sem, sem],
    )(inv, r2, cot, norms, slots)


def attention_backward(
    captions, images,
    inv, meta, g2, x_h, q_h, k_h, v_h, att_h, r1_h, cq_h, kk_h, vv_h, cross, atf_h, crf_h, fst_h, snd_h,
    slse, clse, enc_h, norms, slots, grads_in, ng3,
    gt_o, ng_o, dk_h, dv_h, grads,
    wbuf, gbuf, x, q, kpad, vpad, att, r1, cq, kk, vv, enc, gca, dq, acck, accv, big, out32,
    low_n, delta, wsem, gsem, isem, osem,
):
    rows = g2.shape[0]
    patches = enc.shape[0] // images
    names = (C_O, C_Q, W_O, W_Q, W_K, W_V)
    loads = [weight_copies(slots, inv, wbuf, wsem, m, i) for i, m in enumerate(names)]
    body = pl.ds(QB, rows)
    inputs = [
        pltpu.make_async_copy(hbm, vmem, isem.at[i])
        for i, (hbm, vmem) in enumerate(
            (
                (crf_h, out32), (cq_h, cq), (kk_h, kk), (vv_h, vv), (enc_h, enc), (r1_h, r1),
                (snd_h, low_n), (att_h, att), (q_h, q), (k_h, kpad.at[body]),
                (v_h, vpad.at[body]), (x_h, x), (atf_h, out32), (fst_h, low_n),
            )
        )
    ]
    start(loads[0])
    start(inputs[:5])
    start(loads[1])
    start(inputs[5:12])
    for load in loads[2:]:
        start(load)

    def store(matrix, slot):
        copies = grad_copies(grads, inv, gbuf, gsem, matrix, slot)
        start(copies)
        return copies

    masks = head_masks()
    ng_o[...] = jnp.zeros_like(ng_o)
    ng_o[2:3, :] = ng3[0:1, :]
    ng_o[6:7, :] = ng3[1:2, :]
    low = dq
    low[...] = g2[...].astype(BF)
    gbuf[0] = tn(cross[...], low[...]).astype(BF)
    store_co = store(C_O, 0)
    wait(loads[0])
    gca[...] = nt(low[...], wbuf[0]).astype(BF)
    dq[...] = jnp.zeros_like(dq)
    wait(inputs[:4])

    def deltas(b, _):
        delta[b] = head_products(gca[blk(b), :], out32[blk(b), :])
        return 0

    lax.fori_loop(0, rows // QB, deltas, 0)
    start(inputs[12:13])

    def image(i, _):
        first_row, end_row, first, last = image_blocks(meta, i)
        ik = acck.at[pl.ds(0, patches)]
        iv = accv.at[pl.ds(0, patches)]
        ik[...] = jnp.zeros_like(ik)
        iv[...] = jnp.zeros_like(iv)

        def attend_image(b, _):
            token = lax.broadcasted_iota(jnp.int32, (QB, LANES), 0) + b * QB
            here = ((token >= first_row) & (token < end_row)).astype(F32).astype(BF)
            column = lax.broadcasted_iota(jnp.int32, (1, QB), 1) + b * QB
            inside = (column >= first_row) & (column < end_row)
            inside = jnp.concatenate([inside, inside], axis=1)
            at = blk_of(i, patches)
            table = delta[b]
            for group in PAIR_GROUPS:
                q2 = [two_heads(cq[blk(b), lanes(p)], masks) for p in group]
                go2 = [two_heads(gca[blk(b), lanes(p)] * here, masks) for p in group]
                scores = [nt(kk[at, lanes(p)], one) for p, one in zip(group, q2)]
                gps = [nt(vv[at, lanes(p)], go) for p, go in zip(group, go2)]
                probs = [
                    jnp.exp(score - jnp.where(inside, clse[b, p : p + 1, :], -masked_score))
                    for p, score in zip(group, scores)
                ]
                for p, prob, go in zip(group, probs, go2):
                    iv[:, lanes(p)] += nn(prob.astype(BF), go)
                gss = [
                    (prob * (gp - pair_row(table, p))).astype(BF)
                    for p, prob, gp in zip(group, probs, gps)
                ]
                for p, gs, one in zip(group, gss, q2):
                    ik[:, lanes(p)] += nn(gs, one)
                for p, gs in zip(group, gss):
                    gq = merge_heads(tn(kk[at, lanes(p)], gs)).T * SCALE
                    dq[blk(b), lanes(p)] += gq.astype(BF)
            return 0

        lax.fori_loop(first, last, attend_image, 0)
        kk[blk_of(i, patches), :] = ik[...].astype(BF)
        vv[blk_of(i, patches), :] = iv[...].astype(BF)
        return 0

    lax.fori_loop(0, images, image, 0)
    dk, dv = kk, vv
    out_k = pltpu.make_async_copy(dk, dk_h, osem.at[0])
    out_v = pltpu.make_async_copy(dv, dv_h, osem.at[1])
    start([out_k, out_v])
    wait(inputs[4:5])
    stores = []
    for slot, matrix, grad in ((1, C_K, dk), (2, C_V, dv)):
        gbuf[slot] = tn(enc[...], grad[...]).astype(BF)
        stores.append(store(matrix, slot))
    wait(inputs[5:7])
    gbuf[3] = tn(low_n[...], dq[...]).astype(BF)
    start(inputs[13:])
    stores.append(store(C_Q, 3))
    wait(loads[1])
    big[...] = nt(dq[...], wbuf[1])

    def back_two(i, _):
        normed, inv_std = normalise(r1[blk(i), :])
        grad = big[blk(i), :]
        ng_o[1:2, :] += jnp.sum(grad * normed, axis=0, keepdims=True)
        ng_o[5:6, :] += jnp.sum(grad, axis=0, keepdims=True)
        total = g2[blk(i), :] + norm_back(grad, normed, inv_std, norms[1:2, :])
        r1[blk(i), :] = total
        low[blk(i), :] = total.astype(BF)
        return 0

    lax.fori_loop(0, rows // QB, back_two, 0, unroll=True)
    g1 = r1
    wait(inputs[7:13])
    wait(store_co)
    gbuf[0] = tn(att[...], low[...]).astype(BF)
    stores.append(store(W_O, 0))
    wait(loads[2])
    gca[...] = nt(low[...], wbuf[2]).astype(BF)
    kpad[pl.ds(0, QB), :] = jnp.zeros((QB, D), BF)
    vpad[pl.ds(0, QB), :] = jnp.zeros((QB, D), BF)
    acck[...] = jnp.zeros_like(acck)
    accv[...] = jnp.zeros_like(accv)
    lax.fori_loop(0, rows // QB, deltas, 0)
    wait([out_k, out_v])

    def attend(b, _):
        allowed = causal_mask(meta, captions, b)
        span = pl.ds(pl.multiple_of(b * QB, QB), 2 * QB)
        group = range(PAIRS)
        q2 = [two_heads(q[blk(b), lanes(p)], masks) for p in group]
        go2 = [two_heads(gca[blk(b), lanes(p)], masks) for p in group]
        scores = [nt(kpad[span, lanes(p)], q2[p]) for p in group]
        gps = [nt(vpad[span, lanes(p)], go2[p]) for p in group]
        table = delta[b]
        probs = [
            jnp.where(allowed, jnp.exp(scores[p] - slse[b, p : p + 1, :]), 0.0) for p in group
        ]
        for p in group:
            accv[span, lanes(p)] += nn(probs[p].astype(BF), go2[p])
        gss = [(probs[p] * (gps[p] - pair_row(table, p))).astype(BF) for p in group]
        for p in group:
            acck[span, lanes(p)] += nn(gss[p], q2[p])
        for p in group:
            gq = merge_heads(tn(kpad[span, lanes(p)], gss[p])).T * SCALE
            dq[blk(b), lanes(p)] = gq.astype(BF)
        return 0

    lax.fori_loop(0, rows // QB, attend, 0)
    sk, sv = dk.at[pl.ds(0, rows)], dv.at[pl.ds(0, rows)]
    sk[...] = acck[body, :].astype(BF)
    sv[...] = accv[body, :].astype(BF)

    for done in stores[:3]:
        wait(done)
    wait(inputs[13:])
    for slot, matrix, grad in ((1, W_Q, dq), (2, W_K, sk), (3, W_V, sv)):
        gbuf[slot] = tn(low_n[...], grad[...]).astype(BF)
        stores.append(store(matrix, slot))
    for load in loads[3:]:
        wait(load)
    big[...] = nt(dq[...], wbuf[3]) + nt(sk[...], wbuf[4]) + nt(sv[...], wbuf[5])

    def back_one(i, _):
        normed, inv_std = normalise(x[blk(i), :].astype(F32))
        grad = big[blk(i), :]
        ng_o[0:1, :] += jnp.sum(grad * normed, axis=0, keepdims=True)
        ng_o[4:5, :] += jnp.sum(grad, axis=0, keepdims=True)
        gt_o[blk(i), :] = (g1[blk(i), :] + norm_back(grad, normed, inv_std, norms[0:1, :])).astype(
            BF
        )
        return 0

    lax.fori_loop(0, rows // QB, back_one, 0, unroll=True)
    for done in stores[3:]:
        wait(done)


def run_attention_backward(captions, images, inv, meta, g2, x, kept, enc, norms, slots, grads, ng3):
    rows = g2.shape[0]
    low = pltpu.VMEM((rows, D), BF)
    pad = pltpu.VMEM((rows + QB, D), BF)
    padf = pltpu.VMEM((rows + QB, D), F32)
    big = pltpu.VMEM((rows, D), F32)
    wide = pltpu.VMEM(enc.shape, BF)
    kv = jax.ShapeDtypeStruct(enc.shape, BF)
    dma = pltpu.SemaphoreType.DMA
    return call(
        functools.partial(attention_backward, captions, images),
        (
            jax.ShapeDtypeStruct((rows, D), BF),
            jax.ShapeDtypeStruct((8, D), F32),
            kv,
            kv,
            jax.ShapeDtypeStruct(slots.shape, BF),
        ),
        [SM, SM, VM] + [ANY] * 9 + [VM, ANY, ANY, ANY, ANY, VM, VM, ANY, VM, ANY, ANY, VM],
        (VM, VM, ANY, ANY, ANY),
        [
            pltpu.VMEM((6, D, D), BF), pltpu.VMEM((4, D, D), BF), low, low, pad, pad, low, big, low,
            wide, wide, wide, low, low, padf, padf, big, big, low,
            pltpu.VMEM((rows // QB, HEAD_ROWS, QB), F32),
            dma((6, PER)), dma((4, PER)), dma((14,)), dma((2,)),
        ],
        aliases={22: 4},
    )(inv, meta, g2, x, *kept, enc, norms, slots, grads, ng3)


MESH = pl.DeviceIdType.MESH
X_, Y_, UP_, DN_ = 0, 1, 2, 3
OPPOSITE = (X_, Y_, DN_, UP_)
Z_CHIPS = 4
DIMS = {"x": 2, "y": 2, "z": Z_CHIPS}


class Plan:
    def __init__(self, parts, arrivals):
        self.rows = [rows for rows, _ in parts]
        self.order = [order for _, order in parts]
        self.off = [sum(self.rows[:i]) for i in range(len(parts))]
        self.count = len(parts)
        self.shard = sum(self.rows)
        self.pieces = [
            (part, dt, step, dy)
            for part, dt, dz, dy in arrivals
            for step in ((-dz, dz) if dz else (0,))
        ]

    def last_axis(self, part, dt, dz, dy):
        moved = {"x": dt, "y": dy, "z": dz}
        return max((i for i, axis in enumerate(self.order[part]) if moved[axis]), default=-1)

    def routes(self, part, dt, dz, dy):
        order = self.order[part]
        last = self.last_axis(part, dt, dz, dy)
        kinds = []
        if last >= 0 and order[last] == "z":
            kinds.append(UP_ if dz < 0 else DN_)
        for axis in order[last + 1 :]:
            kinds += {"x": [X_], "y": [Y_], "z": [UP_, DN_]}[axis]
        return kinds

    def source(self, part, dt, dz, dy):
        axis = self.order[part][self.last_axis(part, dt, dz, dy)]
        return {"x": X_, "y": Y_, "z": UP_ if dz > 0 else DN_}[axis]

    def landing_spots(self, part, kind):
        axis = "xyzz"[kind]
        ahead = self.order[part]
        ahead = ahead[: ahead.index(axis)] + ("z" if axis == "z" else "")
        spots = 1
        for name in ahead:
            spots *= DIMS[name]
        return ahead, spots

    def slot_rows(self, chip, core, part):
        first = (chip * 2 + core) * self.shard + self.off[part]
        return pl.ds(pl.multiple_of(first, 32), self.rows[part])


G_PLAN = Plan(
    ((64, "xyz"), (64, "zxy"), (128, "zyx"), (128, "xzy")),
    (
        (0, 0, 1, 0), (3, 1, 0, 0), (2, 0, 0, 1), (0, 1, 0, 0), (1, 0, 0, 1), (1, 0, 1, 0),
        (0, 0, 0, 1), (3, 0, 1, 0), (2, 0, 1, 0), (2, 1, 0, 0), (1, 1, 0, 0), (3, 0, 0, 1),
        (0, 0, 2, 0), (3, 1, 1, 0), (3, 1, 0, 1), (0, 1, 1, 0), (0, 1, 0, 1), (1, 0, 2, 0),
        (0, 0, 1, 1), (1, 0, 1, 1), (3, 0, 2, 0), (2, 0, 1, 1), (3, 0, 1, 1), (2, 0, 2, 0),
        (1, 1, 1, 0), (1, 1, 0, 1), (0, 1, 1, 1), (3, 1, 2, 0), (0, 0, 3, 0), (0, 1, 2, 0),
        (2, 1, 0, 1), (0, 0, 2, 1), (1, 0, 3, 0), (3, 1, 1, 1), (1, 0, 2, 1), (2, 1, 1, 0),
        (3, 0, 3, 0), (2, 0, 2, 1), (3, 0, 2, 1), (1, 1, 1, 1), (2, 0, 3, 0), (0, 1, 2, 1),
        (1, 0, 3, 1), (1, 1, 2, 0), (3, 1, 2, 1), (2, 1, 1, 1), (3, 0, 3, 1), (2, 1, 2, 0),
        (2, 0, 3, 1), (3, 1, 3, 0), (0, 1, 3, 0), (1, 1, 3, 0), (0, 0, 3, 1), (1, 1, 2, 1),
        (2, 1, 3, 0), (2, 1, 2, 1), (0, 1, 3, 1), (1, 1, 3, 1), (3, 1, 3, 1), (2, 1, 3, 1),
    ),
)
OWN_SENDS = ((3, 0), (0, 2), (0, 0), (1, 3), (3, 2), (2, 1), (1, 1), (2, 0), (2, 2), (0, 3), (0, 1), (1, 2), (2, 3), (1, 0), (3, 3), (3, 1))
S_PLAN = Plan(
    ((160, "zxy"), (96, "zyx"), (128, "xyz")),
    (
        (1, 1, 3, 1), (2, 1, 3, 1), (2, 0, 3, 1), (2, 0, 3, 0), (0, 1, 2, 1), (2, 1, 3, 0),
        (0, 1, 3, 1), (0, 0, 3, 1), (2, 1, 2, 1), (1, 0, 3, 1), (2, 0, 2, 1), (1, 1, 3, 0),
        (0, 1, 3, 0), (0, 1, 1, 1), (2, 1, 2, 0), (1, 1, 2, 0), (2, 1, 1, 1), (0, 1, 0, 1),
        (1, 1, 2, 1), (2, 0, 1, 1), (1, 0, 3, 0), (0, 0, 1, 1), (0, 0, 2, 1), (0, 0, 3, 0),
        (1, 1, 0, 1), (0, 1, 2, 0), (2, 0, 2, 0), (1, 1, 1, 1), (2, 1, 1, 0), (2, 1, 0, 1),
        (0, 1, 1, 0), (1, 0, 2, 1), (1, 1, 1, 0), (0, 0, 2, 0), (2, 0, 1, 0), (0, 1, 0, 0),
        (1, 0, 1, 1), (0, 0, 0, 1), (1, 1, 0, 0), (1, 0, 2, 0), (2, 0, 0, 1), (1, 0, 0, 1),
        (0, 0, 1, 0), (2, 1, 0, 0), (1, 0, 1, 0),
    ),
)
GT_AT = 3


class Place:
    def __init__(self):
        self.t = lax.axis_index("tower")
        d = lax.axis_index("dp")
        self.z, self.y, self.c = d // 4, (d // 2) % 2, d % 2

    def device(self, t, z, y, c):
        return (t, z * 4 + y * 2 + c)

    def neighbour(self, kind):
        t, z, y, c = self.t, self.z, self.y, self.c
        return (
            self.device(1 - t, z, y, c),
            self.device(t, z, 1 - y, c),
            self.device(t, jnp.minimum(z + 1, Z_CHIPS - 1), y, c),
            self.device(t, jnp.maximum(z - 1, 0), y, c),
        )[kind]

    def line(self):
        return [
            self.device(self.t, lax.rem(self.z + k, Z_CHIPS), self.y, self.c)
            for k in range(1, Z_CHIPS)
        ]

    def sibling(self):
        return self.device(self.t, self.z, self.y, 1 - self.c)

    def has(self, kind):
        return {UP_: self.z < Z_CHIPS - 1, DN_: self.z > 0}.get(kind)

    def chip(self, dt=0, dz=0, dy=0):
        t = 1 - self.t if dt else self.t
        y = 1 - self.y if dy else self.y
        return t * 8 + (self.z + dz) * 2 + y

    def exists(self, dz):
        return None if dz == 0 else self.z >= -dz if dz < 0 else self.z < Z_CHIPS - dz


def both(first, second):
    return second if first is None else first if second is None else first & second


def when(condition, body):
    if condition is None:
        body()
    else:
        pl.when(condition)(body)


def greet(place, whole_line):
    barrier = pltpu.get_barrier_semaphore()
    targets = [place.neighbour(X_), place.neighbour(Y_), place.sibling()]
    if whole_line:
        targets += place.line()
    for target in targets:
        pl.semaphore_signal(barrier, inc=1, device_id=target, device_id_type=MESH)
    if whole_line:
        pl.semaphore_wait(barrier, len(targets))
        return
    for kind in (UP_, DN_):

        @pl.when(place.has(kind))
        def _(kind=kind):
            pl.semaphore_signal(
                barrier, inc=1, device_id=place.neighbour(kind), device_id_type=MESH
            )

    inner = (place.z > 0) & (place.z < Z_CHIPS - 1)
    pl.semaphore_wait(barrier, jnp.where(inner, len(targets) + 2, len(targets) + 1))


def plan_captions(lengths, picks, start_s, sorted_s, bound_s, images):
    captions = lengths.shape[1]

    def begin(c, run):
        start_s[c] = run
        return run + lengths[0, c]

    lax.fori_loop(0, captions, begin, jnp.int32(0))

    def image(i, run):
        bound_s[i] = run

        def caption(c, run):
            hit = picks[0, c] == i
            sorted_s[c] = jnp.where(hit, run, sorted_s[c])
            return run + jnp.where(hit, lengths[0, c], 0)

        return lax.fori_loop(0, captions, caption, run)

    def clear(c, run):
        sorted_s[c] = 0
        return run

    lax.fori_loop(0, captions, clear, 0)
    bound_s[images] = lax.fori_loop(0, images, image, jnp.int32(0))


def gather_kernel(
    images, lengths, picks, tokens, cot, img, master, norms,
    slots, x_o, meta_o, cot_o, enc_o, place_o,
    own, xs, metas, start_s, sorted_s, bound_s,
    ssem, rsem, sibsem, sibrecv, xsem, lsem,
):
    place = Place()
    rows = tokens.shape[0]
    captions = lengths.shape[1]
    own[...] = master[...].astype(BF)
    greet(place, False)
    sends = []

    def push(condition, part, chip, kind, mine=False):
        target = place.sibling() if kind == 4 else place.neighbour(kind)
        if kind < 4:
            condition = both(condition, place.has(kind))
        rows_p = G_PLAN.slot_rows(chip, place.c, part)
        src = own.at[pl.ds(G_PLAN.off[part], G_PLAN.rows[part])] if mine else slots.at[rows_p]
        sem = sibrecv if kind == 4 else rsem
        out = sibsem.at[part, chip] if kind == 4 else ssem.at[kind, part, chip]
        copy = pltpu.make_async_remote_copy(
            src_ref=src, dst_ref=slots.at[rows_p], send_sem=out, recv_sem=sem.at[part, chip],
            device_id=target, device_id_type=MESH,
        )
        when(condition, copy.start)
        sends.append((condition, copy))

    me = place.chip()
    for part, kind in OWN_SENDS + tuple((part, 4) for part in range(G_PLAN.count)):
        push(None, part, me, kind, mine=True)
    keep = pltpu.make_async_copy(
        own, slots.at[pl.ds(pl.multiple_of((me * 2 + place.c) * own.shape[0], 128), own.shape[0])], lsem
    )
    keep.start()

    plan_captions(lengths, picks, start_s, sorted_s, bound_s, images)
    token = lax.broadcasted_iota(jnp.int32, (1, rows), 1)

    def locate(c, where_to):
        inside = (token >= start_s[c]) & (token < start_s[c] + lengths[0, c])
        return jnp.where(inside, token + (sorted_s[c] - start_s[c]), where_to)

    where_to = lax.fori_loop(0, captions, locate, token)
    place_o[...] = jnp.broadcast_to(where_to, place_o.shape)
    lane = lax.broadcasted_iota(jnp.int32, metas.shape, 1)

    def note(c, row):
        return jnp.where(lane == c, sorted_s[c], row)

    row = lax.fori_loop(0, captions, note, jnp.zeros(metas.shape, jnp.int32))
    for i in range(images + 1):
        row = jnp.where(lane == BOUND_LANE + i, bound_s[i], row)
    metas[...] = row

    def sort(out, array):
        def body(b, _):
            target = lax.broadcasted_iota(jnp.int32, (QB, rows), 0) + b * QB
            onehot = (target == place_o[0:1, :]).astype(F32).astype(BF)
            out[blk(b), :] = nn(onehot, array[...]).astype(BF)
            return 0

        lax.fori_loop(0, rows // QB, body, 0)

    sort(xs, tokens)
    swaps = []
    for i, (src, dst) in enumerate(((metas, meta_o), (xs, x_o))):
        swaps.append(
            pltpu.make_async_remote_copy(
                src_ref=src, dst_ref=dst, send_sem=xsem.at[0, i], recv_sem=xsem.at[1, i],
                device_id=place.neighbour(X_), device_id_type=MESH,
            )
        )
        swaps[-1].start()

    def encode(i):
        def body(j, _):
            at = pl.ds(pl.multiple_of(i * IMG_ROWS + j * 64, 64), 64)
            normed, _i = normalise(img[at, :].astype(F32))
            enc_o[at, :] = (normed * norms[3:4, :] + norms[7:8, :]).astype(BF)
            return 0

        lax.fori_loop(0, IMG_ROWS // 64, body, 0)

    steps = img.shape[0] // IMG_ROWS
    done = 0
    for number, (part, dt, dz, dy) in enumerate(G_PLAN.pieces):
        there = place.exists(dz)
        chip = place.chip(dt, dz, dy)

        def arrived(part=part, chip=chip):
            rows_p = G_PLAN.slot_rows(chip, place.c, part)
            pltpu.make_async_remote_copy(
                src_ref=slots.at[rows_p], dst_ref=slots.at[rows_p], send_sem=ssem.at[0, part, chip],
                recv_sem=rsem.at[part, chip], device_id=place.neighbour(X_), device_id_type=MESH,
            ).wait_recv()

        when(there, arrived)
        for kind in G_PLAN.routes(part, dt, dz, dy) + [4]:
            push(there, part, chip, kind)
        if number == 4:
            sort(cot_o, cot)
        if number >= 6 and done < steps:
            encode(done)
            done += 1
    for i in range(done, steps):
        encode(i)

    def from_sibling(chip, _):
        for part in range(G_PLAN.count):
            rows_p = G_PLAN.slot_rows(chip, 1 - place.c, part)
            pltpu.make_async_remote_copy(
                src_ref=slots.at[rows_p], dst_ref=slots.at[rows_p], send_sem=sibsem.at[part, chip],
                recv_sem=sibrecv.at[part, chip], device_id=place.sibling(), device_id_type=MESH,
            ).wait_recv()
        return 0

    lax.fori_loop(0, 4 * Z_CHIPS, from_sibling, 0)
    for condition, copy in sends:
        when(condition, copy.wait_send)
    for swap in swaps:
        swap.wait()
    keep.wait()


IMG_ROWS = 192
ENC_ROWS = 192


def run_gather(images, lengths, picks, tokens, cot, img, master, norms, total_rows):
    rows = tokens.shape[0]
    dma = pltpu.SemaphoreType.DMA
    low = jax.ShapeDtypeStruct((rows, D), BF)
    return pl.pallas_call(
        functools.partial(gather_kernel, images),
        out_shape=(
            jax.ShapeDtypeStruct((total_rows, D), BF),
            low,
            jax.ShapeDtypeStruct((8, 128), jnp.int32),
            low,
            jax.ShapeDtypeStruct(img.shape, BF),
            jax.ShapeDtypeStruct((8, rows), jnp.int32),
        ),
        in_specs=[SM, SM, VM, VM, VM, VM, VM],
        out_specs=(ANY, ANY, ANY, VM, VM, VM),
        scratch_shapes=[
            pltpu.VMEM(master.shape, BF),
            pltpu.VMEM((rows, D), BF),
            pltpu.VMEM((8, 128), jnp.int32),
            pltpu.SMEM((lengths.shape[1],), jnp.int32),
            pltpu.SMEM((lengths.shape[1],), jnp.int32),
            pltpu.SMEM((images + 1,), jnp.int32),
            dma((4, G_PLAN.count, 16)),
            dma((G_PLAN.count, 16)),
            dma((G_PLAN.count, 16)),
            dma((G_PLAN.count, 16)),
            dma((2, 2)),
            dma,
        ],
        compiler_params=pltpu.CompilerParams(
            vmem_limit_bytes=VLIM, has_side_effects=True, collective_id=0
        ),
    )(lengths, picks, tokens, cot, img, master, norms)


def sum_kernel(
    grads, norm_terms, place_row, gt, out_back, dk_h, dv_h, w_h, img_h, norms,
    red_o, norm_o, gt_o, lay_o, gi_h,
    out_b, obsem, wkv, ebuf, obuf, ng, esem, osem, wksem, acc, sib, gtr, nbuf, nrecv,
    lsem, sibsem, sibrecv, ssem, rsem, gsem, nsend, nrs, *land,
):
    place = Place()
    rows = gt.shape[0]
    greet(place, True)
    order = S_PLAN.pieces + [(part, 0, 0, 0) for part in range(S_PLAN.count)]
    sends = []

    def local(part, chip):
        off = pl.ds(S_PLAN.off[part], S_PLAN.rows[part])
        return pltpu.make_async_copy(
            grads.at[S_PLAN.slot_rows(chip, place.c, part)], acc.at[chip, off], lsem.at[part, chip]
        )

    def across(part, chip):
        off = pl.ds(S_PLAN.off[part], S_PLAN.rows[part])
        return pltpu.make_async_remote_copy(
            src_ref=grads.at[S_PLAN.slot_rows(chip, 1 - place.c, part)], dst_ref=sib.at[chip, off],
            send_sem=sibsem.at[part, chip], recv_sem=sibrecv.at[part, chip],
            device_id=place.sibling(), device_id_type=MESH,
        )

    for part, dt, dz, dy in order:
        chip = place.chip(dt, dz, dy)

        def begin(part=part, chip=chip):
            across(part, chip).start()
            local(part, chip).start()

        when(place.exists(dz), begin)
    back = pltpu.make_async_remote_copy(
        src_ref=gt, dst_ref=gtr, send_sem=gsem.at[0], recv_sem=gsem.at[1],
        device_id=place.neighbour(X_), device_id_type=MESH,
    )

    def landing(part, kind, chip):
        at = {"x": chip // 8, "z": (chip // 2) % Z_CHIPS, "y": chip % 2}
        spot = 0
        for name in S_PLAN.landing_spots(part, kind)[0]:
            spot = spot * DIMS[name] + at[name]
        return land[part * 4 + kind].at[spot]

    def flow(part, kind, chip):
        off = pl.ds(S_PLAN.off[part], S_PLAN.rows[part])
        return pltpu.make_async_remote_copy(
            src_ref=acc.at[chip, off], dst_ref=landing(part, kind, chip),
            send_sem=ssem.at[part, chip], recv_sem=rsem.at[kind, part, chip],
            device_id=place.neighbour(kind), device_id_type=MESH,
        )

    def add(part, chip, other, final):
        def body(i, _):
            at = pl.ds(pl.multiple_of(S_PLAN.off[part] + i * 32, 32), 32)
            value = acc[chip, at, :].astype(F32)
            for ref in other:
                value = value + ref(part, pl.ds(pl.multiple_of(i * 32, 32), 32), at).astype(F32)
            if final:
                red_o[at, :] = value
            else:
                acc[chip, at, :] = value.astype(BF)
            return 0

        lax.fori_loop(0, S_PLAN.rows[part] // 32, body, 0)

    def norm_round(i, target):
        return pltpu.make_async_remote_copy(
            src_ref=nbuf.at[i], dst_ref=nrecv.at[i], send_sem=nsend.at[i], recv_sem=nrs.at[i],
            device_id=target, device_id_type=MESH,
        )

    def norm_line(k, target):
        return pltpu.make_async_remote_copy(
            src_ref=nbuf.at[3], dst_ref=nrecv.at[3 + place.z], send_sem=nsend.at[3 + k],
            recv_sem=nrs.at[3 + place.z], device_id=target, device_id_type=MESH,
        )

    def norm_from(z):
        return pltpu.make_async_remote_copy(
            src_ref=nbuf.at[3], dst_ref=nrecv.at[3 + z], send_sem=nsend.at[3], recv_sem=nrs.at[3 + z],
            device_id=place.neighbour(X_), device_id_type=MESH,
        )

    line = [norm_line(k, target) for k, target in enumerate(place.line())]
    rounds = [place.sibling(), place.neighbour(X_), place.neighbour(Y_)]
    keys = pltpu.make_async_copy(w_h, wkv, wksem)
    keys.start()
    out_copy = pltpu.make_async_copy(out_back, out_b, obsem)
    out_copy.start()
    steps = dk_h.shape[0] // ENC_ROWS
    ng[...] = jnp.zeros_like(ng)

    def fetch(i):
        at = pl.ds(i * ENC_ROWS, ENC_ROWS)
        return [
            pltpu.make_async_copy(ref.at[at], ebuf.at[j, i % 2], esem.at[j, i % 2])
            for j, ref in enumerate((dk_h, dv_h, img_h))
        ]

    def put(i):
        at = pl.ds(i * ENC_ROWS, ENC_ROWS)
        return [pltpu.make_async_copy(obuf.at[i % 2], gi_h.at[at], osem.at[i % 2])]

    def encoder_back(i):
        wait(fetch(i))
        if i >= 2:
            wait(put(i - 2))
        out = obuf.at[i % 2]
        out[...] = nt(ebuf[0, i % 2], wkv[0]) + nt(ebuf[1, i % 2], wkv[1])

        def body(j, _):
            normed, inv_std = normalise(ebuf[2, i % 2, blk(j, 64), :].astype(F32))
            grad = out[blk(j, 64), :].astype(BF).astype(F32)
            ng[0:1, :] += jnp.sum(grad * normed, axis=0, keepdims=True)
            ng[1:2, :] += jnp.sum(grad, axis=0, keepdims=True)
            out[blk(j, 64), :] = norm_back(grad, normed, inv_std, norms[3:4, :])
            return 0

        lax.fori_loop(0, ENC_ROWS // 64, body, 0, unroll=True)
        start(put(i))
        if i + 2 < steps:
            start(fetch(i + 2))

    start(fetch(0))
    start(fetch(1))

    def unsort(out, array):
        def body(b, _):
            target = lax.broadcasted_iota(jnp.int32, (rows, QB), 0)
            onehot = (target == place_row[0:1, blk(b)]).astype(F32).astype(BF)
            out[blk(b), :] = tn(onehot, array[...]).astype(out.dtype)
            return 0

        lax.fori_loop(0, rows // QB, body, 0)

    span = len(order) // 2 - 4
    enc_at = [2 + i * span // steps for i in range(steps)]
    norm_at = [span + 3 + (i * len(order)) // 14 for i in range(4)]
    for number, (part, dt, dz, dy) in enumerate(order):
        chip = place.chip(dt, dz, dy)
        if number == GT_AT:
            back.start()
        there = place.exists(dz)
        final = (dt, dz, dy) == (0, 0, 0)
        kinds = S_PLAN.routes(part, dt, dz, dy)

        def step(part=part, chip=chip, kinds=kinds, final=final, dt=dt, dz=dz, dy=dy):
            local(part, chip).wait()
            across(part, chip).wait_recv()
            refs = [lambda p, i, at: sib[chip, at, :]]
            fixed = [kind for kind in kinds if kind in (X_, Y_)]
            edge = [kind for kind in kinds if kind in (UP_, DN_)]
            for kind in fixed:
                flow(part, OPPOSITE[kind], chip).wait_recv()
                refs.append(
                    lambda p, i, at, kind=kind: landing(part, OPPOSITE[kind], chip)[i, :]
                )
            for kind in edge:

                def one(kind=kind):
                    flow(part, OPPOSITE[kind], chip).wait_recv()
                    add(part, chip, [lambda p, i, at: landing(part, OPPOSITE[kind], chip)[i, :]], False)

                pl.when(place.has(kind))(one)
            add(part, chip, refs, final)
            if not final:
                flow(part, S_PLAN.source(part, dt, dz, dy), chip).start()

        when(there, step)
        if not final:
            sends.append((there, part, chip, S_PLAN.source(part, dt, dz, dy)))
        if number in enc_at:
            if number == enc_at[0]:
                keys.wait()
            encoder_back(enc_at.index(number))
        if number == norm_at[0]:
            nbuf[0] = norm_terms[...]
            nbuf[0, 3:4, :] = ng[0:1, :]
            nbuf[0, 7:8, :] = ng[1:2, :]
            norm_round(0, rounds[0]).start()
        if number in norm_at[1:]:
            i = norm_at.index(number) - 1
            norm_round(i, rounds[i]).wait()
            nbuf[i + 1] = nbuf[i] + nrecv[i]
            if i < 2:
                norm_round(i + 1, rounds[i + 1]).start()
            else:
                for copy in line:
                    copy.start()
        if number == norm_at[0] + 1:
            out_copy.wait()
            unsort(lay_o, out_b)
        if number == norm_at[3] + 1:
            back.wait()
            unsort(gt_o, gtr)

    for z in range(Z_CHIPS):

        @pl.when(place.z != z)
        def _(z=z):
            norm_from(z).wait_recv()

        @pl.when(place.z == z)
        def _(z=z):
            nrecv[3 + z] = nbuf[3]

    wait(put(steps - 2) + put(steps - 1))
    norm_o[...] = (nrecv[3] + nrecv[4]) + (nrecv[5] + nrecv[6])
    for copy in line:
        copy.wait_send()
    for there, part, chip, kind in sends:
        when(there, flow(part, kind, chip).wait_send)

    def sent(chip, _):
        for part in range(S_PLAN.count):
            across(part, chip).wait_send()
        return 0

    lax.fori_loop(0, 4 * Z_CHIPS, sent, 0)


def run_sum(grads, norm_terms, place_row, gt, out_back, dk, dv, kv_weights, img, norms):
    rows = gt.shape[0]
    dma = pltpu.SemaphoreType.DMA
    shard = S_PLAN.shard
    line = 4 * Z_CHIPS
    return pl.pallas_call(
        sum_kernel,
        out_shape=(
            jax.ShapeDtypeStruct((shard, D), F32),
            jax.ShapeDtypeStruct((8, D), F32),
            jax.ShapeDtypeStruct((rows, D), F32),
            jax.ShapeDtypeStruct((rows, D), BF),
            jax.ShapeDtypeStruct(img.shape, F32),
        ),
        in_specs=[ANY, VM, VM, ANY, ANY, ANY, ANY, ANY, ANY, VM],
        out_specs=(VM,) * 4 + (ANY,),
        scratch_shapes=[
            pltpu.VMEM((rows, D), BF),
            dma,
            pltpu.VMEM((2, D, D), BF),
            pltpu.VMEM((3, 2, ENC_ROWS, D), BF),
            pltpu.VMEM((2, ENC_ROWS, D), F32),
            pltpu.VMEM((8, D), F32),
            dma((3, 2)),
            dma((2,)),
            dma,
            pltpu.VMEM((line, shard, D), BF),
            pltpu.VMEM((line, shard, D), BF),
            pltpu.VMEM((rows, D), BF),
            pltpu.VMEM((4, 8, D), F32),
            pltpu.VMEM((7, 8, D), F32),
            dma((S_PLAN.count, line)),
            dma((S_PLAN.count, line)),
            dma((S_PLAN.count, line)),
            dma((S_PLAN.count, line)),
            dma((4, S_PLAN.count, line)),
            dma((2,)),
            dma((7,)),
            dma((7,)),
        ]
        + [
            pltpu.VMEM((S_PLAN.landing_spots(part, kind)[1], S_PLAN.rows[part], D), BF)
            for part in range(S_PLAN.count)
            for kind in range(4)
        ],
        compiler_params=pltpu.CompilerParams(
            vmem_limit_bytes=VLIM, has_side_effects=True, collective_id=1
        ),
    )(grads, norm_terms, place_row, gt, out_back, dk, dv, kv_weights, img, norms)


def from_partner(block, axis):
    half = lax.axis_size(axis) // 2
    count = lax.axis_size(axis)
    return lax.ppermute(block, axis, [(i, (i + half) % count) for i in range(count)])


def adamw_update(weight, moment, second, grad_in, rate, decay_rate):
    new_moment = beta_one * moment + (1.0 - beta_one) * grad_in
    new_second = beta_two * second + (1.0 - beta_two) * grad_in * grad_in
    moment_hat = new_moment / (1.0 - beta_one**STEP)
    second_hat = new_second / (1.0 - beta_two**STEP)
    new_weight = weight - rate * (
        moment_hat / (jnp.sqrt(second_hat) + epsilon) + decay_rate * weight
    )
    return (new_weight, new_moment, new_second)


def caption_plan(lengths, picks, rows, images):
    ends = jnp.cumsum(lengths)
    starts = ends - lengths
    rank = picks * lengths.shape[0] + jnp.arange(lengths.shape[0], dtype=jnp.int32)
    ahead = rank[None, :] < rank[:, None]
    sorted_starts = jnp.sum(jnp.where(ahead, lengths[None, :], 0), axis=1)
    token = jnp.arange(rows, dtype=jnp.int32)
    inside = (token[:, None] >= starts[None, :]) & (token[:, None] < ends[None, :])
    place = token + jnp.sum(jnp.where(inside, (sorted_starts - starts)[None, :], 0), axis=1)
    edges = jnp.arange(images + 1, dtype=jnp.int32)
    bounds = jnp.sum(jnp.where(picks[None, :] < edges[:, None], lengths[None, :], 0), axis=1)
    return place, sorted_starts, bounds


def per_device(
    kernels,
    tokens,
    cotangent,
    caption_lengths,
    image_index,
    image_states,
    master_weights,
    first_moments,
    second_moments,
    owner_list,
    norm_params,
    norm_first,
    norm_second,
):
    rows = tokens.shape[0]
    groups = owner_list.shape[0]
    total_rows = 8 * D + 2 * FF
    group_rows = total_rows // groups
    images = image_states.shape[0]
    captions = caption_lengths.shape[1]
    axes = ("tower", "dp")
    direct = group_rows == GROUP
    ids = jnp.arange(groups, dtype=jnp.int32)
    inverse = jnp.sum(jnp.where(owner_list[None, :] == ids[:, None], ids[None, :], 0), axis=1)
    img = image_states.reshape(-1, D)
    if kernels:
        gathered, x, meta, sent_cot, enc, place_row = run_gather(
            images, caption_lengths, image_index, tokens, cotangent, img, master_weights,
            norm_params, total_rows,
        )
    else:
        gathered = lax.all_gather(master_weights.astype(BF), axes, axis=0, tiled=True)
        place, starts, bounds = caption_plan(caption_lengths[0], image_index[0], rows, images)
        into = (place[None, :] == jnp.arange(rows, dtype=jnp.int32)[:, None]).astype(BF)
        meta = jnp.zeros((8, 128), jnp.int32)
        meta = meta.at[0, :captions].set(starts)
        meta = meta.at[0, BOUND_LANE : BOUND_LANE + images + 1].set(bounds)
        meta = from_partner(meta, "tower")
        x = from_partner(nn(into, tokens).astype(BF), "tower")
        sent_cot = nn(into, cotangent).astype(BF)
        normed, _i = normalise(img.astype(F32))
        enc = (normed * norm_params[3] + norm_params[7]).astype(BF)
    if direct:
        slots = gathered.reshape(groups, GROUP, D)
        inv = inverse
    else:
        slots = gathered.reshape(groups, group_rows, D)[inverse].reshape(-1, GROUP, D)
        inv = jnp.arange(total_rows // GROUP, dtype=jnp.int32)
    cot = from_partner(sent_cot, "tower")
    *kept, kv_weights, r2 = run_attention_forward(
        captions, images, inv, meta, x, enc, norm_params, slots
    )
    out, g2, ng3, grads = run_feed_forward(inv, r2, cot, norm_params, slots)
    out_back = from_partner(out, "tower")
    gt, norm_terms, dk, dv, grads = run_attention_backward(
        captions, images, inv, meta, g2, x, kept, enc, norm_params, slots, grads, ng3
    )
    if kernels:
        reduced, norm_grads, grad_tokens, layer_out, grad_images = run_sum(
            grads.reshape(total_rows, D), norm_terms, place_row, gt, out_back, dk, dv, kv_weights,
            img, norm_params,
        )
    else:
        layer_out = tn(into, out_back).astype(BF)
        grad_tokens = tn(into, from_partner(gt, "tower"))
        grad_enc = (nt(dk, kv_weights[0]) + nt(dv, kv_weights[1])).astype(BF).astype(F32)
        normed, inv_std = normalise(img.astype(F32))
        grad_images = norm_back(grad_enc, normed, inv_std, norm_params[3:4])
        norm_terms = norm_terms.at[3].set(jnp.sum(grad_enc * normed, axis=0))
        norm_terms = norm_terms.at[7].set(jnp.sum(grad_enc, axis=0))
        if direct:
            arranged = grads.reshape(total_rows, D)
        else:
            arranged = grads.reshape(groups, group_rows, D)[owner_list].reshape(total_rows, D)
        reduced = lax.psum_scatter(arranged, axes, scatter_dimension=0, tiled=True).astype(F32)
        norm_grads = lax.psum(norm_terms, axes)
    new_weights, new_first, new_second = adamw_update(
        master_weights, first_moments, second_moments, reduced, learn_rate, weight_decay
    )
    norm_new, norm_first_new, norm_second_new = adamw_update(
        norm_params, norm_first, norm_second, norm_grads, norm_rate, 0.0
    )
    return (
        layer_out,
        grad_tokens,
        grad_images.reshape(image_states.shape),
        new_weights,
        new_first,
        new_second,
        new_weights.astype(BF),
        norm_new,
        norm_first_new,
        norm_second_new,
    )


def solution(mesh):
    split = P(("tower", "dp"), None)
    wide = P(("tower", "dp"), None, None)
    in_specs = (split,) * 4 + (wide,) + (split,) * 3 + (P(),) * 4
    out_specs = (split, split, wide) + (split,) * 4 + (P(),) * 3
    shape = dict(mesh.shape)
    kernels = shape["tower"] == 2 and shape["dp"] == 4 * Z_CHIPS
    return jax.shard_map(
        functools.partial(per_device, kernels),
        mesh=mesh,
        in_specs=in_specs,
        out_specs=out_specs,
        check_vma=False,
    )
```

```python
import functools

import jax
import jax.numpy as jnp
from jax import lax
from jax.experimental import pallas as pl
from jax.experimental.pallas import tpu as pltpu
from jax.sharding import PartitionSpec as P

D = 768
HEADS = 12
HDIM = 64
FF = 3072
STEP = 5
PAIRS = HEADS // 2
LANES = 2 * HDIM
QB = 128
HEAD_ROWS = 16
PAIR_GROUPS = ((0, 1, 2), (3, 4, 5))
GROUP = 192
BOUND_LANE = 64
PER = D // GROUP
SCALE = HDIM ** (-0.5)

beta_one = 0.5
beta_two = 0.6
learn_rate = 0.03
norm_rate = 0.4
weight_decay = 0.01
epsilon = 1e-08
norm_eps = 1e-05
masked_score = -1000000000.0

W_Q, W_K, W_V, W_O, C_Q, C_K, C_V, C_O, UP, DOWN = 0, 1, 2, 3, 4, 5, 6, 7, 8, 12

BF = jnp.bfloat16
F32 = jnp.float32
VM = pl.BlockSpec(memory_space=pltpu.VMEM)
SM = pl.BlockSpec(memory_space=pltpu.SMEM)
ANY = pl.BlockSpec(memory_space=pl.ANY)
VLIM = 58 * 2**20


def nn(a, b):
    return lax.dot_general(a, b, (((1,), (0,)), ((), ())), preferred_element_type=F32)


def nt(a, b):
    return lax.dot_general(a, b, (((1,), (1,)), ((), ())), preferred_element_type=F32)


def tn(a, b):
    return lax.dot_general(a, b, (((0,), (0,)), ((), ())), preferred_element_type=F32)


def blk(i, size=QB):
    return pl.ds(pl.multiple_of(i * size, size), size)


def lanes(p):
    return slice(p * LANES, (p + 1) * LANES)


def normalise(x):
    centred = x - jnp.mean(x, axis=-1, keepdims=True)
    inv = lax.rsqrt(jnp.mean(centred * centred, axis=-1, keepdims=True) + norm_eps)
    return centred * inv, inv


def norm_back(grad, normed, inv, gain):
    gn = grad * gain
    m1 = jnp.mean(gn, axis=-1, keepdims=True)
    m2 = jnp.mean(gn * normed, axis=-1, keepdims=True)
    return inv * (gn - m1 - normed * m2)


def head_masks():
    low = (lax.broadcasted_iota(jnp.int32, (1, LANES), 1) < HDIM).astype(F32)
    return low.astype(BF), (1.0 - low).astype(BF)


def two_heads(x, masks):
    return jnp.concatenate([x * masks[0], x * masks[1]], axis=0)


def merge_heads(both):
    return jnp.concatenate([both[:HDIM, :QB], both[HDIM:, QB:]], axis=0)


def weight_copies(slots, inv, buf, sem, matrix, slot):
    return [
        pltpu.make_async_copy(
            slots.at[inv[matrix * PER + j]], buf.at[slot, pl.ds(j * GROUP, GROUP)], sem.at[slot, j]
        )
        for j in range(PER)
    ]


def grad_copies(grads, inv, buf, sem, matrix, slot):
    return [
        pltpu.make_async_copy(
            buf.at[slot, pl.ds(j * GROUP, GROUP)], grads.at[inv[matrix * PER + j]], sem.at[slot, j]
        )
        for j in range(PER)
    ]


def start(copies):
    for copy in copies:
        copy.start()


def wait(copies):
    for copy in copies:
        copy.wait()


def causal_mask(meta, captions, b):
    query = lax.broadcasted_iota(jnp.int32, (1, QB), 1) + b * QB
    first = jnp.zeros((1, QB), jnp.int32)
    for c in range(captions):
        first = jnp.maximum(first, jnp.where(query >= meta[0, c], meta[0, c], 0))
    key = lax.broadcasted_iota(jnp.int32, (2 * QB, QB), 0) + (b - 1) * QB
    allowed = (key >= first) & (key <= query)
    return jnp.concatenate([allowed, allowed], axis=1)


def column_softmax(scores):
    top = jnp.max(scores, axis=0, keepdims=True)
    exponent = jnp.exp(scores - top)
    total = jnp.sum(exponent, axis=0, keepdims=True)
    return exponent, 1.0 / total, top + jnp.log(total)


def head_products(grad, out):
    prod = grad.astype(F32) * out
    high = prod.astype(BF)
    low = (prod - high.astype(F32)).astype(BF)
    head = lax.broadcasted_iota(jnp.int32, (HEAD_ROWS, D), 0)
    lane = lax.broadcasted_iota(jnp.int32, (HEAD_ROWS, D), 1)
    pick = ((lane >= head * HDIM) & (lane < (head + 1) * HDIM)).astype(F32).astype(BF)
    return nt(pick, high) + nt(pick, low)


def pair_row(table, p):
    return jnp.concatenate([table[2 * p : 2 * p + 1], table[2 * p + 1 : 2 * p + 2]], axis=1)


def call(body, out_shape, in_specs, out_specs, scratch, aliases=None, effects=False):
    return pl.pallas_call(
        body,
        out_shape=out_shape,
        in_specs=in_specs,
        out_specs=out_specs,
        scratch_shapes=scratch,
        input_output_aliases=aliases or {},
        compiler_params=pltpu.CompilerParams(vmem_limit_bytes=VLIM, has_side_effects=effects),
    )


def image_blocks(meta, i):
    low, high = meta[0, BOUND_LANE + i], meta[0, BOUND_LANE + i + 1]
    first = low // QB
    last = jnp.where(high > low, (high + QB - 1) // QB, first)
    return low, high, first, last


def blk_of(i, size):
    return pl.ds(pl.multiple_of(i * size, 64), size)


def attention_forward(
    captions, images, inv, meta, x, enc_h, norms, slots,
    q_h, k_h, v_h, att_h, r1_h, cq_h, kk_h, vv_h, cross_h, atf_h, crf_h, fst_h, snd_h, slse_o, clse_o, w_h, r2_o,
    wbuf, low, second, q, kpad, vpad, att, atf, r1, cq, enc, kv, cross, acc, wsem, esem, osem,
):
    rows = x.shape[0]
    patches = enc.shape[0] // images
    loads = [weight_copies(slots, inv, wbuf, wsem, m, m) for m in range(8)]
    for load in loads[:3]:
        start(load)
    enc_copy = pltpu.make_async_copy(enc_h, enc, esem)
    enc_copy.start()
    for m in (C_K, C_V, W_O, C_Q, C_O):
        start(loads[m])
    masks = head_masks()
    kk, vv = kv.at[0], kv.at[1]
    pieces = enc.shape[0] // D
    copies = []

    def store(i, vmem, hbm):
        copies.append(pltpu.make_async_copy(vmem, hbm, osem.at[i]))
        copies[-1].start()

    def norm_one(i, _):
        normed, _i = normalise(x[blk(i), :].astype(F32))
        low[blk(i), :] = (normed * norms[0:1, :] + norms[4:5, :]).astype(BF)
        return 0

    lax.fori_loop(0, rows // QB, norm_one, 0, unroll=True)
    store(12, low, fst_h)
    kpad[pl.ds(0, QB), :] = jnp.zeros((QB, D), BF)
    vpad[pl.ds(0, QB), :] = jnp.zeros((QB, D), BF)
    wait(loads[W_Q])
    q[...] = (nn(low[...], wbuf[W_Q]) * SCALE).astype(BF)
    store(0, q, q_h)
    wait(loads[W_K])
    kpad[pl.ds(QB, rows), :] = nn(low[...], wbuf[W_K]).astype(BF)
    store(1, kpad.at[pl.ds(QB, rows)], k_h)
    wait(loads[W_V])
    vpad[pl.ds(QB, rows), :] = nn(low[...], wbuf[W_V]).astype(BF)
    store(2, vpad.at[pl.ds(QB, rows)], v_h)
    enc_copy.wait()
    wait(loads[C_K])
    wait(loads[C_V])
    store(3, wbuf.at[pl.ds(C_K, 2)], w_h)

    def attend(b, _):
        allowed = causal_mask(meta, captions, b)
        span = pl.ds(pl.multiple_of(b * QB, QB), 2 * QB)
        scores = [
            nt(kpad[span, lanes(p)], two_heads(q[blk(b), lanes(p)], masks)) for p in range(PAIRS)
        ]
        piece = blk(b % pieces, D)
        kv[b // pieces, piece, :] = nn(enc[piece, :], wbuf[C_K + b // pieces]).astype(BF)
        soft = [column_softmax(jnp.where(allowed, score, masked_score)) for score in scores]
        for p in range(PAIRS):
            exponent, scale, lse = soft[p]
            out = merge_heads(tn(vpad[span, lanes(p)], exponent.astype(BF)) * scale).T
            atf[blk(b), lanes(p)] = out
            att[blk(b), lanes(p)] = out.astype(BF)
            slse_o[b, p : p + 1, :] = lse
        return 0

    assert rows // QB == 2 * pieces
    lax.fori_loop(0, rows // QB, attend, 0)
    store(4, att, att_h)
    store(10, atf, atf_h)

    store(5, kk, kk_h)
    store(6, vv, vv_h)
    wait(loads[W_O])
    r1[...] = x[...].astype(F32) + nn(att[...], wbuf[W_O])
    store(7, r1, r1_h)

    def norm_two(i, _):
        normed, _i = normalise(r1[blk(i), :])
        second[blk(i), :] = (normed * norms[1:2, :] + norms[5:6, :]).astype(BF)
        return 0

    lax.fori_loop(0, rows // QB, norm_two, 0, unroll=True)
    store(13, second, snd_h)
    wait(loads[C_Q])
    cq[...] = (nn(second[...], wbuf[C_Q]) * SCALE).astype(BF)
    store(8, cq, cq_h)
    acc[...] = jnp.zeros_like(acc)
    clse_o[...] = jnp.zeros_like(clse_o)

    def image(i, _):
        first_row, end_row, first, last = image_blocks(meta, i)

        def attend_image(b, _):
            token = lax.broadcasted_iota(jnp.int32, (1, QB), 1) + b * QB
            here = ((token >= first_row) & (token < end_row)).astype(F32)
            here = jnp.concatenate([here, here], axis=1)
            at = blk_of(i, patches)
            scores = [
                nt(kk[at, lanes(p)], two_heads(cq[blk(b), lanes(p)], masks)) for p in range(PAIRS)
            ]
            soft = [column_softmax(score) for score in scores]
            for p in range(PAIRS):
                exponent, scale, lse = soft[p]
                clse_o[b, p : p + 1, :] = jnp.where(here > 0, lse, clse_o[b, p : p + 1, :])
                out = tn(vv[at, lanes(p)], exponent.astype(BF)) * (scale * here)
                acc[blk(b), lanes(p)] += merge_heads(out).T
            return 0

        lax.fori_loop(first, last, attend_image, 0)
        return 0

    lax.fori_loop(0, images, image, 0)
    cross[...] = acc[...].astype(BF)
    store(9, cross, cross_h)
    store(11, acc, crf_h)
    wait(loads[C_O])
    r2_o[...] = r1[...] + nn(cross[...], wbuf[C_O])
    for copy in copies:
        copy.wait()


def run_attention_forward(captions, images, inv, meta, x, enc, norms, slots):
    rows = x.shape[0]
    one = jax.ShapeDtypeStruct((rows, D), BF)
    full = jax.ShapeDtypeStruct((rows, D), F32)
    kv = jax.ShapeDtypeStruct(enc.shape, BF)
    lse = jax.ShapeDtypeStruct((rows // QB, 8, 2 * QB), F32)
    low = pltpu.VMEM((rows, D), BF)
    pad = pltpu.VMEM((rows + QB, D), BF)
    big = pltpu.VMEM((rows, D), F32)
    wide = pltpu.VMEM(enc.shape, BF)
    return call(
        functools.partial(attention_forward, captions, images),
        (one, one, one, one, full, one, kv, kv, one, full, full, one, one, lse, lse)
        + (jax.ShapeDtypeStruct((2, D, D), BF), full),
        [SM, SM, VM, ANY, VM, ANY],
        (ANY,) * 13 + (VM, VM, ANY, VM),
        [
            pltpu.VMEM((8, D, D), BF), low, low, low, pad, pad, low, big, big, low, wide,
            pltpu.VMEM((2,) + enc.shape, BF), low, big, pltpu.SemaphoreType.DMA((8, PER)), pltpu.SemaphoreType.DMA,
            pltpu.SemaphoreType.DMA((14,)),
        ],
    )(inv, meta, x, enc, norms, slots)


GELU_A = 0.7978845608028654
GELU_B = GELU_A * 0.044715


def feed_forward(
    inv, r2, cot_h, norms, slots, out_o, g2_o, ng_o, grads,
    cot, csem, wup, wdown, third, pre, gh, hid, gpre, acc, gthird, gup, gdown, usem, dsem, gusem, gdsem,
):
    rows = r2.shape[0]
    chunks = FF // D

    def loads(c, slot):
        return weight_copies(slots, inv, wup, usem, UP + c, slot) + weight_copies(
            slots, inv, wdown, dsem, DOWN + c, slot
        )

    def stores(c, slot):
        return grad_copies(grads, inv, gup, gusem, UP + c, slot) + grad_copies(
            grads, inv, gdown, gdsem, DOWN + c, slot
        )

    start(loads(0, 0))
    cot_copy = pltpu.make_async_copy(cot_h, cot, csem)
    cot_copy.start()

    def norm_three(i, _):
        normed, _i = normalise(r2[blk(i), :])
        third[blk(i), :] = (normed * norms[2:3, :] + norms[6:7, :]).astype(BF)
        return 0

    lax.fori_loop(0, rows // QB, norm_three, 0, unroll=2)
    cot_copy.wait()
    acc[...] = r2[...]
    gthird[...] = jnp.zeros_like(gthird)

    def chunk(c, _):
        slot = c % 2

        @pl.when(c + 1 < chunks)
        def _():
            start(loads(c + 1, 1 - slot))

        wait(loads(c, slot))
        pre[...] = nt(third[...], wup[slot])
        gh[...] = nt(cot[...], wdown[slot])

        def gelu(i, _):
            x = pre[blk(i, 64), :]
            x2 = x * x
            t = jnp.tanh(x * (GELU_A + GELU_B * x2))
            half = 0.5 + 0.5 * t
            value = x * half
            hid[blk(i, 64), :] = value.astype(BF)
            slope = half + value * (1.0 - t) * (GELU_A + 3.0 * GELU_B * x2)
            gpre[blk(i, 64), :] = (gh[blk(i, 64), :] * slope).astype(BF)
            return 0

        lax.fori_loop(0, rows // 64, gelu, 0, unroll=2)

        @pl.when(c >= 2)
        def _():
            wait(stores(c - 2, slot))

        acc[...] += nn(hid[...], wdown[slot])
        gdown[slot] = tn(hid[...], cot[...]).astype(BF)
        gup[slot] = tn(gpre[...], third[...]).astype(BF)
        start(stores(c, slot))
        gthird[...] += nn(gpre[...], wup[slot])
        return 0

    lax.fori_loop(0, chunks, chunk, 0)
    out_o[...] = acc[...].astype(BF)
    ng_o[...] = jnp.zeros_like(ng_o)

    def back(i, _):
        normed, inv_std = normalise(r2[blk(i), :])
        grad = gthird[blk(i), :]
        ng_o[0:1, :] += jnp.sum(grad * normed, axis=0, keepdims=True)
        ng_o[1:2, :] += jnp.sum(grad, axis=0, keepdims=True)
        g2_o[blk(i), :] = cot[blk(i), :].astype(F32) + norm_back(
            grad, normed, inv_std, norms[2:3, :]
        )
        return 0

    lax.fori_loop(0, rows // QB, back, 0, unroll=2)
    for c in range(chunks - 2, chunks):
        wait(stores(c, c % 2))


def run_feed_forward(inv, r2, cot, norms, slots):
    rows = r2.shape[0]
    big = pltpu.VMEM((rows, D), F32)
    low = pltpu.VMEM((rows, D), BF)
    two = pltpu.VMEM((2, D, D), BF)
    sem = pltpu.SemaphoreType.DMA((2, PER))
    return call(
        feed_forward,
        (
            jax.ShapeDtypeStruct((rows, D), BF),
            jax.ShapeDtypeStruct((rows, D), F32),
            jax.ShapeDtypeStruct((2, D), F32),
            jax.ShapeDtypeStruct(slots.shape, BF),
        ),
        [SM, VM, ANY, VM, ANY],
        (VM, VM, VM, ANY),
        [low, pltpu.SemaphoreType.DMA, two, two, low, big, big, low, low, big, big, two, two, sem, sem, sem, sem],
    )(inv, r2, cot, norms, slots)


def attention_backward(
    captions, images,
    inv, meta, g2, x_h, q_h, k_h, v_h, att_h, r1_h, cq_h, kk_h, vv_h, cross, atf_h, crf_h, fst_h, snd_h,
    slse, clse, enc_h, norms, slots, grads_in, ng3,
    gt_o, ng_o, dk_h, dv_h, grads,
    wbuf, gbuf, x, q, kpad, vpad, att, r1, cq, kk, vv, enc, gca, dq, acck, accv, big, out32,
    low_n, delta, wsem, gsem, isem, osem,
):
    rows = g2.shape[0]
    patches = enc.shape[0] // images
    names = (C_O, C_Q, W_O, W_Q, W_K, W_V)
    loads = [weight_copies(slots, inv, wbuf, wsem, m, i) for i, m in enumerate(names)]
    body = pl.ds(QB, rows)
    inputs = [
        pltpu.make_async_copy(hbm, vmem, isem.at[i])
        for i, (hbm, vmem) in enumerate(
            (
                (crf_h, out32), (cq_h, cq), (kk_h, kk), (vv_h, vv), (enc_h, enc), (r1_h, r1),
                (snd_h, low_n), (att_h, att), (q_h, q), (k_h, kpad.at[body]),
                (v_h, vpad.at[body]), (x_h, x), (atf_h, out32), (fst_h, low_n),
            )
        )
    ]
    start(loads[0])
    start(inputs[:5])
    start(loads[1])
    start(inputs[5:12])
    for load in loads[2:]:
        start(load)

    def store(matrix, slot):
        copies = grad_copies(grads, inv, gbuf, gsem, matrix, slot)
        start(copies)
        return copies

    masks = head_masks()
    ng_o[...] = jnp.zeros_like(ng_o)
    ng_o[2:3, :] = ng3[0:1, :]
    ng_o[6:7, :] = ng3[1:2, :]
    low = dq
    low[...] = g2[...].astype(BF)
    gbuf[0] = tn(cross[...], low[...]).astype(BF)
    store_co = store(C_O, 0)
    wait(loads[0])
    gca[...] = nt(low[...], wbuf[0]).astype(BF)
    dq[...] = jnp.zeros_like(dq)
    wait(inputs[:4])

    def deltas(b, _):
        delta[b] = head_products(gca[blk(b), :], out32[blk(b), :])
        return 0

    lax.fori_loop(0, rows // QB, deltas, 0)
    start(inputs[12:13])

    def image(i, _):
        first_row, end_row, first, last = image_blocks(meta, i)
        ik = acck.at[pl.ds(0, patches)]
        iv = accv.at[pl.ds(0, patches)]
        ik[...] = jnp.zeros_like(ik)
        iv[...] = jnp.zeros_like(iv)

        def attend_image(b, _):
            token = lax.broadcasted_iota(jnp.int32, (QB, LANES), 0) + b * QB
            here = ((token >= first_row) & (token < end_row)).astype(F32).astype(BF)
            column = lax.broadcasted_iota(jnp.int32, (1, QB), 1) + b * QB
            inside = (column >= first_row) & (column < end_row)
            inside = jnp.concatenate([inside, inside], axis=1)
            at = blk_of(i, patches)
            table = delta[b]
            for group in PAIR_GROUPS:
                q2 = [two_heads(cq[blk(b), lanes(p)], masks) for p in group]
                go2 = [two_heads(gca[blk(b), lanes(p)] * here, masks) for p in group]
                scores = [nt(kk[at, lanes(p)], one) for p, one in zip(group, q2)]
                gps = [nt(vv[at, lanes(p)], go) for p, go in zip(group, go2)]
                probs = [
                    jnp.exp(score - jnp.where(inside, clse[b, p : p + 1, :], -masked_score))
                    for p, score in zip(group, scores)
                ]
                for p, prob, go in zip(group, probs, go2):
                    iv[:, lanes(p)] += nn(prob.astype(BF), go)
                gss = [
                    (prob * (gp - pair_row(table, p))).astype(BF)
                    for p, prob, gp in zip(group, probs, gps)
                ]
                for p, gs, one in zip(group, gss, q2):
                    ik[:, lanes(p)] += nn(gs, one)
                for p, gs in zip(group, gss):
                    gq = merge_heads(tn(kk[at, lanes(p)], gs)).T * SCALE
                    dq[blk(b), lanes(p)] += gq.astype(BF)
            return 0

        lax.fori_loop(first, last, attend_image, 0)
        kk[blk_of(i, patches), :] = ik[...].astype(BF)
        vv[blk_of(i, patches), :] = iv[...].astype(BF)
        return 0

    lax.fori_loop(0, images, image, 0)
    dk, dv = kk, vv
    out_k = pltpu.make_async_copy(dk, dk_h, osem.at[0])
    out_v = pltpu.make_async_copy(dv, dv_h, osem.at[1])
    start([out_k, out_v])
    wait(inputs[4:5])
    stores = []
    for slot, matrix, grad in ((1, C_K, dk), (2, C_V, dv)):
        gbuf[slot] = tn(enc[...], grad[...]).astype(BF)
        stores.append(store(matrix, slot))
    wait(inputs[5:7])
    gbuf[3] = tn(low_n[...], dq[...]).astype(BF)
    start(inputs[13:])
    stores.append(store(C_Q, 3))
    wait(loads[1])
    big[...] = nt(dq[...], wbuf[1])

    def back_two(i, _):
        normed, inv_std = normalise(r1[blk(i), :])
        grad = big[blk(i), :]
        ng_o[1:2, :] += jnp.sum(grad * normed, axis=0, keepdims=True)
        ng_o[5:6, :] += jnp.sum(grad, axis=0, keepdims=True)
        total = g2[blk(i), :] + norm_back(grad, normed, inv_std, norms[1:2, :])
        r1[blk(i), :] = total
        low[blk(i), :] = total.astype(BF)
        return 0

    lax.fori_loop(0, rows // QB, back_two, 0, unroll=True)
    g1 = r1
    wait(inputs[7:13])
    wait(store_co)
    gbuf[0] = tn(att[...], low[...]).astype(BF)
    stores.append(store(W_O, 0))
    wait(loads[2])
    gca[...] = nt(low[...], wbuf[2]).astype(BF)
    kpad[pl.ds(0, QB), :] = jnp.zeros((QB, D), BF)
    vpad[pl.ds(0, QB), :] = jnp.zeros((QB, D), BF)
    acck[...] = jnp.zeros_like(acck)
    accv[...] = jnp.zeros_like(accv)
    lax.fori_loop(0, rows // QB, deltas, 0)
    wait([out_k, out_v])

    def attend(b, _):
        allowed = causal_mask(meta, captions, b)
        span = pl.ds(pl.multiple_of(b * QB, QB), 2 * QB)
        group = range(PAIRS)
        q2 = [two_heads(q[blk(b), lanes(p)], masks) for p in group]
        go2 = [two_heads(gca[blk(b), lanes(p)], masks) for p in group]
        scores = [nt(kpad[span, lanes(p)], q2[p]) for p in group]
        gps = [nt(vpad[span, lanes(p)], go2[p]) for p in group]
        table = delta[b]
        probs = [
            jnp.where(allowed, jnp.exp(scores[p] - slse[b, p : p + 1, :]), 0.0) for p in group
        ]
        for p in group:
            accv[span, lanes(p)] += nn(probs[p].astype(BF), go2[p])
        gss = [(probs[p] * (gps[p] - pair_row(table, p))).astype(BF) for p in group]
        for p in group:
            acck[span, lanes(p)] += nn(gss[p], q2[p])
        for p in group:
            gq = merge_heads(tn(kpad[span, lanes(p)], gss[p])).T * SCALE
            dq[blk(b), lanes(p)] = gq.astype(BF)
        return 0

    lax.fori_loop(0, rows // QB, attend, 0)
    sk, sv = dk.at[pl.ds(0, rows)], dv.at[pl.ds(0, rows)]
    sk[...] = acck[body, :].astype(BF)
    sv[...] = accv[body, :].astype(BF)

    for done in stores[:3]:
        wait(done)
    wait(inputs[13:])
    for slot, matrix, grad in ((1, W_Q, dq), (2, W_K, sk), (3, W_V, sv)):
        gbuf[slot] = tn(low_n[...], grad[...]).astype(BF)
        stores.append(store(matrix, slot))
    for load in loads[3:]:
        wait(load)
    big[...] = nt(dq[...], wbuf[3]) + nt(sk[...], wbuf[4]) + nt(sv[...], wbuf[5])

    def back_one(i, _):
        normed, inv_std = normalise(x[blk(i), :].astype(F32))
        grad = big[blk(i), :]
        ng_o[0:1, :] += jnp.sum(grad * normed, axis=0, keepdims=True)
        ng_o[4:5, :] += jnp.sum(grad, axis=0, keepdims=True)
        gt_o[blk(i), :] = (g1[blk(i), :] + norm_back(grad, normed, inv_std, norms[0:1, :])).astype(
            BF
        )
        return 0

    lax.fori_loop(0, rows // QB, back_one, 0, unroll=True)
    for done in stores[3:]:
        wait(done)


def run_attention_backward(captions, images, inv, meta, g2, x, kept, enc, norms, slots, grads, ng3):
    rows = g2.shape[0]
    low = pltpu.VMEM((rows, D), BF)
    pad = pltpu.VMEM((rows + QB, D), BF)
    padf = pltpu.VMEM((rows + QB, D), F32)
    big = pltpu.VMEM((rows, D), F32)
    wide = pltpu.VMEM(enc.shape, BF)
    kv = jax.ShapeDtypeStruct(enc.shape, BF)
    dma = pltpu.SemaphoreType.DMA
    return call(
        functools.partial(attention_backward, captions, images),
        (
            jax.ShapeDtypeStruct((rows, D), BF),
            jax.ShapeDtypeStruct((8, D), F32),
            kv,
            kv,
            jax.ShapeDtypeStruct(slots.shape, BF),
        ),
        [SM, SM, VM] + [ANY] * 9 + [VM, ANY, ANY, ANY, ANY, VM, VM, ANY, VM, ANY, ANY, VM],
        (VM, VM, ANY, ANY, ANY),
        [
            pltpu.VMEM((6, D, D), BF), pltpu.VMEM((4, D, D), BF), low, low, pad, pad, low, big, low,
            wide, wide, wide, low, low, padf, padf, big, big, low,
            pltpu.VMEM((rows // QB, HEAD_ROWS, QB), F32),
            dma((6, PER)), dma((4, PER)), dma((14,)), dma((2,)),
        ],
        aliases={22: 4},
    )(inv, meta, g2, x, *kept, enc, norms, slots, grads, ng3)


MESH = pl.DeviceIdType.MESH
X_, Y_, UP_, DN_ = 0, 1, 2, 3
OPPOSITE = (X_, Y_, DN_, UP_)
Z_CHIPS = 4
DIMS = {"x": 2, "y": 2, "z": Z_CHIPS}


class Plan:
    def __init__(self, parts, arrivals):
        self.rows = [rows for rows, _ in parts]
        self.order = [order for _, order in parts]
        self.off = [sum(self.rows[:i]) for i in range(len(parts))]
        self.count = len(parts)
        self.shard = sum(self.rows)
        self.pieces = [
            (part, dt, step, dy)
            for part, dt, dz, dy in arrivals
            for step in ((-dz, dz) if dz else (0,))
        ]

    def last_axis(self, part, dt, dz, dy):
        moved = {"x": dt, "y": dy, "z": dz}
        return max((i for i, axis in enumerate(self.order[part]) if moved[axis]), default=-1)

    def routes(self, part, dt, dz, dy):
        order = self.order[part]
        last = self.last_axis(part, dt, dz, dy)
        kinds = []
        if last >= 0 and order[last] == "z":
            kinds.append(UP_ if dz < 0 else DN_)
        for axis in order[last + 1 :]:
            kinds += {"x": [X_], "y": [Y_], "z": [UP_, DN_]}[axis]
        return kinds

    def source(self, part, dt, dz, dy):
        axis = self.order[part][self.last_axis(part, dt, dz, dy)]
        return {"x": X_, "y": Y_, "z": UP_ if dz > 0 else DN_}[axis]

    def landing_spots(self, part, kind):
        axis = "xyzz"[kind]
        ahead = self.order[part]
        ahead = ahead[: ahead.index(axis)] + ("z" if axis == "z" else "")
        spots = 1
        for name in ahead:
            spots *= DIMS[name]
        return ahead, spots

    def slot_rows(self, chip, core, part):
        first = (chip * 2 + core) * self.shard + self.off[part]
        return pl.ds(pl.multiple_of(first, 32), self.rows[part])


G_PLAN = Plan(
    ((64, "xyz"), (64, "zxy"), (128, "zyx"), (128, "xzy")),
    (
        (0, 0, 1, 0), (3, 1, 0, 0), (2, 0, 0, 1), (0, 1, 0, 0), (1, 0, 0, 1), (1, 0, 1, 0),
        (0, 0, 0, 1), (3, 0, 1, 0), (2, 0, 1, 0), (2, 1, 0, 0), (1, 1, 0, 0), (3, 0, 0, 1),
        (0, 0, 2, 0), (3, 1, 1, 0), (3, 1, 0, 1), (0, 1, 1, 0), (0, 1, 0, 1), (1, 0, 2, 0),
        (0, 0, 1, 1), (1, 0, 1, 1), (3, 0, 2, 0), (2, 0, 1, 1), (3, 0, 1, 1), (2, 0, 2, 0),
        (1, 1, 1, 0), (1, 1, 0, 1), (0, 1, 1, 1), (3, 1, 2, 0), (0, 0, 3, 0), (0, 1, 2, 0),
        (2, 1, 0, 1), (0, 0, 2, 1), (1, 0, 3, 0), (3, 1, 1, 1), (1, 0, 2, 1), (2, 1, 1, 0),
        (3, 0, 3, 0), (2, 0, 2, 1), (3, 0, 2, 1), (1, 1, 1, 1), (2, 0, 3, 0), (0, 1, 2, 1),
        (1, 0, 3, 1), (1, 1, 2, 0), (3, 1, 2, 1), (2, 1, 1, 1), (3, 0, 3, 1), (2, 1, 2, 0),
        (2, 0, 3, 1), (3, 1, 3, 0), (0, 1, 3, 0), (1, 1, 3, 0), (0, 0, 3, 1), (1, 1, 2, 1),
        (2, 1, 3, 0), (2, 1, 2, 1), (0, 1, 3, 1), (1, 1, 3, 1), (3, 1, 3, 1), (2, 1, 3, 1),
    ),
)
OWN_SENDS = ((3, 0), (0, 2), (0, 0), (1, 3), (3, 2), (2, 1), (1, 1), (2, 0), (2, 2), (0, 3), (0, 1), (1, 2), (2, 3), (1, 0), (3, 3), (3, 1))
S_PLAN = Plan(
    ((160, "zxy"), (96, "zyx"), (128, "xyz")),
    (
        (1, 1, 3, 1), (2, 1, 3, 1), (2, 0, 3, 1), (2, 0, 3, 0), (0, 1, 2, 1), (2, 1, 3, 0),
        (0, 1, 3, 1), (0, 0, 3, 1), (2, 1, 2, 1), (1, 0, 3, 1), (2, 0, 2, 1), (1, 1, 3, 0),
        (0, 1, 3, 0), (0, 1, 1, 1), (2, 1, 2, 0), (1, 1, 2, 0), (2, 1, 1, 1), (0, 1, 0, 1),
        (1, 1, 2, 1), (2, 0, 1, 1), (1, 0, 3, 0), (0, 0, 1, 1), (0, 0, 2, 1), (0, 0, 3, 0),
        (1, 1, 0, 1), (0, 1, 2, 0), (2, 0, 2, 0), (1, 1, 1, 1), (2, 1, 1, 0), (2, 1, 0, 1),
        (0, 1, 1, 0), (1, 0, 2, 1), (1, 1, 1, 0), (0, 0, 2, 0), (2, 0, 1, 0), (0, 1, 0, 0),
        (1, 0, 1, 1), (0, 0, 0, 1), (1, 1, 0, 0), (1, 0, 2, 0), (2, 0, 0, 1), (1, 0, 0, 1),
        (0, 0, 1, 0), (2, 1, 0, 0), (1, 0, 1, 0),
    ),
)
GT_AT = 3


class Place:
    def __init__(self):
        self.t = lax.axis_index("tower")
        d = lax.axis_index("dp")
        self.z, self.y, self.c = d // 4, (d // 2) % 2, d % 2

    def device(self, t, z, y, c):
        return (t, z * 4 + y * 2 + c)

    def neighbour(self, kind):
        t, z, y, c = self.t, self.z, self.y, self.c
        return (
            self.device(1 - t, z, y, c),
            self.device(t, z, 1 - y, c),
            self.device(t, jnp.minimum(z + 1, Z_CHIPS - 1), y, c),
            self.device(t, jnp.maximum(z - 1, 0), y, c),
        )[kind]

    def line(self):
        return [
            self.device(self.t, lax.rem(self.z + k, Z_CHIPS), self.y, self.c)
            for k in range(1, Z_CHIPS)
        ]

    def sibling(self):
        return self.device(self.t, self.z, self.y, 1 - self.c)

    def has(self, kind):
        return {UP_: self.z < Z_CHIPS - 1, DN_: self.z > 0}.get(kind)

    def chip(self, dt=0, dz=0, dy=0):
        t = 1 - self.t if dt else self.t
        y = 1 - self.y if dy else self.y
        return t * 8 + (self.z + dz) * 2 + y

    def exists(self, dz):
        return None if dz == 0 else self.z >= -dz if dz < 0 else self.z < Z_CHIPS - dz


def both(first, second):
    return second if first is None else first if second is None else first & second


def when(condition, body):
    if condition is None:
        body()
    else:
        pl.when(condition)(body)


def greet(place, whole_line):
    barrier = pltpu.get_barrier_semaphore()
    targets = [place.neighbour(X_), place.neighbour(Y_), place.sibling()]
    if whole_line:
        targets += place.line()
    for target in targets:
        pl.semaphore_signal(barrier, inc=1, device_id=target, device_id_type=MESH)
    if whole_line:
        pl.semaphore_wait(barrier, len(targets))
        return
    for kind in (UP_, DN_):

        @pl.when(place.has(kind))
        def _(kind=kind):
            pl.semaphore_signal(
                barrier, inc=1, device_id=place.neighbour(kind), device_id_type=MESH
            )

    inner = (place.z > 0) & (place.z < Z_CHIPS - 1)
    pl.semaphore_wait(barrier, jnp.where(inner, len(targets) + 2, len(targets) + 1))


def plan_captions(lengths, picks, start_s, sorted_s, bound_s, images):
    captions = lengths.shape[1]

    def begin(c, run):
        start_s[c] = run
        return run + lengths[0, c]

    lax.fori_loop(0, captions, begin, jnp.int32(0))

    def image(i, run):
        bound_s[i] = run

        def caption(c, run):
            hit = picks[0, c] == i
            sorted_s[c] = jnp.where(hit, run, sorted_s[c])
            return run + jnp.where(hit, lengths[0, c], 0)

        return lax.fori_loop(0, captions, caption, run)

    def clear(c, run):
        sorted_s[c] = 0
        return run

    lax.fori_loop(0, captions, clear, 0)
    bound_s[images] = lax.fori_loop(0, images, image, jnp.int32(0))


def gather_kernel(
    images, lengths, picks, tokens, cot, img, master, norms,
    slots, x_o, meta_o, cot_o, enc_o, place_o,
    own, xs, metas, start_s, sorted_s, bound_s,
    ssem, rsem, sibsem, sibrecv, xsem, lsem,
):
    place = Place()
    rows = tokens.shape[0]
    captions = lengths.shape[1]
    own[...] = master[...].astype(BF)
    greet(place, False)
    sends = []

    def push(condition, part, chip, kind, mine=False):
        target = place.sibling() if kind == 4 else place.neighbour(kind)
        if kind < 4:
            condition = both(condition, place.has(kind))
        rows_p = G_PLAN.slot_rows(chip, place.c, part)
        src = own.at[pl.ds(G_PLAN.off[part], G_PLAN.rows[part])] if mine else slots.at[rows_p]
        sem = sibrecv if kind == 4 else rsem
        out = sibsem.at[part, chip] if kind == 4 else ssem.at[kind, part, chip]
        copy = pltpu.make_async_remote_copy(
            src_ref=src, dst_ref=slots.at[rows_p], send_sem=out, recv_sem=sem.at[part, chip],
            device_id=target, device_id_type=MESH,
        )
        when(condition, copy.start)
        sends.append((condition, copy))

    me = place.chip()
    for part, kind in OWN_SENDS + tuple((part, 4) for part in range(G_PLAN.count)):
        push(None, part, me, kind, mine=True)
    keep = pltpu.make_async_copy(
        own, slots.at[pl.ds(pl.multiple_of((me * 2 + place.c) * own.shape[0], 128), own.shape[0])], lsem
    )
    keep.start()

    plan_captions(lengths, picks, start_s, sorted_s, bound_s, images)
    token = lax.broadcasted_iota(jnp.int32, (1, rows), 1)

    def locate(c, where_to):
        inside = (token >= start_s[c]) & (token < start_s[c] + lengths[0, c])
        return jnp.where(inside, token + (sorted_s[c] - start_s[c]), where_to)

    where_to = lax.fori_loop(0, captions, locate, token)
    place_o[...] = jnp.broadcast_to(where_to, place_o.shape)
    lane = lax.broadcasted_iota(jnp.int32, metas.shape, 1)

    def note(c, row):
        return jnp.where(lane == c, sorted_s[c], row)

    row = lax.fori_loop(0, captions, note, jnp.zeros(metas.shape, jnp.int32))
    for i in range(images + 1):
        row = jnp.where(lane == BOUND_LANE + i, bound_s[i], row)
    metas[...] = row

    def sort(out, array):
        def body(b, _):
            target = lax.broadcasted_iota(jnp.int32, (QB, rows), 0) + b * QB
            onehot = (target == place_o[0:1, :]).astype(F32).astype(BF)
            out[blk(b), :] = nn(onehot, array[...]).astype(BF)
            return 0

        lax.fori_loop(0, rows // QB, body, 0)

    sort(xs, tokens)
    swaps = []
    for i, (src, dst) in enumerate(((metas, meta_o), (xs, x_o))):
        swaps.append(
            pltpu.make_async_remote_copy(
                src_ref=src, dst_ref=dst, send_sem=xsem.at[0, i], recv_sem=xsem.at[1, i],
                device_id=place.neighbour(X_), device_id_type=MESH,
            )
        )
        swaps[-1].start()

    def encode(i):
        def body(j, _):
            at = pl.ds(pl.multiple_of(i * IMG_ROWS + j * 64, 64), 64)
            normed, _i = normalise(img[at, :].astype(F32))
            enc_o[at, :] = (normed * norms[3:4, :] + norms[7:8, :]).astype(BF)
            return 0

        lax.fori_loop(0, IMG_ROWS // 64, body, 0)

    steps = img.shape[0] // IMG_ROWS
    done = 0
    for number, (part, dt, dz, dy) in enumerate(G_PLAN.pieces):
        there = place.exists(dz)
        chip = place.chip(dt, dz, dy)

        def arrived(part=part, chip=chip):
            rows_p = G_PLAN.slot_rows(chip, place.c, part)
            pltpu.make_async_remote_copy(
                src_ref=slots.at[rows_p], dst_ref=slots.at[rows_p], send_sem=ssem.at[0, part, chip],
                recv_sem=rsem.at[part, chip], device_id=place.neighbour(X_), device_id_type=MESH,
            ).wait_recv()

        when(there, arrived)
        for kind in G_PLAN.routes(part, dt, dz, dy) + [4]:
            push(there, part, chip, kind)
        if number == 4:
            sort(cot_o, cot)
        if number >= 6 and done < steps:
            encode(done)
            done += 1
    for i in range(done, steps):
        encode(i)

    def from_sibling(chip, _):
        for part in range(G_PLAN.count):
            rows_p = G_PLAN.slot_rows(chip, 1 - place.c, part)
            pltpu.make_async_remote_copy(
                src_ref=slots.at[rows_p], dst_ref=slots.at[rows_p], send_sem=sibsem.at[part, chip],
                recv_sem=sibrecv.at[part, chip], device_id=place.sibling(), device_id_type=MESH,
            ).wait_recv()
        return 0

    lax.fori_loop(0, 4 * Z_CHIPS, from_sibling, 0)
    for condition, copy in sends:
        when(condition, copy.wait_send)
    for swap in swaps:
        swap.wait()
    keep.wait()


IMG_ROWS = 192
ENC_ROWS = 192


def run_gather(images, lengths, picks, tokens, cot, img, master, norms, total_rows):
    rows = tokens.shape[0]
    dma = pltpu.SemaphoreType.DMA
    low = jax.ShapeDtypeStruct((rows, D), BF)
    return pl.pallas_call(
        functools.partial(gather_kernel, images),
        out_shape=(
            jax.ShapeDtypeStruct((total_rows, D), BF),
            low,
            jax.ShapeDtypeStruct((8, 128), jnp.int32),
            low,
            jax.ShapeDtypeStruct(img.shape, BF),
            jax.ShapeDtypeStruct((8, rows), jnp.int32),
        ),
        in_specs=[SM, SM, VM, VM, VM, VM, VM],
        out_specs=(ANY, ANY, ANY, VM, VM, VM),
        scratch_shapes=[
            pltpu.VMEM(master.shape, BF),
            pltpu.VMEM((rows, D), BF),
            pltpu.VMEM((8, 128), jnp.int32),
            pltpu.SMEM((lengths.shape[1],), jnp.int32),
            pltpu.SMEM((lengths.shape[1],), jnp.int32),
            pltpu.SMEM((images + 1,), jnp.int32),
            dma((4, G_PLAN.count, 16)),
            dma((G_PLAN.count, 16)),
            dma((G_PLAN.count, 16)),
            dma((G_PLAN.count, 16)),
            dma((2, 2)),
            dma,
        ],
        compiler_params=pltpu.CompilerParams(
            vmem_limit_bytes=VLIM, has_side_effects=True, collective_id=0
        ),
    )(lengths, picks, tokens, cot, img, master, norms)


def sum_kernel(
    grads, norm_terms, place_row, gt, out_back, dk_h, dv_h, w_h, img_h, norms,
    red_o, norm_o, gt_o, lay_o, gi_h,
    out_b, obsem, wkv, ebuf, obuf, ng, esem, osem, wksem, acc, sib, gtr, nbuf, nrecv,
    lsem, sibsem, sibrecv, ssem, rsem, gsem, nsend, nrs, *land,
):
    place = Place()
    rows = gt.shape[0]
    greet(place, True)
    order = S_PLAN.pieces + [(part, 0, 0, 0) for part in range(S_PLAN.count)]
    sends = []

    def local(part, chip):
        off = pl.ds(S_PLAN.off[part], S_PLAN.rows[part])
        return pltpu.make_async_copy(
            grads.at[S_PLAN.slot_rows(chip, place.c, part)], acc.at[chip, off], lsem.at[part, chip]
        )

    def across(part, chip):
        off = pl.ds(S_PLAN.off[part], S_PLAN.rows[part])
        return pltpu.make_async_remote_copy(
            src_ref=grads.at[S_PLAN.slot_rows(chip, 1 - place.c, part)], dst_ref=sib.at[chip, off],
            send_sem=sibsem.at[part, chip], recv_sem=sibrecv.at[part, chip],
            device_id=place.sibling(), device_id_type=MESH,
        )

    for part, dt, dz, dy in order:
        chip = place.chip(dt, dz, dy)

        def begin(part=part, chip=chip):
            across(part, chip).start()
            local(part, chip).start()

        when(place.exists(dz), begin)
    back = pltpu.make_async_remote_copy(
        src_ref=gt, dst_ref=gtr, send_sem=gsem.at[0], recv_sem=gsem.at[1],
        device_id=place.neighbour(X_), device_id_type=MESH,
    )

    def landing(part, kind, chip):
        at = {"x": chip // 8, "z": (chip // 2) % Z_CHIPS, "y": chip % 2}
        spot = 0
        for name in S_PLAN.landing_spots(part, kind)[0]:
            spot = spot * DIMS[name] + at[name]
        return land[part * 4 + kind].at[spot]

    def flow(part, kind, chip):
        off = pl.ds(S_PLAN.off[part], S_PLAN.rows[part])
        return pltpu.make_async_remote_copy(
            src_ref=acc.at[chip, off], dst_ref=landing(part, kind, chip),
            send_sem=ssem.at[part, chip], recv_sem=rsem.at[kind, part, chip],
            device_id=place.neighbour(kind), device_id_type=MESH,
        )

    def add(part, chip, other, final):
        def body(i, _):
            at = pl.ds(pl.multiple_of(S_PLAN.off[part] + i * 32, 32), 32)
            value = acc[chip, at, :].astype(F32)
            for ref in other:
                value = value + ref(part, pl.ds(pl.multiple_of(i * 32, 32), 32), at).astype(F32)
            if final:
                red_o[at, :] = value
            else:
                acc[chip, at, :] = value.astype(BF)
            return 0

        lax.fori_loop(0, S_PLAN.rows[part] // 32, body, 0)

    def norm_round(i, target):
        return pltpu.make_async_remote_copy(
            src_ref=nbuf.at[i], dst_ref=nrecv.at[i], send_sem=nsend.at[i], recv_sem=nrs.at[i],
            device_id=target, device_id_type=MESH,
        )

    def norm_line(k, target):
        return pltpu.make_async_remote_copy(
            src_ref=nbuf.at[3], dst_ref=nrecv.at[3 + place.z], send_sem=nsend.at[3 + k],
            recv_sem=nrs.at[3 + place.z], device_id=target, device_id_type=MESH,
        )

    def norm_from(z):
        return pltpu.make_async_remote_copy(
            src_ref=nbuf.at[3], dst_ref=nrecv.at[3 + z], send_sem=nsend.at[3], recv_sem=nrs.at[3 + z],
            device_id=place.neighbour(X_), device_id_type=MESH,
        )

    line = [norm_line(k, target) for k, target in enumerate(place.line())]
    rounds = [place.sibling(), place.neighbour(X_), place.neighbour(Y_)]
    keys = pltpu.make_async_copy(w_h, wkv, wksem)
    keys.start()
    out_copy = pltpu.make_async_copy(out_back, out_b, obsem)
    out_copy.start()
    steps = dk_h.shape[0] // ENC_ROWS
    ng[...] = jnp.zeros_like(ng)

    def fetch(i):
        at = pl.ds(i * ENC_ROWS, ENC_ROWS)
        return [
            pltpu.make_async_copy(ref.at[at], ebuf.at[j, i % 2], esem.at[j, i % 2])
            for j, ref in enumerate((dk_h, dv_h, img_h))
        ]

    def put(i):
        at = pl.ds(i * ENC_ROWS, ENC_ROWS)
        return [pltpu.make_async_copy(obuf.at[i % 2], gi_h.at[at], osem.at[i % 2])]

    def encoder_back(i):
        wait(fetch(i))
        if i >= 2:
            wait(put(i - 2))
        out = obuf.at[i % 2]
        out[...] = nt(ebuf[0, i % 2], wkv[0]) + nt(ebuf[1, i % 2], wkv[1])

        def body(j, _):
            normed, inv_std = normalise(ebuf[2, i % 2, blk(j, 64), :].astype(F32))
            grad = out[blk(j, 64), :].astype(BF).astype(F32)
            ng[0:1, :] += jnp.sum(grad * normed, axis=0, keepdims=True)
            ng[1:2, :] += jnp.sum(grad, axis=0, keepdims=True)
            out[blk(j, 64), :] = norm_back(grad, normed, inv_std, norms[3:4, :])
            return 0

        lax.fori_loop(0, ENC_ROWS // 64, body, 0, unroll=True)
        start(put(i))
        if i + 2 < steps:
            start(fetch(i + 2))

    start(fetch(0))
    start(fetch(1))

    def unsort(out, array):
        def body(b, _):
            target = lax.broadcasted_iota(jnp.int32, (rows, QB), 0)
            onehot = (target == place_row[0:1, blk(b)]).astype(F32).astype(BF)
            out[blk(b), :] = tn(onehot, array[...]).astype(out.dtype)
            return 0

        lax.fori_loop(0, rows // QB, body, 0)

    span = len(order) // 2 - 4
    enc_at = [2 + i * span // steps for i in range(steps)]
    norm_at = [span + 3 + (i * len(order)) // 14 for i in range(4)]
    for number, (part, dt, dz, dy) in enumerate(order):
        chip = place.chip(dt, dz, dy)
        if number == GT_AT:
            back.start()
        there = place.exists(dz)
        final = (dt, dz, dy) == (0, 0, 0)
        kinds = S_PLAN.routes(part, dt, dz, dy)

        def step(part=part, chip=chip, kinds=kinds, final=final, dt=dt, dz=dz, dy=dy):
            local(part, chip).wait()
            across(part, chip).wait_recv()
            refs = [lambda p, i, at: sib[chip, at, :]]
            fixed = [kind for kind in kinds if kind in (X_, Y_)]
            edge = [kind for kind in kinds if kind in (UP_, DN_)]
            for kind in fixed:
                flow(part, OPPOSITE[kind], chip).wait_recv()
                refs.append(
                    lambda p, i, at, kind=kind: landing(part, OPPOSITE[kind], chip)[i, :]
                )
            for kind in edge:

                def one(kind=kind):
                    flow(part, OPPOSITE[kind], chip).wait_recv()
                    add(part, chip, [lambda p, i, at: landing(part, OPPOSITE[kind], chip)[i, :]], False)

                pl.when(place.has(kind))(one)
            add(part, chip, refs, final)
            if not final:
                flow(part, S_PLAN.source(part, dt, dz, dy), chip).start()

        when(there, step)
        if not final:
            sends.append((there, part, chip, S_PLAN.source(part, dt, dz, dy)))
        if number in enc_at:
            if number == enc_at[0]:
                keys.wait()
            encoder_back(enc_at.index(number))
        if number == norm_at[0]:
            nbuf[0] = norm_terms[...]
            nbuf[0, 3:4, :] = ng[0:1, :]
            nbuf[0, 7:8, :] = ng[1:2, :]
            norm_round(0, rounds[0]).start()
        if number in norm_at[1:]:
            i = norm_at.index(number) - 1
            norm_round(i, rounds[i]).wait()
            nbuf[i + 1] = nbuf[i] + nrecv[i]
            if i < 2:
                norm_round(i + 1, rounds[i + 1]).start()
            else:
                for copy in line:
                    copy.start()
        if number == norm_at[0] + 1:
            out_copy.wait()
            unsort(lay_o, out_b)
        if number == norm_at[3] + 1:
            back.wait()
            unsort(gt_o, gtr)

    for z in range(Z_CHIPS):

        @pl.when(place.z != z)
        def _(z=z):
            norm_from(z).wait_recv()

        @pl.when(place.z == z)
        def _(z=z):
            nrecv[3 + z] = nbuf[3]

    wait(put(steps - 2) + put(steps - 1))
    norm_o[...] = (nrecv[3] + nrecv[4]) + (nrecv[5] + nrecv[6])
    for copy in line:
        copy.wait_send()
    for there, part, chip, kind in sends:
        when(there, flow(part, kind, chip).wait_send)

    def sent(chip, _):
        for part in range(S_PLAN.count):
            across(part, chip).wait_send()
        return 0

    lax.fori_loop(0, 4 * Z_CHIPS, sent, 0)


def run_sum(grads, norm_terms, place_row, gt, out_back, dk, dv, kv_weights, img, norms):
    rows = gt.shape[0]
    dma = pltpu.SemaphoreType.DMA
    shard = S_PLAN.shard
    line = 4 * Z_CHIPS
    return pl.pallas_call(
        sum_kernel,
        out_shape=(
            jax.ShapeDtypeStruct((shard, D), F32),
            jax.ShapeDtypeStruct((8, D), F32),
            jax.ShapeDtypeStruct((rows, D), F32),
            jax.ShapeDtypeStruct((rows, D), BF),
            jax.ShapeDtypeStruct(img.shape, F32),
        ),
        in_specs=[ANY, VM, VM, ANY, ANY, ANY, ANY, ANY, ANY, VM],
        out_specs=(VM,) * 4 + (ANY,),
        scratch_shapes=[
            pltpu.VMEM((rows, D), BF),
            dma,
            pltpu.VMEM((2, D, D), BF),
            pltpu.VMEM((3, 2, ENC_ROWS, D), BF),
            pltpu.VMEM((2, ENC_ROWS, D), F32),
            pltpu.VMEM((8, D), F32),
            dma((3, 2)),
            dma((2,)),
            dma,
            pltpu.VMEM((line, shard, D), BF),
            pltpu.VMEM((line, shard, D), BF),
            pltpu.VMEM((rows, D), BF),
            pltpu.VMEM((4, 8, D), F32),
            pltpu.VMEM((7, 8, D), F32),
            dma((S_PLAN.count, line)),
            dma((S_PLAN.count, line)),
            dma((S_PLAN.count, line)),
            dma((S_PLAN.count, line)),
            dma((4, S_PLAN.count, line)),
            dma((2,)),
            dma((7,)),
            dma((7,)),
        ]
        + [
            pltpu.VMEM((S_PLAN.landing_spots(part, kind)[1], S_PLAN.rows[part], D), BF)
            for part in range(S_PLAN.count)
            for kind in range(4)
        ],
        compiler_params=pltpu.CompilerParams(
            vmem_limit_bytes=VLIM, has_side_effects=True, collective_id=1
        ),
    )(grads, norm_terms, place_row, gt, out_back, dk, dv, kv_weights, img, norms)


def from_partner(block, axis):
    half = lax.axis_size(axis) // 2
    count = lax.axis_size(axis)
    return lax.ppermute(block, axis, [(i, (i + half) % count) for i in range(count)])


def adamw_update(weight, moment, second, grad_in, rate, decay_rate):
    new_moment = beta_one * moment + (1.0 - beta_one) * grad_in
    new_second = beta_two * second + (1.0 - beta_two) * grad_in * grad_in
    moment_hat = new_moment / (1.0 - beta_one**STEP)
    second_hat = new_second / (1.0 - beta_two**STEP)
    new_weight = weight - rate * (
        moment_hat / (jnp.sqrt(second_hat) + epsilon) + decay_rate * weight
    )
    return (new_weight, new_moment, new_second)


def caption_plan(lengths, picks, rows, images):
    ends = jnp.cumsum(lengths)
    starts = ends - lengths
    rank = picks * lengths.shape[0] + jnp.arange(lengths.shape[0], dtype=jnp.int32)
    ahead = rank[None, :] < rank[:, None]
    sorted_starts = jnp.sum(jnp.where(ahead, lengths[None, :], 0), axis=1)
    token = jnp.arange(rows, dtype=jnp.int32)
    inside = (token[:, None] >= starts[None, :]) & (token[:, None] < ends[None, :])
    place = token + jnp.sum(jnp.where(inside, (sorted_starts - starts)[None, :], 0), axis=1)
    edges = jnp.arange(images + 1, dtype=jnp.int32)
    bounds = jnp.sum(jnp.where(picks[None, :] < edges[:, None], lengths[None, :], 0), axis=1)
    return place, sorted_starts, bounds


def per_device(
    kernels,
    tokens,
    cotangent,
    caption_lengths,
    image_index,
    image_states,
    master_weights,
    first_moments,
    second_moments,
    owner_list,
    norm_params,
    norm_first,
    norm_second,
):
    rows = tokens.shape[0]
    groups = owner_list.shape[0]
    total_rows = 8 * D + 2 * FF
    group_rows = total_rows // groups
    images = image_states.shape[0]
    captions = caption_lengths.shape[1]
    axes = ("tower", "dp")
    direct = group_rows == GROUP
    ids = jnp.arange(groups, dtype=jnp.int32)
    inverse = jnp.sum(jnp.where(owner_list[None, :] == ids[:, None], ids[None, :], 0), axis=1)
    img = image_states.reshape(-1, D)
    if kernels:
        gathered, x, meta, sent_cot, enc, place_row = run_gather(
            images, caption_lengths, image_index, tokens, cotangent, img, master_weights,
            norm_params, total_rows,
        )
    else:
        gathered = lax.all_gather(master_weights.astype(BF), axes, axis=0, tiled=True)
        place, starts, bounds = caption_plan(caption_lengths[0], image_index[0], rows, images)
        into = (place[None, :] == jnp.arange(rows, dtype=jnp.int32)[:, None]).astype(BF)
        meta = jnp.zeros((8, 128), jnp.int32)
        meta = meta.at[0, :captions].set(starts)
        meta = meta.at[0, BOUND_LANE : BOUND_LANE + images + 1].set(bounds)
        meta = from_partner(meta, "tower")
        x = from_partner(nn(into, tokens).astype(BF), "tower")
        sent_cot = nn(into, cotangent).astype(BF)
        normed, _i = normalise(img.astype(F32))
        enc = (normed * norm_params[3] + norm_params[7]).astype(BF)
    if direct:
        slots = gathered.reshape(groups, GROUP, D)
        inv = inverse
    else:
        slots = gathered.reshape(groups, group_rows, D)[inverse].reshape(-1, GROUP, D)
        inv = jnp.arange(total_rows // GROUP, dtype=jnp.int32)
    cot = from_partner(sent_cot, "tower")
    *kept, kv_weights, r2 = run_attention_forward(
        captions, images, inv, meta, x, enc, norm_params, slots
    )
    out, g2, ng3, grads = run_feed_forward(inv, r2, cot, norm_params, slots)
    out_back = from_partner(out, "tower")
    gt, norm_terms, dk, dv, grads = run_attention_backward(
        captions, images, inv, meta, g2, x, kept, enc, norm_params, slots, grads, ng3
    )
    if kernels:
        reduced, norm_grads, grad_tokens, layer_out, grad_images = run_sum(
            grads.reshape(total_rows, D), norm_terms, place_row, gt, out_back, dk, dv, kv_weights,
            img, norm_params,
        )
    else:
        layer_out = tn(into, out_back).astype(BF)
        grad_tokens = tn(into, from_partner(gt, "tower"))
        grad_enc = (nt(dk, kv_weights[0]) + nt(dv, kv_weights[1])).astype(BF).astype(F32)
        normed, inv_std = normalise(img.astype(F32))
        grad_images = norm_back(grad_enc, normed, inv_std, norm_params[3:4])
        norm_terms = norm_terms.at[3].set(jnp.sum(grad_enc * normed, axis=0))
        norm_terms = norm_terms.at[7].set(jnp.sum(grad_enc, axis=0))
        if direct:
            arranged = grads.reshape(total_rows, D)
        else:
            arranged = grads.reshape(groups, group_rows, D)[owner_list].reshape(total_rows, D)
        reduced = lax.psum_scatter(arranged, axes, scatter_dimension=0, tiled=True).astype(F32)
        norm_grads = lax.psum(norm_terms, axes)
    new_weights, new_first, new_second = adamw_update(
        master_weights, first_moments, second_moments, reduced, learn_rate, weight_decay
    )
    norm_new, norm_first_new, norm_second_new = adamw_update(
        norm_params, norm_first, norm_second, norm_grads, norm_rate, 0.0
    )
    return (
        layer_out,
        grad_tokens,
        grad_images.reshape(image_states.shape),
        new_weights,
        new_first,
        new_second,
        new_weights.astype(BF),
        norm_new,
        norm_first_new,
        norm_second_new,
    )


def solution(mesh):
    split = P(("tower", "dp"), None)
    wide = P(("tower", "dp"), None, None)
    in_specs = (split,) * 4 + (wide,) + (split,) * 3 + (P(),) * 4
    out_specs = (split, split, wide) + (split,) * 4 + (P(),) * 3
    shape = dict(mesh.shape)
    kernels = shape["tower"] == 2 and shape["dp"] == 4 * Z_CHIPS
    return jax.shard_map(
        functools.partial(per_device, kernels),
        mesh=mesh,
        in_specs=in_specs,
        out_specs=out_specs,
        check_vma=False,
    )
```
